32 devices in a mesh: wide: 8 (over z, x), narrow: 4 (over y, core).
Axes of the slice: x: 2, y: 2, z: 4, core: 2. Of those that a mesh axis runs over, the one named last changes fastest.
Arguments:
- tokens: bfloat16 [64, 1024, 768], P(('wide', 'narrow')), may hold values from -6 to 6
- item_ids: int32 [64], P(('wide', 'narrow')), may hold values from 0 to 63, as said below
- w_mem: bfloat16 [768, 2304], P(('wide', 'narrow')), may hold values from -0.21875 to 0.21875
- w_qkv: bfloat16 [768, 2304], P(('wide', 'narrow')), may hold values from -0.21875 to 0.21875
- w_out: bfloat16 [768, 768], P(('wide', 'narrow')), may hold values from -6 to 6
- w_up: bfloat16 [768, 3072], P(('wide', 'narrow')), may hold values from -0.21875 to 0.21875
- w_down: bfloat16 [3072, 768], P(('wide', 'narrow')), may hold values from -0.109375 to 0.109375
- mem_tokens: bfloat16 [16, 768], replicated, may hold values from -6 to 6
- gains: bfloat16 [2, 768], replicated, may hold values from 0.5 to 1.5
- w_beta: bfloat16 [768], replicated, may hold values from -0.21875 to 0.21875
- out_grad: bfloat16 [64, 1024, 768], P(('wide', 'narrow')), may hold values from -6 to 6
Outputs:
- block_out: bfloat16 [64, 1024, 768], P(('wide', 'narrow'))
- grad_tokens: float32 [64, 1024, 768], P(('wide', 'narrow'))
- grad_w_mem: float32 [768, 2304], P(('wide', 'narrow'))
- grad_w_qkv: float32 [768, 2304], P(('wide', 'narrow'))
- grad_w_out: float32 [768, 768], P(('wide', 'narrow'))
- grad_w_up: float32 [768, 3072], P(('wide', 'narrow'))
- grad_w_down: float32 [3072, 768], P(('wide', 'narrow'))
- grad_mem_tokens: float32 [16, 768], replicated
- grad_gains: float32 [2, 768], replicated
- grad_w_beta: float32 [768], replicated
The draws below stay inside these ranges and needn't reach their ends.
Inputs may be any that keep to these rules, and one draw needn't show every extreme that they name: `item_ids`: A segment's number is the index, counted from 0 over all 64 segments, of the first segment of its item; an item's segments are consecutive and lie in one group of 2; every group begins a new item; an item has 1 to 2 segments.
All inputs are finite; a program needn't handle non-finite values.
Results may differ from the reference program's by a relative error of at most 0.017.
Values may be sent and summed in bfloat16 or wider, within the bound.
A program may use at most 448 MiB of HBM per device.

```python
import jax
import jax.numpy as jnp
from jax import lax

D = 768
HEADS = 12
HD = 64
FF = 3072
MEMS = 16
SEG = 1024
SLOTS = 2
SLOTS_ALL = 64
N_WIDE = 8
N_NARROW = 4


def draw_item_ids(key, part):
    key = jax.random.fold_in(key, 11)
    groups = SLOTS_ALL // SLOTS
    joins = jax.random.randint(key, (groups, SLOTS), 0, 2)
    slot_pos = lax.broadcasted_iota(jnp.int32, (groups, SLOTS), 1)
    group_pos = lax.broadcasted_iota(jnp.int32, (groups, SLOTS), 0)
    joins = jnp.where(group_pos == 0, 1, joins)
    joins = jnp.where(group_pos == 1, 0, joins)
    joins = jnp.where(group_pos == groups - 1, 0, joins)
    joins = jnp.where(slot_pos == 0, 0, joins)
    starts = (1 - joins).reshape(-1)
    position = lax.broadcasted_iota(jnp.int32, (SLOTS_ALL,), 0)
    marked = jnp.where(starts == 1, position, 0).astype(jnp.int32)
    return lax.cummax(marked, axis=0).astype(jnp.int32)


def level_of(rng, shape, pieces, smallest, high):
    level = 1.0
    for dim, shards_of in pieces:
        draws = jax.random.uniform(jax.random.fold_in(jax.random.fold_in(rng, 6), dim), (shards_of,), jnp.float32, smallest / len(pieces), high / len(pieces))
        level = level * jnp.repeat(jnp.exp(draws), shape[dim] // shards_of).reshape((-1,) + (1,) * (len(shape) - 1 - dim))
    return level


def scatter_about(own_key, dims, scale, limit, pieces=(), held_as=jnp.bfloat16):
    entries = scale * jax.random.normal(own_key, dims, jnp.float32)
    if pieces:
        entries = entries * level_of(own_key, dims, pieces, -0.22, 0.18)
    return jnp.clip(entries, -limit, limit).astype(held_as)


def setup_inputs(seed: int = 0) -> dict:
    arg_keys = jax.random.split(jax.random.key(seed), 12)
    tokens = scatter_about(arg_keys[0], (SLOTS_ALL, SEG, D), 1.0, 6.0, ((0, 32),))
    item_ids = draw_item_ids(jax.random.fold_in(arg_keys[11], 71), 0)
    w_mem = scatter_about(arg_keys[2], (D, 3 * D), D ** -0.5, 0.21875, ((0, 32),))
    w_qkv = scatter_about(arg_keys[3], (D, 3 * D), D ** -0.5, 0.21875, ((0, 32),))
    w_out = scatter_about(arg_keys[4], (D, D), (2 * D // SEG) ** -0.5, 6.0, ((0, 32),))
    w_up = scatter_about(arg_keys[5], (D, FF), D ** -0.5, 0.21875, ((0, 32),))
    w_down = scatter_about(arg_keys[6], (FF, D), FF ** -0.5, 0.109375, ((0, 32),))
    mem_tokens = scatter_about(arg_keys[7], (MEMS, D), 1.0, 6.0)
    gains = jnp.clip(1.0 + 0.1 * jax.random.normal(arg_keys[8], (2, D), jnp.float32), 0.5, 1.5).astype(jnp.bfloat16)
    w_beta = scatter_about(arg_keys[9], (D,), D ** -0.5, 0.21875)
    out_grad = scatter_about(arg_keys[10], (SLOTS_ALL, SEG, D), 1.0, 6.0, ((0, 32),))
    return dict(tokens=tokens, item_ids=item_ids, w_mem=w_mem, w_qkv=w_qkv, w_out=w_out, w_up=w_up, w_down=w_down, mem_tokens=mem_tokens, gains=gains, w_beta=w_beta, out_grad=out_grad)


@jax.custom_vjp
def low(v):
    return lax.optimization_barrier(v.astype(jnp.bfloat16)).astype(jnp.float32)

@jax.custom_vjp
def low_back(v):
    return v

def low_keep(v):
    return (low(v), None)

def low_pass(kept, grad):
    return (grad,)

def back_keep(v):
    return (v, None)

def back_low(kept, grad):
    return (low(grad),)
low.defvjp(low_keep, low_pass)
low_back.defvjp(back_keep, back_low)
highest = lax.Precision.HIGHEST
eps_norm = 1e-05
score_scale = 0.125

def product(left, right):
    return jnp.dot(left, right, precision=highest)

def layer_norm(values, gain):
    average = lax.optimization_barrier(jnp.mean(values, axis=-1, keepdims=True))
    centered = values - average
    spread = lax.optimization_barrier(jnp.mean(centered * centered, axis=-1, keepdims=True))
    return centered * lax.rsqrt(spread + eps_norm) * gain

def feature_map(values):
    softer = jax.nn.softplus(values)
    return jnp.concatenate([softer * jnp.roll(softer, offset, axis=-1) for offset in (1, 2, 3)], axis=-1)

def gelu_tanh(values):
    return jax.nn.gelu(values, approximate=True)

def normalized(numerator, phi_rows, normalizer):
    return numerator / (1.0 + jnp.dot(phi_rows, normalizer, precision=highest))[:, None]

def write_terms(mem_out, w_beta, values, recall, phi_keys, normalizer):
    beta = jax.nn.sigmoid(jnp.dot(mem_out, w_beta, precision=highest))
    recalled = normalized(recall, phi_keys, normalizer)
    delta = beta[:, None] * (values - recalled)
    grown = jnp.dot(beta, phi_keys, precision=highest)
    return (delta, grown)

def segment_pass(weights, inputs, memory, normalizer, writes):
    w_mem, w_qkv, w_out, w_up, w_down, mem_tokens, gains, w_beta = weights
    rows = SEG + MEMS
    first = jnp.concatenate([inputs, mem_tokens], axis=0)
    memory_low = low(memory)
    query_mem = low_back(product(low(first), w_mem[:, :D]))
    phi_query = feature_map(query_mem)
    numerator = low_back(product(low(phi_query), memory_low))
    states = first + normalized(numerator, phi_query, normalizer)
    normed = low(layer_norm(states, gains[0]))
    qkv = low(low_back(product(normed, w_qkv)))
    queries = qkv[:, :D].reshape(rows, HEADS, HD)
    keys_all = qkv[:, D:2 * D].reshape(rows, HEADS, HD)
    values_all = qkv[:, 2 * D:].reshape(rows, HEADS, HD)
    raw = low_back(jnp.einsum('qhd,khd->hqk', queries, keys_all, precision=highest)) * score_scale
    positions = jnp.arange(rows)
    causal = positions[:, None] >= positions[None, :]
    masked = jnp.where(causal[None], raw, -1e+30)
    probs = low(jax.nn.softmax(masked, axis=-1))
    attended = jnp.einsum('hqk,khd->qhd', probs, values_all, precision=highest)
    attended = low(low_back(attended.reshape(rows, D)))
    states = states + low_back(product(attended, w_out))
    normed_two = low(layer_norm(states, gains[1]))
    upward = low_back(product(normed_two, w_up))
    states = states + low_back(product(low(gelu_tanh(upward)), w_down))
    output = states[:SEG]
    if writes:
        mem_out = states[SEG:]
        key_value = low_back(product(low(mem_out), w_mem[:, D:]))
        phi_keys = feature_map(key_value[:, :D])
        phi_keys_low = low(phi_keys)
        recall = low_back(product(phi_keys_low, memory_low))
        delta, grown = write_terms(mem_out, w_beta, key_value[:, D:], recall, phi_keys, normalizer)
        memory = memory + low_back(product(phi_keys_low.T, low(delta)))
        normalizer = normalizer + grown
    return (output, memory, normalizer)

def device_pass(weights, group_tokens, flags):
    memory = jnp.zeros((3 * D, D), jnp.float32)
    normalizer = jnp.zeros((3 * D,), jnp.float32)
    outputs = []
    for slot in range(SLOTS):
        memory = memory * flags[slot]
        normalizer = normalizer * flags[slot]
        output, memory, normalizer = segment_pass(weights, group_tokens[slot], memory, normalizer, slot + 1 < SLOTS)
        outputs.append(output)
    return jnp.stack(outputs)

def reference(tokens, item_ids, w_mem, w_qkv, w_out, w_up, w_down, mem_tokens, gains, w_beta, out_grad):
    groups = N_WIDE * N_NARROW
    weights = (w_mem.astype(jnp.float32), w_qkv.astype(jnp.float32), w_out.astype(jnp.float32), w_up.astype(jnp.float32), w_down.astype(jnp.float32), mem_tokens.astype(jnp.float32), gains.astype(jnp.float32), w_beta.astype(jnp.float32))
    grouped = tokens.astype(jnp.float32).reshape(groups, SLOTS, SEG, D)
    item_grid = item_ids.reshape(groups, SLOTS)
    same_item = item_grid[:, 1:] == item_grid[:, :-1]
    flags = jnp.concatenate([jnp.zeros((groups, 1), jnp.float32), jnp.where(same_item, 1.0, 0.0).astype(jnp.float32)], axis=1)

    def forward(weights, grouped):

        def one_group(pair):
            return device_pass(weights, pair[0], pair[1])
        return lax.map(jax.checkpoint(one_group), (grouped, flags))
    outputs, pullback = jax.vjp(forward, weights, grouped)
    grad_weights, grad_grouped = pullback(out_grad.astype(jnp.float32).reshape(groups, SLOTS, SEG, D))
    return (outputs.reshape(SLOTS_ALL, SEG, D).astype(jnp.bfloat16), grad_grouped.reshape(SLOTS_ALL, SEG, D), grad_weights[0], grad_weights[1], grad_weights[2], grad_weights[3], grad_weights[4], grad_weights[5], grad_weights[6], grad_weights[7])
```

```python
import functools

import jax
import jax.numpy as jnp
from jax import lax
from jax.experimental import pallas as pl
from jax.experimental.pallas import tpu as pltpu
from jax.sharding import PartitionSpec as P

HD = 64
PAIR = 2 * HD
AXES = ("wide", "narrow")
eps_norm = 1e-05
score_scale = 0.125
gelu_c = 0.7978845608028654
gelu_a = 0.044715
f32 = jnp.float32
low_type = jnp.bfloat16
VMEM_BYTES = 60 * 2**20


def nn(left, right):
    return lax.dot_general(left, right, (((1,), (0,)), ((), ())), preferred_element_type=f32)


def nt(left, right):
    return lax.dot_general(left, right, (((1,), (1,)), ((), ())), preferred_element_type=f32)


def tn(left, right):
    return lax.dot_general(left, right, (((0,), (0,)), ((), ())), preferred_element_type=f32)


def low(values):
    return values.astype(low_type)


def split(values):
    high = low(values)
    return high, low(values - high.astype(f32))


def row_chunk(rows):
    for count in (208, 256, 128, 80, 64, 16):
        if rows % count == 0:
            return count
    return rows


def over_rows(rows, body):
    count = row_chunk(rows)

    @pl.loop(0, rows // count)
    def _(step):
        body(pl.ds(pl.multiple_of(step * count, count), count))


def normal_form(values):
    average = jnp.mean(values, axis=-1, keepdims=True)
    centered = values - average
    spread = jnp.mean(centered * centered, axis=-1, keepdims=True)
    inverse = lax.rsqrt(spread + eps_norm)
    return centered * inverse, inverse


def norm_back(grad, unit, inverse, gain):
    scaled = grad * gain
    mean_grad = jnp.mean(scaled, axis=-1, keepdims=True)
    mean_unit = jnp.mean(scaled * unit, axis=-1, keepdims=True)
    return inverse * (scaled - mean_grad - unit * mean_unit)


def softplus(values):
    return jnp.maximum(values, 0.0) + jnp.log1p(jnp.exp(-jnp.abs(values)))


def feature_parts(softer):
    return [softer * pltpu.roll(softer, offset, 1) for offset in (1, 2, 3)]


def feature_back(grads, softer, values):
    width = softer.shape[1]
    total = None
    for offset, grad in zip((1, 2, 3), grads):
        term = grad * pltpu.roll(softer, offset, 1) + pltpu.roll(grad * softer, width - offset, 1)
        total = term if total is None else total + term
    return total * jax.nn.sigmoid(values)


def whole(shape, memory=None):
    zeros = (0,) * len(shape)
    return pl.BlockSpec(shape, lambda *_: zeros, pipeline_mode=pl.Buffered(1))


def result(shape):
    zeros = (0,) * len(shape)
    return pl.BlockSpec(shape, lambda *_: zeros)


def params(**extra):
    return pltpu.CompilerParams(vmem_limit_bytes=VMEM_BYTES, **extra)


def shaped(shape, dtype):
    return jax.ShapeDtypeStruct(shape, dtype)


def load_first(tokens_ref, mem_ref, first_ref):
    seg_rows = tokens_ref.shape[0]
    first_ref[:seg_rows, :] = tokens_ref[...]
    first_ref[seg_rows:, :] = mem_ref[...]


def enter_kernel(tokens_ref, mem_ref, gains_ref, w_ref, normed_ref, qkv_ref, first_ref):
    @pl.when(pl.program_id(0) == 0)
    def _():
        load_first(tokens_ref, mem_ref, first_ref)

        def chunk(at):
            unit, _ = normal_form(first_ref[at, :].astype(f32))
            normed_ref[at, :] = low(unit * gains_ref[0:1, :])

        over_rows(first_ref.shape[0], chunk)

    qkv_ref[0] = low(nn(normed_ref[...], w_ref[...]))


def enter_read_kernel(
    tokens_ref,
    mem_ref,
    gains_ref,
    w_ref,
    w_query_ref,
    phi_keys_ref,
    delta_ref,
    beta_ref,
    normed_ref,
    qkv_ref,
    states_ref,
    query_ref,
    match_ref,
    first_ref,
):
    @pl.when(pl.program_id(0) == 0)
    def _():
        load_first(tokens_ref, mem_ref, first_ref)
        width = first_ref.shape[1]
        delta_twice = jnp.concatenate([delta_ref[...], delta_ref[...]], axis=0)

        def chunk(at):
            first = first_ref[at, :]
            query = nn(first, w_query_ref[...])
            query_ref[at, :] = query
            parts = feature_parts(softplus(query))
            match = None
            for index, part in enumerate(parts):
                term = nt(low(part), phi_keys_ref[:, index * width : (index + 1) * width])
                match = term if match is None else match + term
            match_ref[at, :] = match
            numerator = nn(jnp.concatenate(split(match), axis=1), delta_twice)
            below = 1.0 + jnp.sum(match * beta_ref[...], axis=1, keepdims=True)
            states = first.astype(f32) + numerator / below
            states_ref[at, :] = states
            unit, _ = normal_form(states)
            normed_ref[at, :] = low(unit * gains_ref[0:1, :])

        over_rows(first_ref.shape[0], chunk)

    qkv_ref[0] = low(nn(normed_ref[...], w_ref[...]))


def enter_segment(slot, tokens, mem_tokens, gains, w_qkv, w_mem, written):
    slots, seg_rows, width = tokens.shape
    mems = mem_tokens.shape[0]
    rows = seg_rows + mems
    parts = w_qkv.shape[1] // width
    in_specs = [
        pl.BlockSpec((None, seg_rows, width), lambda j: (slot, 0, 0), pipeline_mode=pl.Buffered(1)),
        whole((mems, width)),
        whole(gains.shape),
        pl.BlockSpec((width, width), lambda j: (0, j)),
    ]
    out_shape = [shaped((rows, width), low_type), shaped((parts, rows, width), low_type)]
    out_specs = [
        result((rows, width)),
        pl.BlockSpec((1, rows, width), lambda j: (j, 0, 0)),
    ]
    args = [tokens, mem_tokens, gains, w_qkv]
    body = enter_kernel
    macs = rows * width * width * parts
    if written is not None:
        body = enter_read_kernel
        args += [w_mem, written["phi_keys_low"], written["delta_low"], written["beta_row"]]
        in_specs += [whole((width, width))] + [whole(a.shape) for a in args[5:]]
        out_shape += [
            shaped((rows, width), f32),
            shaped((rows, width), f32),
            shaped((rows, mems), f32),
        ]
        out_specs += [result((rows, width)), result((rows, width)), result((rows, mems))]
        macs += rows * width * width
    return pl.pallas_call(
        body,
        grid=(parts,),
        in_specs=in_specs,
        out_specs=out_specs,
        out_shape=out_shape,
        scratch_shapes=[pltpu.VMEM((rows, width), low_type)],
        compiler_params=params(),
        cost_estimate=pl.CostEstimate(
            flops=2 * macs, bytes_accessed=20 * 2**20, transcendentals=0
        ),
        name="enter_read" if written is not None else "enter",
    )(*args)


def query_blocks(rows, seg_rows):
    step = 256 if seg_rows % 256 == 0 else seg_rows
    blocks = [(at, step) for at in range(0, seg_rows, step)]
    return blocks + [(seg_rows, rows - seg_rows)]


def packed_lanes(rows, seg_rows):
    places = []
    at = 0
    for _, count in query_blocks(rows, seg_rows):
        places.append(at)
        at += -(-2 * count // 128) * 128
    return places, at


def stack_heads(block):
    lanes = lax.broadcasted_iota(jnp.int32, block.shape, 1)
    zero = jnp.zeros_like(block)
    return jnp.concatenate(
        [jnp.where(lanes < HD, block, zero), jnp.where(lanes < HD, zero, block)], axis=0
    )


def merge_heads(stacked):
    count = stacked.shape[0] // 2
    lanes = lax.broadcasted_iota(jnp.int32, (count, stacked.shape[1]), 1)
    return jnp.where(lanes < HD, stacked[:count], stacked[count:])


def as_row(column):
    count = column.shape[0]
    return jnp.transpose(jnp.broadcast_to(column, (count, 128)))[0:1, :]


def attend_kernel(seg_rows, qkv_ref, attended_ref, log_ref):
    rows = qkv_ref.shape[1]
    places, _ = packed_lanes(rows, seg_rows)
    for (start, count), place in zip(query_blocks(rows, seg_rows), places):
        reach = start + count
        queries = stack_heads(qkv_ref[0, start:reach, :] * score_scale)
        raw = nt(queries, qkv_ref[1, :reach, :])
        place_of = lax.broadcasted_iota(jnp.int32, (2 * count, count), 0)
        place_of = jnp.where(place_of < count, place_of, place_of - count)
        allowed = place_of >= lax.broadcasted_iota(jnp.int32, (2 * count, count), 1)
        edge = jnp.where(allowed, raw[:, start:], -1e30)
        masked = jnp.concatenate([raw[:, :start], edge], axis=1) if start else edge
        peak = jnp.max(masked, axis=1, keepdims=True)
        grown = jnp.exp(masked - peak)
        total = jnp.sum(grown, axis=1, keepdims=True)
        probs = low(grown * (1.0 / total))
        mixed = merge_heads(nn(probs, qkv_ref[2, :reach, :]))
        attended_ref[start:reach, :] = low(mixed)
        log_row = as_row(peak + jnp.log(total))
        log_ref[0, 0:1, place : place + 2 * count] = log_row


def attend(qkv, seg_rows):
    parts, rows, width = qkv.shape
    _, lanes = packed_lanes(rows, seg_rows)
    pairs = width // PAIR
    return pl.pallas_call(
        functools.partial(attend_kernel, seg_rows),
        grid=(pairs,),
        in_specs=[pl.BlockSpec((parts, rows, PAIR), lambda h: (0, 0, h))],
        out_specs=[
            pl.BlockSpec((rows, PAIR), lambda h: (0, h)),
            pl.BlockSpec((1, 1, lanes), lambda h: (h, 0, 0)),
        ],
        out_shape=[shaped((rows, width), low_type), shaped((pairs, 1, lanes), f32)],
        compiler_params=params(),
        cost_estimate=pl.CostEstimate(
            flops=4 * rows * rows * width, bytes_accessed=7 * 2**20, transcendentals=0
        ),
        name="attend",
    )(qkv)


def attend_back_kernel(seg_rows, qkv_ref, grad_ref, attended_ref, log_ref, out_ref, keys_sum, values_sum):
    rows = qkv_ref.shape[1]
    places, _ = packed_lanes(rows, seg_rows)
    ones = jnp.ones((8, PAIR), f32)
    blocks = list(zip(query_blocks(rows, seg_rows), places))
    for order, ((start, count), place) in enumerate(reversed(blocks)):
        reach = start + count
        queries = stack_heads(qkv_ref[0, start:reach, :] * score_scale)
        grads = stack_heads(grad_ref[start:reach, :])
        mixed = attended_ref[start:reach, :].astype(f32)
        both = jnp.concatenate([mixed, mixed], axis=0) * grads.astype(f32)
        inner = lax.dot_general(
            ones,
            both,
            (((1,), (1,)), ((), ())),
            precision=lax.Precision.HIGHEST,
            preferred_element_type=f32,
        )[0:1, :]
        keys = qkv_ref[1, :reach, :]
        raw = nt(keys, queries)
        log_row = log_ref[0, 0:1, place : place + 2 * count]
        probs = jnp.exp(raw - log_row)
        place_of = lax.broadcasted_iota(jnp.int32, (count, 2 * count), 1)
        place_of = jnp.where(place_of < count, place_of, place_of - count)
        allowed = place_of >= lax.broadcasted_iota(jnp.int32, (count, 2 * count), 0)
        edge = jnp.where(allowed, probs[start:], 0.0)
        probs = jnp.concatenate([probs[:start], edge], axis=0) if start else edge
        grad_probs = nt(qkv_ref[2, :reach, :], grads)
        grad_raw = low(probs * (grad_probs - inner))
        value_part = nn(low(probs), grads)
        key_part = nn(grad_raw, queries)
        if order == 0:
            values_sum[...] = value_part
            keys_sum[...] = key_part
        else:
            values_sum[:reach, :] += value_part
            keys_sum[:reach, :] += key_part
        out_ref[0, start:reach, :] = low(merge_heads(tn(grad_raw, keys)) * score_scale)
    out_ref[1] = low(keys_sum[...])
    out_ref[2] = low(values_sum[...])


def attend_back(qkv, grad_attended, attended, logs, seg_rows):
    parts, rows, width = qkv.shape
    pairs = width // PAIR
    column = pl.BlockSpec((rows, PAIR), lambda h: (0, h))
    three = pl.BlockSpec((parts, rows, PAIR), lambda h: (0, 0, h))
    return pl.pallas_call(
        functools.partial(attend_back_kernel, seg_rows),
        grid=(pairs,),
        in_specs=[
            three,
            column,
            column,
            pl.BlockSpec((1,) + logs.shape[1:], lambda h: (h, 0, 0)),
        ],
        out_specs=three,
        out_shape=shaped((parts, rows, width), low_type),
        scratch_shapes=[pltpu.VMEM((rows, PAIR), f32), pltpu.VMEM((rows, PAIR), f32)],
        compiler_params=params(),
        cost_estimate=pl.CostEstimate(
            flops=10 * rows * rows * width, bytes_accessed=13 * 2**20, transcendentals=0
        ),
        name="attend_back",
    )(qkv, grad_attended, attended, logs)


def leave_kernel(
    reads, earlier, *refs
):
    if reads:
        (states_one_ref, *refs) = refs
    else:
        (tokens_ref, mem_ref, *refs) = refs
    (attended_ref, gains_ref, w_out_ref, w_up_ref, w_down_ref, *refs) = refs
    if earlier:
        refs = refs[1:]
    (out_ref, mem_out_ref, states_two_ref, normed_ref, upward_ref, sum_ref, *scratch) = refs
    rows, width = attended_ref.shape
    seg_rows = out_ref.shape[0]
    step = pl.program_id(0)

    @pl.when(step == 0)
    def _():
        if not reads:
            load_first(tokens_ref, mem_ref, scratch[0])

        def chunk(at):
            source = states_one_ref if reads else scratch[0]
            states = source[at, :].astype(f32) + nn(attended_ref[at, :], w_out_ref[...])
            states_two_ref[at, :] = states
            unit, _ = normal_form(states)
            normed_ref[at, :] = low(unit * gains_ref[1:2, :])
            sum_ref[at, :] = states

        over_rows(rows, chunk)

    def chunk(at):
        upward = nn(normed_ref[at, :], w_up_ref[...])
        upward_ref[at, :] = upward
        bent = jnp.tanh(upward * (gelu_c + gelu_c * gelu_a * (upward * upward)))
        active = low(upward * (0.5 + 0.5 * bent))
        sum_ref[at, :] += nn(active, w_down_ref[...])

    chunk(pl.ds(0, rows))

    @pl.when(step == pl.num_programs(0) - 1)
    def _():
        out_ref[...] = low(sum_ref[:seg_rows, :])
        mem_out_ref[...] = sum_ref[seg_rows:, :]


def leave_segment(slot, slots, seg_rows, start, attended, gains, w_out, w_up, w_down, earlier):
    rows, width = attended.shape
    hidden = w_up.shape[1]
    size = 512 if hidden % 512 == 0 else hidden
    reads = not isinstance(start, tuple)
    args = []
    in_specs = []
    scratch = [pltpu.VMEM((rows, width), f32)]
    if reads:
        args.append(start)
        in_specs.append(whole((rows, width)))
    else:
        tokens, mem_tokens = start
        args += [tokens, mem_tokens]
        in_specs += [
            pl.BlockSpec((None, seg_rows, width), lambda j: (slot, 0, 0), pipeline_mode=pl.Buffered(1)),
            whole(mem_tokens.shape),
        ]
        scratch.append(pltpu.VMEM((rows, width), low_type))
    args += [attended, gains, w_out, w_up, w_down]
    in_specs += [
        whole((rows, width)),
        whole(gains.shape),
        whole((width, width)),
        pl.BlockSpec((width, size), lambda j: (0, j)),
        pl.BlockSpec((size, width), lambda j: (j, 0)),
    ]
    aliases = {}
    if earlier is not None:
        aliases = {len(args): 0}
        args.append(earlier)
        in_specs.append(pl.BlockSpec(memory_space=pl.ANY))
    return pl.pallas_call(
        functools.partial(leave_kernel, reads, earlier is not None),
        grid=(hidden // size,),
        in_specs=in_specs,
        out_specs=[
            pl.BlockSpec((None, seg_rows, width), lambda j: (slot, 0, 0)),
            result((rows - seg_rows, width)),
            result((rows, width)),
            result((rows, width)),
            pl.BlockSpec((rows, size), lambda j: (0, j)),
        ],
        out_shape=[
            shaped((slots, seg_rows, width), low_type),
            shaped((rows - seg_rows, width), f32),
            shaped((rows, width), f32),
            shaped((rows, width), low_type),
            shaped((rows, hidden), f32),
        ],
        scratch_shapes=scratch,
        input_output_aliases=aliases,
        compiler_params=params(),
        cost_estimate=pl.CostEstimate(
            flops=2 * rows * width * (width + 2 * hidden), bytes_accessed=36 * 2**20, transcendentals=0
        ),
        name="leave",
    )(*args)


def beta_parts(mem_out, w_beta):
    column = jnp.sum(mem_out * w_beta, axis=1, keepdims=True)
    row = lax.dot_general(
        w_beta,
        mem_out,
        (((1,), (1,)), ((), ())),
        precision=lax.Precision.HIGHEST,
        preferred_element_type=f32,
    )
    return jax.nn.sigmoid(column), jax.nn.sigmoid(row)


def write_kernel(
    flag_ref,
    mem_out_ref,
    w_key_ref,
    w_value_ref,
    w_beta_ref,
    key_ref,
    value_ref,
    phi_ref,
    phi_rest_ref,
    delta_ref,
    beta_row_ref,
):
    flag = flag_ref[0]
    width = key_ref.shape[1]
    mem_out = mem_out_ref[...]
    mem_low = low(mem_out)
    key = nn(mem_low, w_key_ref[...])
    value = nn(mem_low, w_value_ref[...])
    key_ref[...] = key
    value_ref[...] = value
    for index, part in enumerate(feature_parts(softplus(key))):
        high, rest = split(part)
        phi_ref[:, index * width : (index + 1) * width] = high
        phi_rest_ref[:, index * width : (index + 1) * width] = rest
    beta, beta_row = beta_parts(mem_out, w_beta_ref[...])
    delta_ref[...] = low(low(beta * value).astype(f32) * flag)
    beta_row_ref[...] = beta_row * flag


def write_memory(flag, mem_out, w_mem, w_beta):
    mems, width = mem_out.shape
    names = ("key", "value", "phi_keys_low", "phi_keys_rest", "delta_low", "beta_row")
    out_shape = [
        shaped((mems, width), f32),
        shaped((mems, width), f32),
        shaped((mems, 3 * width), low_type),
        shaped((mems, 3 * width), low_type),
        shaped((mems, width), low_type),
        shaped((1, mems), f32),
    ]
    outs = pl.pallas_call(
        write_kernel,
        grid=(1,),
        in_specs=[
            pl.BlockSpec(memory_space=pltpu.SMEM),
            whole((mems, width)),
            pl.BlockSpec((width, width), lambda j: (0, 1)),
            pl.BlockSpec((width, width), lambda j: (0, 2)),
            whole((1, width)),
        ],
        out_specs=[result(s.shape) for s in out_shape],
        out_shape=out_shape,
        compiler_params=params(),
        name="write",
    )(flag, mem_out, w_mem, w_mem, w_beta)
    return dict(zip(names, outs))


def write_back_kernel(
    flag_ref,
    mem_out_ref,
    w_key_ref,
    w_value_ref,
    w_beta_ref,
    key_ref,
    value_ref,
    grad_delta_ref,
    grad_phi_ref,
    grad_normal_ref,
    grad_rows_ref,
    grad_w_ref,
    grad_beta_ref,
):
    flag = flag_ref[0]
    width = key_ref.shape[1]
    mem_out = mem_out_ref[...]
    mem_low = low(mem_out)
    w_beta = w_beta_ref[...]
    key = key_ref[...]
    value = value_ref[...]
    beta, _ = beta_parts(mem_out, w_beta)
    softer = softplus(key)
    parts = feature_parts(softer)
    grad_delta = grad_delta_ref[...] * flag
    grad_strength = jnp.sum(grad_delta * value, axis=1, keepdims=True)
    grads = []
    for index, part in enumerate(parts):
        at = slice(index * width, (index + 1) * width)
        grad_normal = grad_normal_ref[:, at] * flag
        grad_strength += jnp.sum(part * grad_normal, axis=1, keepdims=True)
        grads.append(grad_phi_ref[:, at] * flag + beta * grad_normal)
    grad_key = low(feature_back(grads, softer, key))
    grad_value = low(beta * grad_delta)
    grad_logit = grad_strength * beta * (1.0 - beta)
    grad_rows_ref[...] = (
        grad_logit * w_beta + nt(grad_key, w_key_ref[...]) + nt(grad_value, w_value_ref[...])
    )
    grad_beta_ref[...] = jnp.sum(grad_logit * mem_out, axis=0, keepdims=True)
    grad_w_ref[:, :width] = low(tn(mem_low, grad_key))
    grad_w_ref[:, width:] = low(tn(mem_low, grad_value))


def write_back(flag, mem_out, w_mem, w_beta, written, grad_delta, grad_phi, grad_normal):
    mems, width = mem_out.shape
    args = [flag, mem_out, w_mem, w_mem, w_beta, written["key"], written["value"]]
    args += [grad_delta, grad_phi, grad_normal]
    out_shape = [
        shaped((mems, width), f32),
        shaped((width, 2 * width), low_type),
        shaped((1, width), f32),
    ]
    return pl.pallas_call(
        write_back_kernel,
        grid=(1,),
        in_specs=[
            pl.BlockSpec(memory_space=pltpu.SMEM),
            whole((mems, width)),
            pl.BlockSpec((width, width), lambda j: (0, 1)),
            pl.BlockSpec((width, width), lambda j: (0, 2)),
        ]
        + [whole(a.shape) for a in args[4:]],
        out_specs=[result(s.shape) for s in out_shape],
        out_shape=out_shape,
        compiler_params=params(),
        name="write_back",
    )(*args)


def leave_back_kernel(writes, adds, *refs):
    (out_grad_ref, *refs) = refs
    if writes:
        (grad_rows_ref, *refs) = refs
    (
        states_two_ref,
        normed_ref,
        upward_ref,
        attended_ref,
        gains_ref,
        w_out_ref,
        w_up_ref,
        w_down_ref,
        *refs,
    ) = refs
    if adds:
        (up_in_ref, down_in_ref, out_in_ref, *refs) = refs
    (
        grad_states_ref,
        grad_attended_ref,
        grad_up_ref,
        grad_down_ref,
        grad_out_ref,
        grad_gain_ref,
        grad_low_ref,
        sum_ref,
        grad_two_ref,
    ) = refs
    rows, width = normed_ref.shape
    seg_rows = out_grad_ref.shape[0]
    step = pl.program_id(0)

    @pl.when(step == 0)
    def _():
        grad_low_ref[:seg_rows, :] = out_grad_ref[...]
        grad_states_ref[:seg_rows, :] = out_grad_ref[...].astype(f32)
        if writes:
            grad_low_ref[seg_rows:, :] = low(grad_rows_ref[...])
            grad_states_ref[seg_rows:, :] = grad_rows_ref[...]
        else:
            grad_low_ref[seg_rows:, :] = jnp.zeros((rows - seg_rows, width), low_type)
            grad_states_ref[seg_rows:, :] = jnp.zeros((rows - seg_rows, width), f32)
        sum_ref[...] = jnp.zeros_like(sum_ref)

    upward = upward_ref[...]
    square = upward * upward
    bent = jnp.tanh(upward * (gelu_c + gelu_c * gelu_a * square))
    half = 0.5 + 0.5 * bent
    active = upward * half
    slope = half + (active - active * half) * (2.0 * gelu_c + 6.0 * gelu_c * gelu_a * square)
    grad_low = grad_low_ref[...]
    grad_upward = low(nt(grad_low, w_down_ref[...]) * slope)
    grad_down = tn(low(active), grad_low)
    grad_up = tn(normed_ref[...], grad_upward)
    sum_ref[...] += nt(grad_upward, w_up_ref[...])
    if adds:
        grad_down += down_in_ref[...]
        grad_up += up_in_ref[...]
    grad_down_ref[...] = grad_down.astype(grad_down_ref.dtype)
    grad_up_ref[...] = grad_up.astype(grad_up_ref.dtype)

    @pl.when(step == pl.num_programs(0) - 1)
    def _():
        gain = gains_ref[1:2, :]
        grad_gain_ref[...] = jnp.zeros_like(grad_gain_ref)

        def chunk(at):
            unit, inverse = normal_form(states_two_ref[at, :])
            grad = sum_ref[at, :]
            grad_gain_ref[...] += jnp.sum(grad * unit, axis=0, keepdims=True)
            total = grad_states_ref[at, :] + norm_back(grad, unit, inverse, gain)
            grad_states_ref[at, :] = total
            total_low = low(total)
            grad_two_ref[at, :] = total_low
            grad_attended_ref[at, :] = low(nt(total_low, w_out_ref[...]))

        over_rows(rows, chunk)
        grad_out = tn(attended_ref[...], grad_two_ref[...])
        if adds:
            grad_out += out_in_ref[...]
        grad_out_ref[...] = grad_out.astype(grad_out_ref.dtype)


def leave_back(slot, out_grad, grad_rows, kept, gains, w_out, w_up, w_down, sums, grad_type):
    _, seg_rows, width = out_grad.shape
    rows = kept["normed_two"].shape[0]
    hidden = w_up.shape[1]
    size = 512 if hidden % 512 == 0 else hidden
    up_spec = pl.BlockSpec((width, size), lambda j: (0, j))
    down_spec = pl.BlockSpec((size, width), lambda j: (j, 0))
    args = [out_grad]
    in_specs = [
        pl.BlockSpec((None, seg_rows, width), lambda j: (slot, 0, 0), pipeline_mode=pl.Buffered(1))
    ]
    if grad_rows is not None:
        args.append(grad_rows)
        in_specs.append(whole(grad_rows.shape))
    args += [kept["states_two"], kept["normed_two"], kept["upward"], kept["attended"]]
    args += [gains, w_out, w_up, w_down]
    in_specs += [
        whole((rows, width)),
        whole((rows, width)),
        pl.BlockSpec((rows, size), lambda j: (0, j)),
        whole((rows, width)),
        whole(gains.shape),
        whole((width, width)),
        up_spec,
        down_spec,
    ]
    if sums is not None:
        args += [sums["up"], sums["down"], sums["out"]]
        in_specs += [up_spec, down_spec, whole((width, width))]
    return pl.pallas_call(
        functools.partial(leave_back_kernel, grad_rows is not None, sums is not None),
        grid=(hidden // size,),
        in_specs=in_specs,
        out_specs=[
            result((rows, width)),
            result((rows, width)),
            up_spec,
            down_spec,
            result((width, width)),
            result((1, width)),
        ],
        out_shape=[
            shaped((rows, width), f32),
            shaped((rows, width), low_type),
            shaped((width, hidden), grad_type),
            shaped((hidden, width), grad_type),
            shaped((width, width), grad_type),
            shaped((1, width), f32),
        ],
        scratch_shapes=[
            pltpu.VMEM((rows, width), low_type),
            pltpu.VMEM((rows, width), f32),
            pltpu.VMEM((rows, width), low_type),
        ],
        compiler_params=params(),
        cost_estimate=pl.CostEstimate(
            flops=4 * rows * width * (width + 2 * hidden), bytes_accessed=60 * 2**20, transcendentals=0
        ),
        name="leave_back",
    )(*args)


def enter_back_kernel(reads, adds, earlier, *refs):
    (tokens_ref, mem_ref, normed_ref, grad_qkv_ref, grad_states_ref, gains_ref, w_ref, *refs) = refs
    if reads:
        (
            states_ref,
            query_ref,
            match_ref,
            w_query_ref,
            phi_keys_ref,
            phi_rest_ref,
            delta_ref,
            beta_ref,
            *refs,
        ) = refs
    if adds:
        (w_in_ref, *refs) = refs
    if earlier:
        refs = refs[1:]
    (grad_tokens_ref, grad_mem_ref, grad_w_ref, grad_gain_ref, *refs) = refs
    if reads:
        (grad_w_query_ref, grad_delta_ref, grad_phi_ref, grad_normal_ref, *refs) = refs
    (first_ref, sum_ref, *refs) = refs
    rows, width = normed_ref.shape
    seg_rows = tokens_ref.shape[0]
    step = pl.program_id(0)

    @pl.when(step == 0)
    def _():
        load_first(tokens_ref, mem_ref, first_ref)
        sum_ref[...] = jnp.zeros_like(sum_ref)

    grad_part = grad_qkv_ref[0]
    sum_ref[...] += nt(grad_part, w_ref[...])
    grad_w = tn(normed_ref[...], grad_part)
    if adds:
        grad_w += w_in_ref[...]
    grad_w_ref[...] = grad_w.astype(grad_w_ref.dtype)

    @pl.when(step == pl.num_programs(0) - 1)
    def _():
        gain = gains_ref[0:1, :]
        grad_gain_ref[...] = jnp.zeros_like(grad_gain_ref)
        if reads:
            (grad_query_ref, packed_sum_ref, delta_sum_ref) = refs
            packed_sum_ref[...] = jnp.zeros_like(packed_sum_ref)
            delta_sum_ref[...] = jnp.zeros_like(delta_sum_ref)
            mems = delta_ref.shape[0]
            beta = beta_ref[...]
            basis = jnp.concatenate([phi_keys_ref[...], phi_keys_ref[...], phi_rest_ref[...]], axis=0)

        def chunk(at):
            first = first_ref[at, :].astype(f32)
            states = states_ref[at, :] if reads else first
            unit, inverse = normal_form(states)
            grad = sum_ref[at, :]
            grad_gain_ref[...] += jnp.sum(grad * unit, axis=0, keepdims=True)
            total = grad_states_ref[at, :] + norm_back(grad, unit, inverse, gain)
            if reads:
                match = match_ref[at, :]
                below = 1.0 + jnp.sum(match * beta, axis=1, keepdims=True)
                grad_num = low(total / below)
                grad_below = -jnp.sum(total * (states - first), axis=1, keepdims=True) / below
                pulled = nt(grad_num, delta_ref[...])
                spread_below = grad_below * beta
                both_high, both_low = split(pulled + spread_below)
                weights = jnp.concatenate([both_high, both_low, low(spread_below)], axis=1)
                query = query_ref[at, :]
                softer = softplus(query)
                parts = feature_parts(softer)
                grads = []
                packed = jnp.concatenate(
                    list(split(pulled))
                    + [low(jnp.broadcast_to(part, pulled.shape)) for part in (grad_below,)]
                    + [
                        low(
                            jnp.broadcast_to(
                                grad_below - low(grad_below).astype(f32), pulled.shape
                            )
                        )
                    ],
                    axis=1,
                )
                for index, part in enumerate(parts):
                    cols = slice(index * width, (index + 1) * width)
                    grads.append(nn(weights, basis[:, cols]))
                    packed_sum_ref[:, cols] += tn(packed, low(part))
                delta_sum_ref[...] += tn(jnp.concatenate(split(match), axis=1), grad_num)
                grad_query = low(feature_back(grads, softer, query))
                grad_query_ref[at, :] = grad_query
                total += nt(grad_query, w_query_ref[...])
            sum_ref[at, :] = total

        over_rows(rows, chunk)
        grad_tokens_ref[...] = sum_ref[:seg_rows, :]
        grad_mem_ref[...] = sum_ref[seg_rows:, :]
        if reads:
            grad_w_query_ref[...] = low(tn(first_ref[...], grad_query_ref[...]))
            grad_delta_ref[...] = delta_sum_ref[:mems, :] + delta_sum_ref[mems:, :]
            grad_phi_ref[...] = packed_sum_ref[:mems, :] + packed_sum_ref[mems : 2 * mems, :]
            grad_normal_ref[...] = (
                packed_sum_ref[2 * mems : 2 * mems + 1, :]
                + packed_sum_ref[3 * mems : 3 * mems + 1, :]
            )


def enter_back(
    slot, tokens, mem_tokens, kept, grad_qkv, grad_states, gains, w_qkv, w_mem, written, w_sum, earlier, grad_type
):
    slots, seg_rows, width = tokens.shape
    mems = mem_tokens.shape[0]
    rows = seg_rows + mems
    parts = grad_qkv.shape[0]
    reads = written is not None
    args = [tokens, mem_tokens, kept["normed_one"], grad_qkv, grad_states, gains, w_qkv]
    in_specs = [
        pl.BlockSpec((None, seg_rows, width), lambda j: (slot, 0, 0), pipeline_mode=pl.Buffered(1)),
        whole((mems, width)),
        whole((rows, width)),
        pl.BlockSpec((1, rows, width), lambda j: (j, 0, 0)),
        whole((rows, width)),
        whole(gains.shape),
        pl.BlockSpec((width, width), lambda j: (0, j)),
    ]
    scratch = [pltpu.VMEM((rows, width), low_type), pltpu.VMEM((rows, width), f32)]
    if reads:
        more = [written["phi_keys_low"], written["phi_keys_rest"]]
        more += [written["delta_low"], written["beta_row"]]
        args += [kept["states_one"], kept["query"], kept["match"], w_mem] + more
        in_specs += [whole((rows, width)), whole((rows, width)), whole((rows, mems)), whole((width, width))]
        in_specs += [whole(a.shape) for a in more]
        scratch += [
            pltpu.VMEM((rows, width), low_type),
            pltpu.VMEM((4 * mems, 3 * width), f32),
            pltpu.VMEM((2 * mems, width), f32),
        ]
    if w_sum is not None:
        args.append(w_sum)
        in_specs.append(pl.BlockSpec((width, width), lambda j: (0, j)))
    aliases = {}
    if earlier is not None:
        aliases = {len(args): 0}
        args.append(earlier)
        in_specs.append(pl.BlockSpec(memory_space=pl.ANY))
    out_specs = [
        pl.BlockSpec((None, seg_rows, width), lambda j: (slot, 0, 0)),
        result((mems, width)),
        pl.BlockSpec((width, width), lambda j: (0, j)),
        result((1, width)),
    ]
    out_shape = [
        shaped((slots, seg_rows, width), f32),
        shaped((mems, width), f32),
        shaped((width, parts * width), grad_type),
        shaped((1, width), f32),
    ]
    if reads:
        extra = [
            shaped((width, width), low_type),
            shaped((mems, width), f32),
            shaped((mems, 3 * width), f32),
            shaped((1, 3 * width), f32),
        ]
        out_shape += extra
        out_specs += [result(s.shape) for s in extra]
    return pl.pallas_call(
        functools.partial(enter_back_kernel, reads, w_sum is not None, earlier is not None),
        grid=(parts,),
        in_specs=in_specs,
        out_specs=out_specs,
        out_shape=out_shape,
        scratch_shapes=scratch,
        input_output_aliases=aliases,
        compiler_params=params(),
        cost_estimate=pl.CostEstimate(
            flops=4 * rows * width * width * (parts + 1), bytes_accessed=30 * 2**20, transcendentals=0
        ),
        name="enter_back",
    )(*args)


def gather_weights(shards):
    return [lax.all_gather(shard, AXES, axis=0, tiled=True) for shard in shards]


def scatter_sums(totals):
    return [
        lax.psum_scatter(total.astype(f32), AXES, scatter_dimension=0, tiled=True)
        for total in totals
    ]


def on_device(
    tokens, item_ids, w_mem, w_qkv, w_out, w_up, w_down, mem_tokens, gains, w_beta, out_grad
):
    slots, seg_rows, width = tokens.shape
    gains = gains.astype(f32)
    w_beta = w_beta.astype(f32).reshape(1, width)
    w_qkv, w_out, w_up, w_down, w_mem = gather_weights([w_qkv, w_out, w_up, w_down, w_mem])
    same_item = jnp.where(item_ids[1:] == item_ids[:-1], 1.0, 0.0).astype(f32)
    kept_all = []
    written = [None] * (slots + 1)
    out = None
    for slot in range(slots):
        kept = {}
        entered = enter_segment(slot, tokens, mem_tokens, gains, w_qkv, w_mem, written[slot])
        kept["normed_one"], kept["qkv"] = entered[:2]
        start = (tokens, mem_tokens)
        if written[slot] is not None:
            kept["states_one"], kept["query"], kept["match"] = entered[2:]
            start = kept["states_one"]
        kept["attended"], kept["logs"] = attend(kept["qkv"], seg_rows)
        out, mem_out, kept["states_two"], kept["normed_two"], kept["upward"] = leave_segment(
            slot, slots, seg_rows, start, kept["attended"], gains, w_out, w_up, w_down, out
        )
        kept["mem_out"] = mem_out
        if slot + 1 < slots:
            written[slot + 1] = write_memory(same_item[slot : slot + 1], mem_out, w_mem, w_beta)
        kept_all.append(kept)

    sums = None
    qkv_sum = None
    grad_tokens = None
    grad_mem_tokens = 0.0
    grad_gains = 0.0
    grad_beta = 0.0
    pulled = None
    for slot in reversed(range(slots)):
        kept = kept_all[slot]
        grad_type = f32 if slot else low_type
        grad_rows = None
        if slot + 1 < slots:
            grad_rows, w_pair_sum, grad_beta_part = write_back(
                same_item[slot : slot + 1], kept["mem_out"], w_mem, w_beta, written[slot + 1], *pulled
            )
            grad_beta += grad_beta_part
        grad_states, grad_attended, up_sum, down_sum, out_sum, gain_two = leave_back(
            slot, out_grad, grad_rows, kept, gains, w_out, w_up, w_down, sums, grad_type
        )
        sums = {"up": up_sum, "down": down_sum, "out": out_sum}
        grad_qkv = attend_back(kept["qkv"], grad_attended, kept["attended"], kept["logs"], seg_rows)
        grad_tokens, grad_mem, qkv_sum, gain_one, *extra = enter_back(
            slot,
            tokens,
            mem_tokens,
            kept,
            grad_qkv,
            grad_states,
            gains,
            w_qkv,
            w_mem,
            written[slot],
            qkv_sum,
            grad_tokens,
            grad_type,
        )
        if written[slot] is not None:
            w_query_sum, *pulled = extra
        grad_mem_tokens += grad_mem
        grad_gains += jnp.concatenate([gain_one, gain_two], axis=0)
    mem_sum = jnp.concatenate([w_query_sum, w_pair_sum], axis=1)
    summed = scatter_sums([mem_sum, qkv_sum, sums["out"], sums["up"], sums["down"]])
    small = lax.psum((grad_mem_tokens, grad_gains, grad_beta.reshape(width)), AXES)
    return (out, grad_tokens, *summed, *small)


def solution(mesh):
    split_rows = P(AXES, None)
    split_items = P(AXES, None, None)
    in_specs = (
        split_items,
        P(AXES),
        split_rows,
        split_rows,
        split_rows,
        split_rows,
        split_rows,
        P(),
        P(),
        P(),
        split_items,
    )
    out_specs = (
        split_items,
        split_items,
        split_rows,
        split_rows,
        split_rows,
        split_rows,
        split_rows,
        P(),
        P(),
        P(),
    )
    return jax.shard_map(
        on_device, mesh=mesh, in_specs=in_specs, out_specs=out_specs, check_vma=False
    )
```

```python
import functools

import jax
import jax.numpy as jnp
from jax import lax
from jax.experimental import pallas as pl
from jax.experimental.pallas import tpu as pltpu
from jax.sharding import PartitionSpec as P

HD = 64
PAIR = 2 * HD
AXES = ("wide", "narrow")
eps_norm = 1e-05
score_scale = 0.125
gelu_c = 0.7978845608028654
gelu_a = 0.044715
f32 = jnp.float32
low_type = jnp.bfloat16
VMEM_BYTES = 60 * 2**20


def nn(left, right):
    return lax.dot_general(left, right, (((1,), (0,)), ((), ())), preferred_element_type=f32)


def nt(left, right):
    return lax.dot_general(left, right, (((1,), (1,)), ((), ())), preferred_element_type=f32)


def tn(left, right):
    return lax.dot_general(left, right, (((0,), (0,)), ((), ())), preferred_element_type=f32)


def low(values):
    return values.astype(low_type)


def split(values):
    high = low(values)
    return high, low(values - high.astype(f32))


def row_chunk(rows):
    for count in (208, 256, 128, 80, 64, 16):
        if rows % count == 0:
            return count
    return rows


def over_rows(rows, body):
    count = row_chunk(rows)

    @pl.loop(0, rows // count)
    def _(step):
        body(pl.ds(pl.multiple_of(step * count, count), count))


def normal_form(values):
    average = jnp.mean(values, axis=-1, keepdims=True)
    centered = values - average
    spread = jnp.mean(centered * centered, axis=-1, keepdims=True)
    inverse = lax.rsqrt(spread + eps_norm)
    return centered * inverse, inverse


def norm_back(grad, unit, inverse, gain):
    scaled = grad * gain
    mean_grad = jnp.mean(scaled, axis=-1, keepdims=True)
    mean_unit = jnp.mean(scaled * unit, axis=-1, keepdims=True)
    return inverse * (scaled - mean_grad - unit * mean_unit)


def softplus(values):
    return jnp.maximum(values, 0.0) + jnp.log1p(jnp.exp(-jnp.abs(values)))


def feature_parts(softer):
    return [softer * pltpu.roll(softer, offset, 1) for offset in (1, 2, 3)]


def feature_back(grads, softer, values):
    width = softer.shape[1]
    total = None
    for offset, grad in zip((1, 2, 3), grads):
        term = grad * pltpu.roll(softer, offset, 1) + pltpu.roll(grad * softer, width - offset, 1)
        total = term if total is None else total + term
    return total * jax.nn.sigmoid(values)


def whole(shape, memory=None):
    zeros = (0,) * len(shape)
    return pl.BlockSpec(shape, lambda *_: zeros, pipeline_mode=pl.Buffered(1))


def result(shape):
    zeros = (0,) * len(shape)
    return pl.BlockSpec(shape, lambda *_: zeros)


def params(**extra):
    return pltpu.CompilerParams(vmem_limit_bytes=VMEM_BYTES, **extra)


def shaped(shape, dtype):
    return jax.ShapeDtypeStruct(shape, dtype)


def load_first(tokens_ref, mem_ref, first_ref):
    seg_rows = tokens_ref.shape[0]
    first_ref[:seg_rows, :] = tokens_ref[...]
    first_ref[seg_rows:, :] = mem_ref[...]


def enter_kernel(tokens_ref, mem_ref, gains_ref, w_ref, normed_ref, qkv_ref, first_ref):
    @pl.when(pl.program_id(0) == 0)
    def _():
        load_first(tokens_ref, mem_ref, first_ref)

        def chunk(at):
            unit, _ = normal_form(first_ref[at, :].astype(f32))
            normed_ref[at, :] = low(unit * gains_ref[0:1, :])

        over_rows(first_ref.shape[0], chunk)

    qkv_ref[0] = low(nn(normed_ref[...], w_ref[...]))


def enter_read_kernel(
    tokens_ref,
    mem_ref,
    gains_ref,
    w_ref,
    w_query_ref,
    phi_keys_ref,
    delta_ref,
    beta_ref,
    normed_ref,
    qkv_ref,
    states_ref,
    query_ref,
    match_ref,
    first_ref,
):
    @pl.when(pl.program_id(0) == 0)
    def _():
        load_first(tokens_ref, mem_ref, first_ref)
        width = first_ref.shape[1]
        delta_twice = jnp.concatenate([delta_ref[...], delta_ref[...]], axis=0)

        def chunk(at):
            first = first_ref[at, :]
            query = nn(first, w_query_ref[...])
            query_ref[at, :] = query
            parts = feature_parts(softplus(query))
            match = None
            for index, part in enumerate(parts):
                term = nt(low(part), phi_keys_ref[:, index * width : (index + 1) * width])
                match = term if match is None else match + term
            match_ref[at, :] = match
            numerator = nn(jnp.concatenate(split(match), axis=1), delta_twice)
            below = 1.0 + jnp.sum(match * beta_ref[...], axis=1, keepdims=True)
            states = first.astype(f32) + numerator / below
            states_ref[at, :] = states
            unit, _ = normal_form(states)
            normed_ref[at, :] = low(unit * gains_ref[0:1, :])

        over_rows(first_ref.shape[0], chunk)

    qkv_ref[0] = low(nn(normed_ref[...], w_ref[...]))


def enter_segment(slot, tokens, mem_tokens, gains, w_qkv, w_mem, written):
    slots, seg_rows, width = tokens.shape
    mems = mem_tokens.shape[0]
    rows = seg_rows + mems
    parts = w_qkv.shape[1] // width
    in_specs = [
        pl.BlockSpec((None, seg_rows, width), lambda j: (slot, 0, 0), pipeline_mode=pl.Buffered(1)),
        whole((mems, width)),
        whole(gains.shape),
        pl.BlockSpec((width, width), lambda j: (0, j)),
    ]
    out_shape = [shaped((rows, width), low_type), shaped((parts, rows, width), low_type)]
    out_specs = [
        result((rows, width)),
        pl.BlockSpec((1, rows, width), lambda j: (j, 0, 0)),
    ]
    args = [tokens, mem_tokens, gains, w_qkv]
    body = enter_kernel
    macs = rows * width * width * parts
    if written is not None:
        body = enter_read_kernel
        args += [w_mem, written["phi_keys_low"], written["delta_low"], written["beta_row"]]
        in_specs += [whole((width, width))] + [whole(a.shape) for a in args[5:]]
        out_shape += [
            shaped((rows, width), f32),
            shaped((rows, width), f32),
            shaped((rows, mems), f32),
        ]
        out_specs += [result((rows, width)), result((rows, width)), result((rows, mems))]
        macs += rows * width * width
    return pl.pallas_call(
        body,
        grid=(parts,),
        in_specs=in_specs,
        out_specs=out_specs,
        out_shape=out_shape,
        scratch_shapes=[pltpu.VMEM((rows, width), low_type)],
        compiler_params=params(),
        cost_estimate=pl.CostEstimate(
            flops=2 * macs, bytes_accessed=20 * 2**20, transcendentals=0
        ),
        name="enter_read" if written is not None else "enter",
    )(*args)


def query_blocks(rows, seg_rows):
    step = 256 if seg_rows % 256 == 0 else seg_rows
    blocks = [(at, step) for at in range(0, seg_rows, step)]
    return blocks + [(seg_rows, rows - seg_rows)]


def packed_lanes(rows, seg_rows):
    places = []
    at = 0
    for _, count in query_blocks(rows, seg_rows):
        places.append(at)
        at += -(-2 * count // 128) * 128
    return places, at


def stack_heads(block):
    lanes = lax.broadcasted_iota(jnp.int32, block.shape, 1)
    zero = jnp.zeros_like(block)
    return jnp.concatenate(
        [jnp.where(lanes < HD, block, zero), jnp.where(lanes < HD, zero, block)], axis=0
    )


def merge_heads(stacked):
    count = stacked.shape[0] // 2
    lanes = lax.broadcasted_iota(jnp.int32, (count, stacked.shape[1]), 1)
    return jnp.where(lanes < HD, stacked[:count], stacked[count:])


def as_row(column):
    count = column.shape[0]
    return jnp.transpose(jnp.broadcast_to(column, (count, 128)))[0:1, :]


def attend_kernel(seg_rows, qkv_ref, attended_ref, log_ref):
    rows = qkv_ref.shape[1]
    places, _ = packed_lanes(rows, seg_rows)
    for (start, count), place in zip(query_blocks(rows, seg_rows), places):
        reach = start + count
        queries = stack_heads(qkv_ref[0, start:reach, :] * score_scale)
        raw = nt(queries, qkv_ref[1, :reach, :])
        place_of = lax.broadcasted_iota(jnp.int32, (2 * count, count), 0)
        place_of = jnp.where(place_of < count, place_of, place_of - count)
        allowed = place_of >= lax.broadcasted_iota(jnp.int32, (2 * count, count), 1)
        edge = jnp.where(allowed, raw[:, start:], -1e30)
        masked = jnp.concatenate([raw[:, :start], edge], axis=1) if start else edge
        peak = jnp.max(masked, axis=1, keepdims=True)
        grown = jnp.exp(masked - peak)
        total = jnp.sum(grown, axis=1, keepdims=True)
        probs = low(grown * (1.0 / total))
        mixed = merge_heads(nn(probs, qkv_ref[2, :reach, :]))
        attended_ref[start:reach, :] = low(mixed)
        log_row = as_row(peak + jnp.log(total))
        log_ref[0, 0:1, place : place + 2 * count] = log_row


def attend(qkv, seg_rows):
    parts, rows, width = qkv.shape
    _, lanes = packed_lanes(rows, seg_rows)
    pairs = width // PAIR
    return pl.pallas_call(
        functools.partial(attend_kernel, seg_rows),
        grid=(pairs,),
        in_specs=[pl.BlockSpec((parts, rows, PAIR), lambda h: (0, 0, h))],
        out_specs=[
            pl.BlockSpec((rows, PAIR), lambda h: (0, h)),
            pl.BlockSpec((1, 1, lanes), lambda h: (h, 0, 0)),
        ],
        out_shape=[shaped((rows, width), low_type), shaped((pairs, 1, lanes), f32)],
        compiler_params=params(),
        cost_estimate=pl.CostEstimate(
            flops=4 * rows * rows * width, bytes_accessed=7 * 2**20, transcendentals=0
        ),
        name="attend",
    )(qkv)


def attend_back_kernel(seg_rows, qkv_ref, grad_ref, attended_ref, log_ref, out_ref, keys_sum, values_sum):
    rows = qkv_ref.shape[1]
    places, _ = packed_lanes(rows, seg_rows)
    ones = jnp.ones((8, PAIR), f32)
    blocks = list(zip(query_blocks(rows, seg_rows), places))
    for order, ((start, count), place) in enumerate(reversed(blocks)):
        reach = start + count
        queries = stack_heads(qkv_ref[0, start:reach, :] * score_scale)
        grads = stack_heads(grad_ref[start:reach, :])
        mixed = attended_ref[start:reach, :].astype(f32)
        both = jnp.concatenate([mixed, mixed], axis=0) * grads.astype(f32)
        inner = lax.dot_general(
            ones,
            both,
            (((1,), (1,)), ((), ())),
            precision=lax.Precision.HIGHEST,
            preferred_element_type=f32,
        )[0:1, :]
        keys = qkv_ref[1, :reach, :]
        raw = nt(keys, queries)
        log_row = log_ref[0, 0:1, place : place + 2 * count]
        probs = jnp.exp(raw - log_row)
        place_of = lax.broadcasted_iota(jnp.int32, (count, 2 * count), 1)
        place_of = jnp.where(place_of < count, place_of, place_of - count)
        allowed = place_of >= lax.broadcasted_iota(jnp.int32, (count, 2 * count), 0)
        edge = jnp.where(allowed, probs[start:], 0.0)
        probs = jnp.concatenate([probs[:start], edge], axis=0) if start else edge
        grad_probs = nt(qkv_ref[2, :reach, :], grads)
        grad_raw = low(probs * (grad_probs - inner))
        value_part = nn(low(probs), grads)
        key_part = nn(grad_raw, queries)
        if order == 0:
            values_sum[...] = value_part
            keys_sum[...] = key_part
        else:
            values_sum[:reach, :] += value_part
            keys_sum[:reach, :] += key_part
        out_ref[0, start:reach, :] = low(merge_heads(tn(grad_raw, keys)) * score_scale)
    out_ref[1] = low(keys_sum[...])
    out_ref[2] = low(values_sum[...])


def attend_back(qkv, grad_attended, attended, logs, seg_rows):
    parts, rows, width = qkv.shape
    pairs = width // PAIR
    column = pl.BlockSpec((rows, PAIR), lambda h: (0, h))
    three = pl.BlockSpec((parts, rows, PAIR), lambda h: (0, 0, h))
    return pl.pallas_call(
        functools.partial(attend_back_kernel, seg_rows),
        grid=(pairs,),
        in_specs=[
            three,
            column,
            column,
            pl.BlockSpec((1,) + logs.shape[1:], lambda h: (h, 0, 0)),
        ],
        out_specs=three,
        out_shape=shaped((parts, rows, width), low_type),
        scratch_shapes=[pltpu.VMEM((rows, PAIR), f32), pltpu.VMEM((rows, PAIR), f32)],
        compiler_params=params(),
        cost_estimate=pl.CostEstimate(
            flops=10 * rows * rows * width, bytes_accessed=13 * 2**20, transcendentals=0
        ),
        name="attend_back",
    )(qkv, grad_attended, attended, logs)


def leave_kernel(
    reads, earlier, *refs
):
    if reads:
        (states_one_ref, *refs) = refs
    else:
        (tokens_ref, mem_ref, *refs) = refs
    (attended_ref, gains_ref, w_out_ref, w_up_ref, w_down_ref, *refs) = refs
    if earlier:
        refs = refs[1:]
    (out_ref, mem_out_ref, states_two_ref, normed_ref, upward_ref, sum_ref, *scratch) = refs
    rows, width = attended_ref.shape
    seg_rows = out_ref.shape[0]
    step = pl.program_id(0)

    @pl.when(step == 0)
    def _():
        if not reads:
            load_first(tokens_ref, mem_ref, scratch[0])

        def chunk(at):
            source = states_one_ref if reads else scratch[0]
            states = source[at, :].astype(f32) + nn(attended_ref[at, :], w_out_ref[...])
            states_two_ref[at, :] = states
            unit, _ = normal_form(states)
            normed_ref[at, :] = low(unit * gains_ref[1:2, :])
            sum_ref[at, :] = states

        over_rows(rows, chunk)

    def chunk(at):
        upward = nn(normed_ref[at, :], w_up_ref[...])
        upward_ref[at, :] = upward
        bent = jnp.tanh(upward * (gelu_c + gelu_c * gelu_a * (upward * upward)))
        active = low(upward * (0.5 + 0.5 * bent))
        sum_ref[at, :] += nn(active, w_down_ref[...])

    chunk(pl.ds(0, rows))

    @pl.when(step == pl.num_programs(0) - 1)
    def _():
        out_ref[...] = low(sum_ref[:seg_rows, :])
        mem_out_ref[...] = sum_ref[seg_rows:, :]


def leave_segment(slot, slots, seg_rows, start, attended, gains, w_out, w_up, w_down, earlier):
    rows, width = attended.shape
    hidden = w_up.shape[1]
    size = 512 if hidden % 512 == 0 else hidden
    reads = not isinstance(start, tuple)
    args = []
    in_specs = []
    scratch = [pltpu.VMEM((rows, width), f32)]
    if reads:
        args.append(start)
        in_specs.append(whole((rows, width)))
    else:
        tokens, mem_tokens = start
        args += [tokens, mem_tokens]
        in_specs += [
            pl.BlockSpec((None, seg_rows, width), lambda j: (slot, 0, 0), pipeline_mode=pl.Buffered(1)),
            whole(mem_tokens.shape),
        ]
        scratch.append(pltpu.VMEM((rows, width), low_type))
    args += [attended, gains, w_out, w_up, w_down]
    in_specs += [
        whole((rows, width)),
        whole(gains.shape),
        whole((width, width)),
        pl.BlockSpec((width, size), lambda j: (0, j)),
        pl.BlockSpec((size, width), lambda j: (j, 0)),
    ]
    aliases = {}
    if earlier is not None:
        aliases = {len(args): 0}
        args.append(earlier)
        in_specs.append(pl.BlockSpec(memory_space=pl.ANY))
    return pl.pallas_call(
        functools.partial(leave_kernel, reads, earlier is not None),
        grid=(hidden // size,),
        in_specs=in_specs,
        out_specs=[
            pl.BlockSpec((None, seg_rows, width), lambda j: (slot, 0, 0)),
            result((rows - seg_rows, width)),
            result((rows, width)),
            result((rows, width)),
            pl.BlockSpec((rows, size), lambda j: (0, j)),
        ],
        out_shape=[
            shaped((slots, seg_rows, width), low_type),
            shaped((rows - seg_rows, width), f32),
            shaped((rows, width), f32),
            shaped((rows, width), low_type),
            shaped((rows, hidden), f32),
        ],
        scratch_shapes=scratch,
        input_output_aliases=aliases,
        compiler_params=params(),
        cost_estimate=pl.CostEstimate(
            flops=2 * rows * width * (width + 2 * hidden), bytes_accessed=36 * 2**20, transcendentals=0
        ),
        name="leave",
    )(*args)


def beta_parts(mem_out, w_beta):
    column = jnp.sum(mem_out * w_beta, axis=1, keepdims=True)
    row = lax.dot_general(
        w_beta,
        mem_out,
        (((1,), (1,)), ((), ())),
        precision=lax.Precision.HIGHEST,
        preferred_element_type=f32,
    )
    return jax.nn.sigmoid(column), jax.nn.sigmoid(row)


def write_kernel(
    flag_ref,
    mem_out_ref,
    w_key_ref,
    w_value_ref,
    w_beta_ref,
    key_ref,
    value_ref,
    phi_ref,
    phi_rest_ref,
    delta_ref,
    beta_row_ref,
):
    flag = flag_ref[0]
    width = key_ref.shape[1]
    mem_out = mem_out_ref[...]
    mem_low = low(mem_out)
    key = nn(mem_low, w_key_ref[...])
    value = nn(mem_low, w_value_ref[...])
    key_ref[...] = key
    value_ref[...] = value
    for index, part in enumerate(feature_parts(softplus(key))):
        high, rest = split(part)
        phi_ref[:, index * width : (index + 1) * width] = high
        phi_rest_ref[:, index * width : (index + 1) * width] = rest
    beta, beta_row = beta_parts(mem_out, w_beta_ref[...])
    delta_ref[...] = low(low(beta * value).astype(f32) * flag)
    beta_row_ref[...] = beta_row * flag


def write_memory(flag, mem_out, w_mem, w_beta):
    mems, width = mem_out.shape
    names = ("key", "value", "phi_keys_low", "phi_keys_rest", "delta_low", "beta_row")
    out_shape = [
        shaped((mems, width), f32),
        shaped((mems, width), f32),
        shaped((mems, 3 * width), low_type),
        shaped((mems, 3 * width), low_type),
        shaped((mems, width), low_type),
        shaped((1, mems), f32),
    ]
    outs = pl.pallas_call(
        write_kernel,
        grid=(1,),
        in_specs=[
            pl.BlockSpec(memory_space=pltpu.SMEM),
            whole((mems, width)),
            pl.BlockSpec((width, width), lambda j: (0, 1)),
            pl.BlockSpec((width, width), lambda j: (0, 2)),
            whole((1, width)),
        ],
        out_specs=[result(s.shape) for s in out_shape],
        out_shape=out_shape,
        compiler_params=params(),
        name="write",
    )(flag, mem_out, w_mem, w_mem, w_beta)
    return dict(zip(names, outs))


def write_back_kernel(
    flag_ref,
    mem_out_ref,
    w_key_ref,
    w_value_ref,
    w_beta_ref,
    key_ref,
    value_ref,
    grad_delta_ref,
    grad_phi_ref,
    grad_normal_ref,
    grad_rows_ref,
    grad_w_ref,
    grad_beta_ref,
):
    flag = flag_ref[0]
    width = key_ref.shape[1]
    mem_out = mem_out_ref[...]
    mem_low = low(mem_out)
    w_beta = w_beta_ref[...]
    key = key_ref[...]
    value = value_ref[...]
    beta, _ = beta_parts(mem_out, w_beta)
    softer = softplus(key)
    parts = feature_parts(softer)
    grad_delta = grad_delta_ref[...] * flag
    grad_strength = jnp.sum(grad_delta * value, axis=1, keepdims=True)
    grads = []
    for index, part in enumerate(parts):
        at = slice(index * width, (index + 1) * width)
        grad_normal = grad_normal_ref[:, at] * flag
        grad_strength += jnp.sum(part * grad_normal, axis=1, keepdims=True)
        grads.append(grad_phi_ref[:, at] * flag + beta * grad_normal)
    grad_key = low(feature_back(grads, softer, key))
    grad_value = low(beta * grad_delta)
    grad_logit = grad_strength * beta * (1.0 - beta)
    grad_rows_ref[...] = (
        grad_logit * w_beta + nt(grad_key, w_key_ref[...]) + nt(grad_value, w_value_ref[...])
    )
    grad_beta_ref[...] = jnp.sum(grad_logit * mem_out, axis=0, keepdims=True)
    grad_w_ref[:, :width] = low(tn(mem_low, grad_key))
    grad_w_ref[:, width:] = low(tn(mem_low, grad_value))


def write_back(flag, mem_out, w_mem, w_beta, written, grad_delta, grad_phi, grad_normal):
    mems, width = mem_out.shape
    args = [flag, mem_out, w_mem, w_mem, w_beta, written["key"], written["value"]]
    args += [grad_delta, grad_phi, grad_normal]
    out_shape = [
        shaped((mems, width), f32),
        shaped((width, 2 * width), low_type),
        shaped((1, width), f32),
    ]
    return pl.pallas_call(
        write_back_kernel,
        grid=(1,),
        in_specs=[
            pl.BlockSpec(memory_space=pltpu.SMEM),
            whole((mems, width)),
            pl.BlockSpec((width, width), lambda j: (0, 1)),
            pl.BlockSpec((width, width), lambda j: (0, 2)),
        ]
        + [whole(a.shape) for a in args[4:]],
        out_specs=[result(s.shape) for s in out_shape],
        out_shape=out_shape,
        compiler_params=params(),
        name="write_back",
    )(*args)


def leave_back_kernel(writes, adds, *refs):
    (out_grad_ref, *refs) = refs
    if writes:
        (grad_rows_ref, *refs) = refs
    (
        states_two_ref,
        normed_ref,
        upward_ref,
        attended_ref,
        gains_ref,
        w_out_ref,
        w_up_ref,
        w_down_ref,
        *refs,
    ) = refs
    if adds:
        (up_in_ref, down_in_ref, out_in_ref, *refs) = refs
    (
        grad_states_ref,
        grad_attended_ref,
        grad_up_ref,
        grad_down_ref,
        grad_out_ref,
        grad_gain_ref,
        grad_low_ref,
        sum_ref,
        grad_two_ref,
    ) = refs
    rows, width = normed_ref.shape
    seg_rows = out_grad_ref.shape[0]
    step = pl.program_id(0)

    @pl.when(step == 0)
    def _():
        grad_low_ref[:seg_rows, :] = out_grad_ref[...]
        grad_states_ref[:seg_rows, :] = out_grad_ref[...].astype(f32)
        if writes:
            grad_low_ref[seg_rows:, :] = low(grad_rows_ref[...])
            grad_states_ref[seg_rows:, :] = grad_rows_ref[...]
        else:
            grad_low_ref[seg_rows:, :] = jnp.zeros((rows - seg_rows, width), low_type)
            grad_states_ref[seg_rows:, :] = jnp.zeros((rows - seg_rows, width), f32)
        sum_ref[...] = jnp.zeros_like(sum_ref)

    upward = upward_ref[...]
    square = upward * upward
    bent = jnp.tanh(upward * (gelu_c + gelu_c * gelu_a * square))
    half = 0.5 + 0.5 * bent
    active = upward * half
    slope = half + (active - active * half) * (2.0 * gelu_c + 6.0 * gelu_c * gelu_a * square)
    grad_low = grad_low_ref[...]
    grad_upward = low(nt(grad_low, w_down_ref[...]) * slope)
    grad_down = tn(low(active), grad_low)
    grad_up = tn(normed_ref[...], grad_upward)
    sum_ref[...] += nt(grad_upward, w_up_ref[...])
    if adds:
        grad_down += down_in_ref[...]
        grad_up += up_in_ref[...]
    grad_down_ref[...] = grad_down.astype(grad_down_ref.dtype)
    grad_up_ref[...] = grad_up.astype(grad_up_ref.dtype)

    @pl.when(step == pl.num_programs(0) - 1)
    def _():
        gain = gains_ref[1:2, :]
        grad_gain_ref[...] = jnp.zeros_like(grad_gain_ref)

        def chunk(at):
            unit, inverse = normal_form(states_two_ref[at, :])
            grad = sum_ref[at, :]
            grad_gain_ref[...] += jnp.sum(grad * unit, axis=0, keepdims=True)
            total = grad_states_ref[at, :] + norm_back(grad, unit, inverse, gain)
            grad_states_ref[at, :] = total
            total_low = low(total)
            grad_two_ref[at, :] = total_low
            grad_attended_ref[at, :] = low(nt(total_low, w_out_ref[...]))

        over_rows(rows, chunk)
        grad_out = tn(attended_ref[...], grad_two_ref[...])
        if adds:
            grad_out += out_in_ref[...]
        grad_out_ref[...] = grad_out.astype(grad_out_ref.dtype)


def leave_back(slot, out_grad, grad_rows, kept, gains, w_out, w_up, w_down, sums, grad_type):
    _, seg_rows, width = out_grad.shape
    rows = kept["normed_two"].shape[0]
    hidden = w_up.shape[1]
    size = 512 if hidden % 512 == 0 else hidden
    up_spec = pl.BlockSpec((width, size), lambda j: (0, j))
    down_spec = pl.BlockSpec((size, width), lambda j: (j, 0))
    args = [out_grad]
    in_specs = [
        pl.BlockSpec((None, seg_rows, width), lambda j: (slot, 0, 0), pipeline_mode=pl.Buffered(1))
    ]
    if grad_rows is not None:
        args.append(grad_rows)
        in_specs.append(whole(grad_rows.shape))
    args += [kept["states_two"], kept["normed_two"], kept["upward"], kept["attended"]]
    args += [gains, w_out, w_up, w_down]
    in_specs += [
        whole((rows, width)),
        whole((rows, width)),
        pl.BlockSpec((rows, size), lambda j: (0, j)),
        whole((rows, width)),
        whole(gains.shape),
        whole((width, width)),
        up_spec,
        down_spec,
    ]
    if sums is not None:
        args += [sums["up"], sums["down"], sums["out"]]
        in_specs += [up_spec, down_spec, whole((width, width))]
    return pl.pallas_call(
        functools.partial(leave_back_kernel, grad_rows is not None, sums is not None),
        grid=(hidden // size,),
        in_specs=in_specs,
        out_specs=[
            result((rows, width)),
            result((rows, width)),
            up_spec,
            down_spec,
            result((width, width)),
            result((1, width)),
        ],
        out_shape=[
            shaped((rows, width), f32),
            shaped((rows, width), low_type),
            shaped((width, hidden), grad_type),
            shaped((hidden, width), grad_type),
            shaped((width, width), grad_type),
            shaped((1, width), f32),
        ],
        scratch_shapes=[
            pltpu.VMEM((rows, width), low_type),
            pltpu.VMEM((rows, width), f32),
            pltpu.VMEM((rows, width), low_type),
        ],
        compiler_params=params(),
        cost_estimate=pl.CostEstimate(
            flops=4 * rows * width * (width + 2 * hidden), bytes_accessed=60 * 2**20, transcendentals=0
        ),
        name="leave_back",
    )(*args)


def enter_back_kernel(reads, adds, earlier, *refs):
    (tokens_ref, mem_ref, normed_ref, grad_qkv_ref, grad_states_ref, gains_ref, w_ref, *refs) = refs
    if reads:
        (
            states_ref,
            query_ref,
            match_ref,
            w_query_ref,
            phi_keys_ref,
            phi_rest_ref,
            delta_ref,
            beta_ref,
            *refs,
        ) = refs
    if adds:
        (w_in_ref, *refs) = refs
    if earlier:
        refs = refs[1:]
    (grad_tokens_ref, grad_mem_ref, grad_w_ref, grad_gain_ref, *refs) = refs
    if reads:
        (grad_w_query_ref, grad_delta_ref, grad_phi_ref, grad_normal_ref, *refs) = refs
    (first_ref, sum_ref, *refs) = refs
    rows, width = normed_ref.shape
    seg_rows = tokens_ref.shape[0]
    step = pl.program_id(0)

    @pl.when(step == 0)
    def _():
        load_first(tokens_ref, mem_ref, first_ref)
        sum_ref[...] = jnp.zeros_like(sum_ref)

    grad_part = grad_qkv_ref[0]
    sum_ref[...] += nt(grad_part, w_ref[...])
    grad_w = tn(normed_ref[...], grad_part)
    if adds:
        grad_w += w_in_ref[...]
    grad_w_ref[...] = grad_w.astype(grad_w_ref.dtype)

    @pl.when(step == pl.num_programs(0) - 1)
    def _():
        gain = gains_ref[0:1, :]
        grad_gain_ref[...] = jnp.zeros_like(grad_gain_ref)
        if reads:
            (grad_query_ref, packed_sum_ref, delta_sum_ref) = refs
            packed_sum_ref[...] = jnp.zeros_like(packed_sum_ref)
            delta_sum_ref[...] = jnp.zeros_like(delta_sum_ref)
            mems = delta_ref.shape[0]
            beta = beta_ref[...]
            basis = jnp.concatenate([phi_keys_ref[...], phi_keys_ref[...], phi_rest_ref[...]], axis=0)

        def chunk(at):
            first = first_ref[at, :].astype(f32)
            states = states_ref[at, :] if reads else first
            unit, inverse = normal_form(states)
            grad = sum_ref[at, :]
            grad_gain_ref[...] += jnp.sum(grad * unit, axis=0, keepdims=True)
            total = grad_states_ref[at, :] + norm_back(grad, unit, inverse, gain)
            if reads:
                match = match_ref[at, :]
                below = 1.0 + jnp.sum(match * beta, axis=1, keepdims=True)
                grad_num = low(total / below)
                grad_below = -jnp.sum(total * (states - first), axis=1, keepdims=True) / below
                pulled = nt(grad_num, delta_ref[...])
                spread_below = grad_below * beta
                both_high, both_low = split(pulled + spread_below)
                weights = jnp.concatenate([both_high, both_low, low(spread_below)], axis=1)
                query = query_ref[at, :]
                softer = softplus(query)
                parts = feature_parts(softer)
                grads = []
                packed = jnp.concatenate(
                    list(split(pulled))
                    + [low(jnp.broadcast_to(part, pulled.shape)) for part in (grad_below,)]
                    + [
                        low(
                            jnp.broadcast_to(
                                grad_below - low(grad_below).astype(f32), pulled.shape
                            )
                        )
                    ],
                    axis=1,
                )
                for index, part in enumerate(parts):
                    cols = slice(index * width, (index + 1) * width)
                    grads.append(nn(weights, basis[:, cols]))
                    packed_sum_ref[:, cols] += tn(packed, low(part))
                delta_sum_ref[...] += tn(jnp.concatenate(split(match), axis=1), grad_num)
                grad_query = low(feature_back(grads, softer, query))
                grad_query_ref[at, :] = grad_query
                total += nt(grad_query, w_query_ref[...])
            sum_ref[at, :] = total

        over_rows(rows, chunk)
        grad_tokens_ref[...] = sum_ref[:seg_rows, :]
        grad_mem_ref[...] = sum_ref[seg_rows:, :]
        if reads:
            grad_w_query_ref[...] = low(tn(first_ref[...], grad_query_ref[...]))
            grad_delta_ref[...] = delta_sum_ref[:mems, :] + delta_sum_ref[mems:, :]
            grad_phi_ref[...] = packed_sum_ref[:mems, :] + packed_sum_ref[mems : 2 * mems, :]
            grad_normal_ref[...] = (
                packed_sum_ref[2 * mems : 2 * mems + 1, :]
                + packed_sum_ref[3 * mems : 3 * mems + 1, :]
            )


def enter_back(
    slot, tokens, mem_tokens, kept, grad_qkv, grad_states, gains, w_qkv, w_mem, written, w_sum, earlier, grad_type
):
    slots, seg_rows, width = tokens.shape
    mems = mem_tokens.shape[0]
    rows = seg_rows + mems
    parts = grad_qkv.shape[0]
    reads = written is not None
    args = [tokens, mem_tokens, kept["normed_one"], grad_qkv, grad_states, gains, w_qkv]
    in_specs = [
        pl.BlockSpec((None, seg_rows, width), lambda j: (slot, 0, 0), pipeline_mode=pl.Buffered(1)),
        whole((mems, width)),
        whole((rows, width)),
        pl.BlockSpec((1, rows, width), lambda j: (j, 0, 0)),
        whole((rows, width)),
        whole(gains.shape),
        pl.BlockSpec((width, width), lambda j: (0, j)),
    ]
    scratch = [pltpu.VMEM((rows, width), low_type), pltpu.VMEM((rows, width), f32)]
    if reads:
        more = [written["phi_keys_low"], written["phi_keys_rest"]]
        more += [written["delta_low"], written["beta_row"]]
        args += [kept["states_one"], kept["query"], kept["match"], w_mem] + more
        in_specs += [whole((rows, width)), whole((rows, width)), whole((rows, mems)), whole((width, width))]
        in_specs += [whole(a.shape) for a in more]
        scratch += [
            pltpu.VMEM((rows, width), low_type),
            pltpu.VMEM((4 * mems, 3 * width), f32),
            pltpu.VMEM((2 * mems, width), f32),
        ]
    if w_sum is not None:
        args.append(w_sum)
        in_specs.append(pl.BlockSpec((width, width), lambda j: (0, j)))
    aliases = {}
    if earlier is not None:
        aliases = {len(args): 0}
        args.append(earlier)
        in_specs.append(pl.BlockSpec(memory_space=pl.ANY))
    out_specs = [
        pl.BlockSpec((None, seg_rows, width), lambda j: (slot, 0, 0)),
        result((mems, width)),
        pl.BlockSpec((width, width), lambda j: (0, j)),
        result((1, width)),
    ]
    out_shape = [
        shaped((slots, seg_rows, width), f32),
        shaped((mems, width), f32),
        shaped((width, parts * width), grad_type),
        shaped((1, width), f32),
    ]
    if reads:
        extra = [
            shaped((width, width), low_type),
            shaped((mems, width), f32),
            shaped((mems, 3 * width), f32),
            shaped((1, 3 * width), f32),
        ]
        out_shape += extra
        out_specs += [result(s.shape) for s in extra]
    return pl.pallas_call(
        functools.partial(enter_back_kernel, reads, w_sum is not None, earlier is not None),
        grid=(parts,),
        in_specs=in_specs,
        out_specs=out_specs,
        out_shape=out_shape,
        scratch_shapes=scratch,
        input_output_aliases=aliases,
        compiler_params=params(),
        cost_estimate=pl.CostEstimate(
            flops=4 * rows * width * width * (parts + 1), bytes_accessed=30 * 2**20, transcendentals=0
        ),
        name="enter_back",
    )(*args)


MESH = pl.DeviceIdType.MESH
DEPTH, SIDE = 4, 2
GRID = (DEPTH, SIDE, SIDE, SIDE)


def my_place():
    wide = lax.axis_index("wide")
    narrow = lax.axis_index("narrow")
    return wide // SIDE, wide % SIDE, narrow // SIDE, narrow % SIDE


def device_at(z, x, y, core):
    return (z * SIDE + x, y * SIDE + core)


def partners(z, x, y, core):
    along = [device_at((z + step) % DEPTH, x, y, core) for step in range(1, DEPTH)]
    return along, device_at(z, 1 - x, y, core), device_at(z, x, 1 - y, core), device_at(z, x, y, 1 - core)


def meet(peers):
    barrier = pltpu.get_barrier_semaphore()
    for peer in peers:
        pl.semaphore_signal(barrier, inc=1, device_id=peer, device_id_type=MESH)
    pl.semaphore_wait(barrier, len(peers))


ORDERS = ("zxy", "zyx", "xyz", "yxz")


def remote(source, target, send, recv, peer):
    return pltpu.make_async_remote_copy(
        src_ref=source, dst_ref=target, send_sem=send, recv_sem=recv, device_id=peer, device_id_type=MESH
    )


def slab(ref, place, known, at):
    z, x, y, core = place
    return ref.at[
        slice(None) if "z" in known else z,
        slice(None) if "x" in known else x,
        slice(None) if "y" in known else y,
        slice(None) if "c" in known else core,
        :,
        at,
    ]


def gather_kernel(groups, lead, count, *refs):
    shards = refs[:count]
    fulls = refs[count : 2 * count]
    own_sem, send_sem, recv_sem = refs[2 * count :]
    place = my_place()
    along, x_peer, y_peer, core_peer = partners(*place)
    meet(along + [x_peer, y_peer, core_peer])
    peers = {"z": along, "x": [x_peer], "y": [y_peer], "c": [core_peer]}
    piece_of = {}
    for group, (a, pieces) in enumerate(groups):
        for piece in pieces:
            piece_of[group, piece] = len(piece_of)

    def begin(index, group):
        a, pieces = groups[group]
        copies = []
        for piece in pieces:
            order, start, size = piece
            number = piece_of[group, piece]
            path = order + "c"
            at = pl.ds(start, size)
            target = slab(fulls[a], place, path[:index], at)
            source = shards[a].at[:, at] if index == 0 else target
            if index == 0:
                copies.append(pltpu.make_async_copy(source, target, own_sem.at[number]))
            for step, peer in enumerate(peers[path[index]]):
                slot = index + step if path[index] == "z" else index + (2 if "z" in path[:index] else 0)
                copies.append(remote(source, target, send_sem.at[number, slot], recv_sem.at[number, slot], peer))
        for copy in copies:
            copy.start()
        return copies

    flying = {}
    total = len(groups)
    for group in range(min(lead, total)):
        flying[0, group] = begin(0, group)
    for tick in range(total + 3):
        for index in (3, 2, 1, 0):
            group = tick - index
            if not 0 <= group < total:
                continue
            for copy in flying.pop((index, group)):
                copy.wait()
            if index < 3:
                flying[index + 1, group] = begin(index + 1, group)
            if index == 0 and group + lead < total:
                flying[0, group + lead] = begin(0, group + lead)


def gather_fast(shards, groups, lead):
    count = len(shards)
    shapes = [s.shape for s in shards]
    number = sum(len(pieces) for _, pieces in groups)
    outs = pl.pallas_call(
        functools.partial(gather_kernel, groups, lead, count),
        in_specs=[pl.BlockSpec(memory_space=pl.ANY)] * count,
        out_specs=[pl.BlockSpec(memory_space=pl.ANY)] * count,
        out_shape=[shaped(GRID + s, low_type) for s in shapes],
        scratch_shapes=[
            pltpu.SemaphoreType.DMA((number,)),
            pltpu.SemaphoreType.DMA((number, 6)),
            pltpu.SemaphoreType.DMA((number, 6)),
        ],
        compiler_params=pltpu.CompilerParams(collective_id=0, has_side_effects=True),
        name="gather",
    )(*shards)
    return [o.reshape(DEPTH * SIDE**3 * s[0], s[1]) for o, s in zip(outs, shapes)]


def cut(cols, shares):
    unit = cols // 128 // sum(shares)
    pieces = []
    at = 0
    for order, share in zip(ORDERS, shares):
        if share:
            pieces.append((order, at, share * unit * 128))
            at += share * unit * 128
    return pieces


def reduce_kernel(groups, lead, count, outs, *refs):
    partials = refs[:count]
    small_ref = refs[count]
    totals = refs[count + 1 : count + 1 + outs]
    small_out_ref = refs[count + 1 + outs]
    scratch = list(refs[count + 2 + outs :])
    small_recv_ref, small_sum_ref, small_z_ref, small_send, small_recv = scratch[:5]
    own_sem, core_send, core_recv, send_sem, recv_sem = scratch[5:10]
    scratch = scratch[10:]
    place = my_place()
    z, x, y, core = place
    along, x_peer, y_peer, core_peer = partners(*place)
    peers = {"x": x_peer, "y": y_peer, "c": core_peer}
    index_of = {"x": x, "y": y}
    buffers = []
    number = 0
    for a, _, _, pieces in groups:
        own, core_in, *scratch = scratch
        entries = []
        for order, start, size in pieces:
            kept, out1, in1, out2, in2, out3, in3, *scratch = scratch
            entries.append((number, order, start, size, kept, (out1, out2, out3), (in1, in2, in3)))
            number += 1
        buffers.append((own, core_in, entries))
    meet(along + [x_peer, y_peer, core_peer])

    def begin_core(group):
        a = groups[group][0]
        own, core_in, _ = buffers[group]
        copies = [
            remote(partials[a].at[:, :, :, 1 - core], core_in, core_send.at[group], core_recv.at[group], core_peer),
            pltpu.make_async_copy(partials[a].at[:, :, :, core], own, own_sem.at[group]),
        ]
        for copy in copies:
            copy.start()
        return copies

    def pair_stage(entry, index, axis):
        item, _, _, _, _, outgoing, incoming = entry
        return remote(outgoing[index], incoming[index], send_sem.at[item, index], recv_sem.at[item, index], peers[axis])

    def after_core(group):
        own, core_in, entries = buffers[group]
        copies = []
        for entry in entries:
            _, order, start, size, kept, outgoing, _ = entry
            axis, other = order[2], order[1]
            at = pl.ds(start, size)
            mine = index_of[axis]
            for far in range(DEPTH):
                for side in range(SIDE):
                    def pick(ref, where):
                        spot = (far, side, where) if axis == "y" else (far, where, side)
                        return ref[spot + (slice(None), at)].astype(f32)

                    kept[far, side] = pick(own, mine) + pick(core_in, mine)
                    outgoing[0][far, side] = (pick(own, 1 - mine) + pick(core_in, 1 - mine)).astype(low_type)
            copies.append(pair_stage(entry, 0, axis))
        for copy in copies:
            copy.start()
        return copies

    def after_first(group):
        copies = []
        for entry in buffers[group][2]:
            _, order, _, _, kept, outgoing, incoming = entry
            axis = order[1]
            mine = index_of[axis]
            for far in range(DEPTH):
                kept[far, mine] = kept[far, mine] + incoming[0][far, mine].astype(f32)
                outgoing[1][far] = (
                    kept[far, 1 - mine] + incoming[0][far, 1 - mine].astype(f32)
                ).astype(low_type)
            copies.append(pair_stage(entry, 1, axis))
        for copy in copies:
            copy.start()
        return copies

    def after_second(group):
        copies = []
        for entry in buffers[group][2]:
            item, order, _, _, kept, outgoing, incoming = entry
            mine = index_of[order[1]]
            kept[z, mine] = kept[z, mine] + incoming[1][z].astype(f32)
            for step in range(1, DEPTH):
                target = (z + step) % DEPTH
                outgoing[2][step - 1] = (
                    kept[target, mine] + incoming[1][target].astype(f32)
                ).astype(low_type)
                copies.append(
                    remote(
                        outgoing[2].at[step - 1],
                        incoming[2].at[step - 1],
                        send_sem.at[item, 1 + step],
                        recv_sem.at[item, 1 + step],
                        along[step - 1],
                    )
                )
        for copy in copies:
            copy.start()
        return copies

    def after_third(group):
        _, out, offset, _ = groups[group]
        for entry in buffers[group][2]:
            _, order, start, size, kept, _, incoming = entry
            mine = index_of[order[1]]
            total = kept[z, mine]
            for step in range(DEPTH - 1):
                total = total + incoming[2][step].astype(f32)
            totals[out][:, pl.ds(offset + start, size)] = total

    steps = [after_core, after_first, after_second, after_third]
    flying = {}
    total = len(groups)
    for group in range(min(lead, total)):
        flying[0, group] = begin_core(group)

    def small_pair(index, axis, source):
        copy = remote(source, small_recv_ref.at[index], small_send.at[index], small_recv.at[index], peers[axis])
        copy.start()
        return copy

    def small_stage(tick):
        if tick == 0:
            flying["small"] = [small_pair(0, "c", small_ref)]
            return
        for copy in flying.pop("small", []):
            copy.wait()
        if tick == 1:
            small_sum_ref[0] = small_ref[...] + small_recv_ref[0]
            flying["small"] = [small_pair(1, "y", small_sum_ref.at[0])]
        elif tick == 2:
            small_sum_ref[1] = small_sum_ref[0] + small_recv_ref[1]
            flying["small"] = [small_pair(2, "x", small_sum_ref.at[1])]
        elif tick == 3:
            small_sum_ref[2] = small_sum_ref[1] + small_recv_ref[2]
            small_z_ref[z] = small_sum_ref[2]
            flying["small"] = []
            for step in range(1, DEPTH):
                copy = remote(
                    small_sum_ref.at[2],
                    small_z_ref.at[z],
                    small_send.at[2 + step],
                    small_recv.at[2 + step],
                    along[step - 1],
                )
                copy.start()
                flying["small"].append(copy)
        elif tick == 4:
            value = small_z_ref[0]
            for far in range(1, DEPTH):
                value = value + small_z_ref[far]
            small_out_ref[...] = value

    for tick in range(total + 3):
        small_stage(tick)
        for index in (3, 2, 1, 0):
            group = tick - index
            if not 0 <= group < total:
                continue
            for copy in flying.pop((index, group)):
                copy.wait()
            flying[index + 1, group] = steps[index](group)
            if index == 0 and group + lead < total:
                flying[0, group + lead] = begin_core(group + lead)


def reduce_fast(partials, small, groups, lead, widths):
    devices = DEPTH * SIDE**3
    views = [p.reshape(GRID + (p.shape[0] // devices, p.shape[1])) for p in partials]
    rows = [v.shape[-2] for v in views]
    scratch = []
    number = 0
    for a, _, _, pieces in groups:
        height = rows[a]
        cols = views[a].shape[-1]
        full = (DEPTH, SIDE, SIDE, height, cols)
        scratch += [pltpu.VMEM(full, low_type), pltpu.VMEM(full, low_type)]
        for _, _, size in pieces:
            number += 1
            scratch.append(pltpu.VMEM((DEPTH, SIDE, height, size), f32))
            for lead_dims in ((DEPTH, SIDE), (DEPTH,), (DEPTH - 1,)):
                scratch += [pltpu.VMEM(lead_dims + (height, size), low_type)] * 2
    total = len(groups)
    sems = pltpu.SemaphoreType.DMA
    out_rows = {out: rows[a] for a, out, _, _ in groups}
    results = pl.pallas_call(
        functools.partial(reduce_kernel, groups, lead, len(views), len(widths)),
        in_specs=[pl.BlockSpec(memory_space=pl.ANY)] * len(views) + [pl.BlockSpec(memory_space=pltpu.VMEM)],
        out_specs=[pl.BlockSpec(memory_space=pltpu.VMEM)] * (len(widths) + 1),
        out_shape=[shaped((out_rows[i], w), f32) for i, w in enumerate(widths)]
        + [shaped(small.shape, f32)],
        scratch_shapes=[
            pltpu.VMEM((3,) + small.shape, f32),
            pltpu.VMEM((3,) + small.shape, f32),
            pltpu.VMEM((DEPTH,) + small.shape, f32),
            sems((6,)),
            sems((6,)),
            sems((total,)),
            sems((total,)),
            sems((total,)),
            sems((number, 5)),
            sems((number, 5)),
        ]
        + scratch,
        compiler_params=pltpu.CompilerParams(
            collective_id=1, has_side_effects=True, vmem_limit_bytes=60 * 2**20
        ),
        name="reduce",
    )(*views, small)
    return results[:-1], results[-1]


def gather_weights(shards):
    return [lax.all_gather(shard, AXES, axis=0, tiled=True) for shard in shards]


def scatter_sums(totals):
    return [
        lax.psum_scatter(total.astype(f32), AXES, scatter_dimension=0, tiled=True)
        for total in totals
    ]


def fast_gather_weights(shards):
    shares = {2304: (8, 8, 1, 1), 768: (3, 3, 0, 0), 3072: (10, 10, 2, 2)}
    groups = []
    for a, shard in enumerate(shards):
        cols = shard.shape[1]
        tall = shard.shape[0] * 32 > cols
        groups.append((a, cut(cols, (2, 2, 1, 1) if tall else shares.get(cols, (1, 1)))))
    return gather_fast(shards, groups, 1)


def fast_scatter_sums(query_sum, pair_sum, qkv_sum, out_sum, up_sum, down_sum, small):
    partials = [query_sum, pair_sum, qkv_sum, out_sum, up_sum, down_sum]
    cols = [p.shape[1] for p in partials]
    places = [(0, 0), (0, cols[0]), (1, 0), (2, 0), (3, 0), (4, 0)]
    order = (5, 4, 0, 1, 3, 2)
    groups = [(a,) + places[a] + (cut(cols[a], (1, 1)),) for a in order]
    return reduce_fast(partials, small, groups, 2, [cols[0] + cols[1]] + cols[2:])


def on_device(
    fast, tokens, item_ids, w_mem, w_qkv, w_out, w_up, w_down, mem_tokens, gains, w_beta, out_grad
):
    slots, seg_rows, width = tokens.shape
    gains = gains.astype(f32)
    w_beta = w_beta.astype(f32).reshape(1, width)
    gather = fast_gather_weights if fast else gather_weights
    w_qkv, w_out, w_up, w_down, w_mem = gather([w_qkv, w_out, w_up, w_down, w_mem])
    same_item = jnp.where(item_ids[1:] == item_ids[:-1], 1.0, 0.0).astype(f32)
    kept_all = []
    written = [None] * (slots + 1)
    out = None
    for slot in range(slots):
        kept = {}
        entered = enter_segment(slot, tokens, mem_tokens, gains, w_qkv, w_mem, written[slot])
        kept["normed_one"], kept["qkv"] = entered[:2]
        start = (tokens, mem_tokens)
        if written[slot] is not None:
            kept["states_one"], kept["query"], kept["match"] = entered[2:]
            start = kept["states_one"]
        kept["attended"], kept["logs"] = attend(kept["qkv"], seg_rows)
        out, mem_out, kept["states_two"], kept["normed_two"], kept["upward"] = leave_segment(
            slot, slots, seg_rows, start, kept["attended"], gains, w_out, w_up, w_down, out
        )
        kept["mem_out"] = mem_out
        if slot + 1 < slots:
            written[slot + 1] = write_memory(same_item[slot : slot + 1], mem_out, w_mem, w_beta)
        kept_all.append(kept)

    sums = None
    qkv_sum = None
    grad_tokens = None
    grad_mem_tokens = 0.0
    grad_gains = 0.0
    grad_beta = 0.0
    pulled = None
    for slot in reversed(range(slots)):
        kept = kept_all[slot]
        grad_type = f32 if slot else low_type
        grad_rows = None
        if slot + 1 < slots:
            grad_rows, w_pair_sum, grad_beta_part = write_back(
                same_item[slot : slot + 1], kept["mem_out"], w_mem, w_beta, written[slot + 1], *pulled
            )
            grad_beta += grad_beta_part
        grad_states, grad_attended, up_sum, down_sum, out_sum, gain_two = leave_back(
            slot, out_grad, grad_rows, kept, gains, w_out, w_up, w_down, sums, grad_type
        )
        sums = {"up": up_sum, "down": down_sum, "out": out_sum}
        grad_qkv = attend_back(kept["qkv"], grad_attended, kept["attended"], kept["logs"], seg_rows)
        grad_tokens, grad_mem, qkv_sum, gain_one, *extra = enter_back(
            slot,
            tokens,
            mem_tokens,
            kept,
            grad_qkv,
            grad_states,
            gains,
            w_qkv,
            w_mem,
            written[slot],
            qkv_sum,
            grad_tokens,
            grad_type,
        )
        if written[slot] is not None:
            w_query_sum, *pulled = extra
        grad_mem_tokens += grad_mem
        grad_gains += jnp.concatenate([gain_one, gain_two], axis=0)
    if fast:
        mems = mem_tokens.shape[0]
        small = jnp.concatenate([grad_mem_tokens, grad_gains, grad_beta], axis=0)
        small = jnp.pad(small, ((0, -small.shape[0] % 8), (0, 0)))
        summed, small = fast_scatter_sums(
            w_query_sum, w_pair_sum, qkv_sum, sums["out"], sums["up"], sums["down"], small
        )
        small = (small[:mems], small[mems : mems + 2], small[mems + 2])
        return (out, grad_tokens, *summed, *small)
    mem_sum = jnp.concatenate([w_query_sum, w_pair_sum], axis=1)
    summed = scatter_sums([mem_sum, qkv_sum, sums["out"], sums["up"], sums["down"]])
    small = lax.psum((grad_mem_tokens, grad_gains, grad_beta.reshape(width)), AXES)
    return (out, grad_tokens, *summed, *small)


def solution(mesh):
    split_rows = P(AXES, None)
    split_items = P(AXES, None, None)
    in_specs = (
        split_items,
        P(AXES),
        split_rows,
        split_rows,
        split_rows,
        split_rows,
        split_rows,
        P(),
        P(),
        P(),
        split_items,
    )
    out_specs = (
        split_items,
        split_items,
        split_rows,
        split_rows,
        split_rows,
        split_rows,
        split_rows,
        P(),
        P(),
        P(),
    )
    fast = mesh.shape["wide"] == DEPTH * SIDE and mesh.shape["narrow"] == SIDE * SIDE
    return jax.shard_map(
        functools.partial(on_device, fast), mesh=mesh, in_specs=in_specs, out_specs=out_specs, check_vma=False
    )
```

```python
import functools

import jax
import jax.numpy as jnp
from jax import lax
from jax.experimental import pallas as pl
from jax.experimental.pallas import tpu as pltpu
from jax.sharding import PartitionSpec as P

HD = 64
PAIR = 2 * HD
AXES = ("wide", "narrow")
eps_norm = 1e-05
score_scale = 0.125
gelu_c = 0.7978845608028654
gelu_a = 0.044715
f32 = jnp.float32
low_type = jnp.bfloat16
VMEM_BYTES = 60 * 2**20


def nn(left, right):
    return lax.dot_general(left, right, (((1,), (0,)), ((), ())), preferred_element_type=f32)


def nt(left, right):
    return lax.dot_general(left, right, (((1,), (1,)), ((), ())), preferred_element_type=f32)


def tn(left, right):
    return lax.dot_general(left, right, (((0,), (0,)), ((), ())), preferred_element_type=f32)


def low(values):
    return values.astype(low_type)


def split(values):
    high = low(values)
    return high, low(values - high.astype(f32))


def row_chunk(rows):
    for count in (208, 256, 128, 80, 64, 16):
        if rows % count == 0:
            return count
    return rows


def over_rows(rows, body):
    count = row_chunk(rows)

    @pl.loop(0, rows // count)
    def _(step):
        body(pl.ds(pl.multiple_of(step * count, count), count))


def normal_form(values):
    average = jnp.mean(values, axis=-1, keepdims=True)
    centered = values - average
    spread = jnp.mean(centered * centered, axis=-1, keepdims=True)
    inverse = lax.rsqrt(spread + eps_norm)
    return centered * inverse, inverse


def norm_back(grad, unit, inverse, gain):
    scaled = grad * gain
    mean_grad = jnp.mean(scaled, axis=-1, keepdims=True)
    mean_unit = jnp.mean(scaled * unit, axis=-1, keepdims=True)
    return inverse * (scaled - mean_grad - unit * mean_unit)


def softplus(values):
    return jnp.maximum(values, 0.0) + jnp.log1p(jnp.exp(-jnp.abs(values)))


def feature_parts(softer):
    return [softer * pltpu.roll(softer, offset, 1) for offset in (1, 2, 3)]


def feature_back(grads, softer, values):
    width = softer.shape[1]
    total = None
    for offset, grad in zip((1, 2, 3), grads):
        term = grad * pltpu.roll(softer, offset, 1) + pltpu.roll(grad * softer, width - offset, 1)
        total = term if total is None else total + term
    return total * jax.nn.sigmoid(values)


def whole(shape, memory=None):
    zeros = (0,) * len(shape)
    return pl.BlockSpec(shape, lambda *_: zeros, pipeline_mode=pl.Buffered(1))


def result(shape):
    zeros = (0,) * len(shape)
    return pl.BlockSpec(shape, lambda *_: zeros)


def params(**extra):
    return pltpu.CompilerParams(vmem_limit_bytes=VMEM_BYTES, **extra)


def shaped(shape, dtype):
    return jax.ShapeDtypeStruct(shape, dtype)


def load_first(tokens_ref, mem_ref, first_ref):
    seg_rows = tokens_ref.shape[0]
    first_ref[:seg_rows, :] = tokens_ref[...]
    first_ref[seg_rows:, :] = mem_ref[...]


def enter_kernel(tokens_ref, mem_ref, gains_ref, w_ref, normed_ref, qkv_ref, first_ref):
    @pl.when(pl.program_id(0) == 0)
    def _():
        load_first(tokens_ref, mem_ref, first_ref)

        def chunk(at):
            unit, _ = normal_form(first_ref[at, :].astype(f32))
            normed_ref[at, :] = low(unit * gains_ref[0:1, :])

        over_rows(first_ref.shape[0], chunk)

    qkv_ref[0] = low(nn(normed_ref[...], w_ref[...]))


def enter_read_kernel(
    tokens_ref,
    mem_ref,
    gains_ref,
    w_ref,
    w_query_ref,
    phi_keys_ref,
    delta_ref,
    beta_ref,
    normed_ref,
    qkv_ref,
    states_ref,
    query_ref,
    match_ref,
    first_ref,
):
    @pl.when(pl.program_id(0) == 0)
    def _():
        load_first(tokens_ref, mem_ref, first_ref)
        width = first_ref.shape[1]
        delta_twice = jnp.concatenate([delta_ref[...], delta_ref[...]], axis=0)

        def chunk(at):
            first = first_ref[at, :]
            query = nn(first, w_query_ref[...])
            query_ref[at, :] = query
            parts = feature_parts(softplus(query))
            match = None
            for index, part in enumerate(parts):
                term = nt(low(part), phi_keys_ref[:, index * width : (index + 1) * width])
                match = term if match is None else match + term
            match_ref[at, :] = match
            numerator = nn(jnp.concatenate(split(match), axis=1), delta_twice)
            below = 1.0 + jnp.sum(match * beta_ref[...], axis=1, keepdims=True)
            states = first.astype(f32) + numerator / below
            states_ref[at, :] = states
            unit, _ = normal_form(states)
            normed_ref[at, :] = low(unit * gains_ref[0:1, :])

        over_rows(first_ref.shape[0], chunk)

    qkv_ref[0] = low(nn(normed_ref[...], w_ref[...]))


def enter_segment(slot, tokens, mem_tokens, gains, w_qkv, w_mem, written):
    slots, seg_rows, width = tokens.shape
    mems = mem_tokens.shape[0]
    rows = seg_rows + mems
    parts = w_qkv.shape[1] // width
    in_specs = [
        pl.BlockSpec((None, seg_rows, width), lambda j: (slot, 0, 0), pipeline_mode=pl.Buffered(1)),
        whole((mems, width)),
        whole(gains.shape),
        pl.BlockSpec((width, width), lambda j: (0, j)),
    ]
    out_shape = [shaped((rows, width), low_type), shaped((parts, rows, width), low_type)]
    out_specs = [
        result((rows, width)),
        pl.BlockSpec((1, rows, width), lambda j: (j, 0, 0)),
    ]
    args = [tokens, mem_tokens, gains, w_qkv]
    body = enter_kernel
    macs = rows * width * width * parts
    if written is not None:
        body = enter_read_kernel
        args += [w_mem, written["phi_keys_low"], written["delta_low"], written["beta_row"]]
        in_specs += [whole((width, width))] + [whole(a.shape) for a in args[5:]]
        out_shape += [
            shaped((rows, width), f32),
            shaped((rows, width), f32),
            shaped((rows, mems), f32),
        ]
        out_specs += [result((rows, width)), result((rows, width)), result((rows, mems))]
        macs += rows * width * width
    return pl.pallas_call(
        body,
        grid=(parts,),
        in_specs=in_specs,
        out_specs=out_specs,
        out_shape=out_shape,
        scratch_shapes=[pltpu.VMEM((rows, width), low_type)],
        compiler_params=params(),
        cost_estimate=pl.CostEstimate(
            flops=2 * macs, bytes_accessed=20 * 2**20, transcendentals=0
        ),
        name="enter_read" if written is not None else "enter",
    )(*args)


def query_blocks(rows, seg_rows):
    step = 256 if seg_rows % 256 == 0 else seg_rows
    blocks = [(at, step) for at in range(0, seg_rows, step)]
    return blocks + [(seg_rows, rows - seg_rows)]


def packed_lanes(rows, seg_rows):
    places = []
    at = 0
    for _, count in query_blocks(rows, seg_rows):
        places.append(at)
        at += -(-2 * count // 128) * 128
    return places, at


def stack_heads(block):
    lanes = lax.broadcasted_iota(jnp.int32, block.shape, 1)
    zero = jnp.zeros_like(block)
    return jnp.concatenate(
        [jnp.where(lanes < HD, block, zero), jnp.where(lanes < HD, zero, block)], axis=0
    )


def merge_heads(stacked):
    count = stacked.shape[0] // 2
    lanes = lax.broadcasted_iota(jnp.int32, (count, stacked.shape[1]), 1)
    return jnp.where(lanes < HD, stacked[:count], stacked[count:])


def as_row(column):
    count = column.shape[0]
    return jnp.transpose(jnp.broadcast_to(column, (count, 128)))[0:1, :]


def attend_kernel(seg_rows, qkv_ref, attended_ref, log_ref, lanes=slice(None)):
    rows = qkv_ref.shape[1]
    places, _ = packed_lanes(rows, seg_rows)
    for (start, count), place in zip(query_blocks(rows, seg_rows), places):
        reach = start + count
        queries = stack_heads(qkv_ref[0, start:reach, lanes] * score_scale)
        raw = nt(queries, qkv_ref[1, :reach, lanes])
        place_of = lax.broadcasted_iota(jnp.int32, (2 * count, count), 0)
        place_of = jnp.where(place_of < count, place_of, place_of - count)
        allowed = place_of >= lax.broadcasted_iota(jnp.int32, (2 * count, count), 1)
        edge = jnp.where(allowed, raw[:, start:], -1e30)
        masked = jnp.concatenate([raw[:, :start], edge], axis=1) if start else edge
        peak = jnp.max(masked, axis=1, keepdims=True)
        grown = jnp.exp(masked - peak)
        total = jnp.sum(grown, axis=1, keepdims=True)
        probs = low(grown * (1.0 / total))
        mixed = merge_heads(nn(probs, qkv_ref[2, :reach, lanes]))
        attended_ref[start:reach, :] = low(mixed)
        log_row = as_row(peak + jnp.log(total))
        log_ref[0, 0:1, place : place + 2 * count] = log_row


def attend(qkv, seg_rows):
    parts, rows, width = qkv.shape
    _, lanes = packed_lanes(rows, seg_rows)
    pairs = width // PAIR
    return pl.pallas_call(
        functools.partial(attend_kernel, seg_rows),
        grid=(pairs,),
        in_specs=[pl.BlockSpec((parts, rows, PAIR), lambda h: (0, 0, h))],
        out_specs=[
            pl.BlockSpec((rows, PAIR), lambda h: (0, h)),
            pl.BlockSpec((1, 1, lanes), lambda h: (h, 0, 0)),
        ],
        out_shape=[shaped((rows, width), low_type), shaped((pairs, 1, lanes), f32)],
        compiler_params=params(),
        cost_estimate=pl.CostEstimate(
            flops=4 * rows * rows * width, bytes_accessed=7 * 2**20, transcendentals=0
        ),
        name="attend",
    )(qkv)


def attend_back_kernel(
    seg_rows,
    qkv_ref,
    grad_ref,
    attended_ref,
    log_ref,
    out_ref,
    keys_sum,
    values_sum,
    lanes=slice(None),
):
    rows = qkv_ref.shape[1]
    places, _ = packed_lanes(rows, seg_rows)
    ones = jnp.ones((8, PAIR), f32)
    blocks = list(zip(query_blocks(rows, seg_rows), places))
    for order, ((start, count), place) in enumerate(reversed(blocks)):
        reach = start + count
        queries = stack_heads(qkv_ref[0, start:reach, :] * score_scale)
        grads = stack_heads(grad_ref[start:reach, :])
        mixed = attended_ref[start:reach, :].astype(f32)
        both = jnp.concatenate([mixed, mixed], axis=0) * grads.astype(f32)
        inner = lax.dot_general(
            ones,
            both,
            (((1,), (1,)), ((), ())),
            precision=lax.Precision.HIGHEST,
            preferred_element_type=f32,
        )[0:1, :]
        keys = qkv_ref[1, :reach, :]
        raw = nt(keys, queries)
        log_row = log_ref[0, 0:1, place : place + 2 * count]
        probs = jnp.exp(raw - log_row)
        place_of = lax.broadcasted_iota(jnp.int32, (count, 2 * count), 1)
        place_of = jnp.where(place_of < count, place_of, place_of - count)
        allowed = place_of >= lax.broadcasted_iota(jnp.int32, (count, 2 * count), 0)
        edge = jnp.where(allowed, probs[start:], 0.0)
        probs = jnp.concatenate([probs[:start], edge], axis=0) if start else edge
        grad_probs = nt(qkv_ref[2, :reach, :], grads)
        grad_raw = low(probs * (grad_probs - inner))
        value_part = nn(low(probs), grads)
        key_part = nn(grad_raw, queries)
        if order == 0:
            values_sum[...] = value_part
            keys_sum[...] = key_part
        else:
            values_sum[:reach, :] += value_part
            keys_sum[:reach, :] += key_part
        out_ref[0, start:reach, lanes] = low(merge_heads(tn(grad_raw, keys)) * score_scale)
    out_ref[1, :, lanes] = low(keys_sum[...])
    out_ref[2, :, lanes] = low(values_sum[...])


def attend_back(qkv, grad_attended, attended, logs, seg_rows):
    parts, rows, width = qkv.shape
    pairs = width // PAIR
    column = pl.BlockSpec((rows, PAIR), lambda h: (0, h))
    three = pl.BlockSpec((parts, rows, PAIR), lambda h: (0, 0, h))
    return pl.pallas_call(
        functools.partial(attend_back_kernel, seg_rows),
        grid=(pairs,),
        in_specs=[
            three,
            column,
            column,
            pl.BlockSpec((1,) + logs.shape[1:], lambda h: (h, 0, 0)),
        ],
        out_specs=three,
        out_shape=shaped((parts, rows, width), low_type),
        scratch_shapes=[pltpu.VMEM((rows, PAIR), f32), pltpu.VMEM((rows, PAIR), f32)],
        compiler_params=params(),
        cost_estimate=pl.CostEstimate(
            flops=10 * rows * rows * width, bytes_accessed=13 * 2**20, transcendentals=0
        ),
        name="attend_back",
    )(qkv, grad_attended, attended, logs)


def leave_kernel(
    reads, earlier, *refs
):
    if reads:
        (states_one_ref, *refs) = refs
    else:
        (tokens_ref, mem_ref, *refs) = refs
    (attended_ref, gains_ref, w_out_ref, w_up_ref, w_down_ref, *refs) = refs
    if earlier:
        refs = refs[1:]
    (out_ref, mem_out_ref, states_two_ref, normed_ref, upward_ref, sum_ref, *scratch) = refs
    rows, width = attended_ref.shape
    seg_rows = out_ref.shape[0]
    step = pl.program_id(0)

    @pl.when(step == 0)
    def _():
        if not reads:
            load_first(tokens_ref, mem_ref, scratch[0])

        def chunk(at):
            source = states_one_ref if reads else scratch[0]
            states = source[at, :].astype(f32) + nn(attended_ref[at, :], w_out_ref[...])
            states_two_ref[at, :] = states
            unit, _ = normal_form(states)
            normed_ref[at, :] = low(unit * gains_ref[1:2, :])
            sum_ref[at, :] = states

        over_rows(rows, chunk)

    def chunk(at):
        upward = nn(normed_ref[at, :], w_up_ref[...])
        upward_ref[at, :] = upward
        bent = jnp.tanh(upward * (gelu_c + gelu_c * gelu_a * (upward * upward)))
        active = low(upward * (0.5 + 0.5 * bent))
        sum_ref[at, :] += nn(active, w_down_ref[...])

    chunk(pl.ds(0, rows))

    @pl.when(step == pl.num_programs(0) - 1)
    def _():
        out_ref[...] = low(sum_ref[:seg_rows, :])
        mem_out_ref[...] = sum_ref[seg_rows:, :]


def leave_segment(slot, slots, seg_rows, start, attended, gains, w_out, w_up, w_down, earlier):
    rows, width = attended.shape
    hidden = w_up.shape[1]
    size = 512 if hidden % 512 == 0 else hidden
    reads = not isinstance(start, tuple)
    args = []
    in_specs = []
    scratch = [pltpu.VMEM((rows, width), f32)]
    if reads:
        args.append(start)
        in_specs.append(whole((rows, width)))
    else:
        tokens, mem_tokens = start
        args += [tokens, mem_tokens]
        in_specs += [
            pl.BlockSpec((None, seg_rows, width), lambda j: (slot, 0, 0), pipeline_mode=pl.Buffered(1)),
            whole(mem_tokens.shape),
        ]
        scratch.append(pltpu.VMEM((rows, width), low_type))
    args += [attended, gains, w_out, w_up, w_down]
    in_specs += [
        whole((rows, width)),
        whole(gains.shape),
        whole((width, width)),
        pl.BlockSpec((width, size), lambda j: (0, j)),
        pl.BlockSpec((size, width), lambda j: (j, 0)),
    ]
    aliases = {}
    if earlier is not None:
        aliases = {len(args): 0}
        args.append(earlier)
        in_specs.append(pl.BlockSpec(memory_space=pl.ANY))
    return pl.pallas_call(
        functools.partial(leave_kernel, reads, earlier is not None),
        grid=(hidden // size,),
        in_specs=in_specs,
        out_specs=[
            pl.BlockSpec((None, seg_rows, width), lambda j: (slot, 0, 0)),
            result((rows - seg_rows, width)),
            result((rows, width)),
            result((rows, width)),
            pl.BlockSpec((rows, size), lambda j: (0, j)),
        ],
        out_shape=[
            shaped((slots, seg_rows, width), low_type),
            shaped((rows - seg_rows, width), f32),
            shaped((rows, width), f32),
            shaped((rows, width), low_type),
            shaped((rows, hidden), f32),
        ],
        scratch_shapes=scratch,
        input_output_aliases=aliases,
        compiler_params=params(),
        cost_estimate=pl.CostEstimate(
            flops=2 * rows * width * (width + 2 * hidden), bytes_accessed=36 * 2**20, transcendentals=0
        ),
        name="leave",
    )(*args)


def beta_parts(mem_out, w_beta):
    column = jnp.sum(mem_out * w_beta, axis=1, keepdims=True)
    row = lax.dot_general(
        w_beta,
        mem_out,
        (((1,), (1,)), ((), ())),
        precision=lax.Precision.HIGHEST,
        preferred_element_type=f32,
    )
    return jax.nn.sigmoid(column), jax.nn.sigmoid(row)


def write_kernel(
    flag_ref,
    mem_out_ref,
    w_key_ref,
    w_value_ref,
    w_beta_ref,
    key_ref,
    value_ref,
    phi_ref,
    phi_rest_ref,
    delta_ref,
    beta_row_ref,
):
    flag = flag_ref[0]
    width = key_ref.shape[1]
    mem_out = mem_out_ref[...]
    mem_low = low(mem_out)
    key = nn(mem_low, w_key_ref[...])
    value = nn(mem_low, w_value_ref[...])
    key_ref[...] = key
    value_ref[...] = value
    for index, part in enumerate(feature_parts(softplus(key))):
        high, rest = split(part)
        phi_ref[:, index * width : (index + 1) * width] = high
        phi_rest_ref[:, index * width : (index + 1) * width] = rest
    beta, beta_row = beta_parts(mem_out, w_beta_ref[...])
    delta_ref[...] = low(low(beta * value).astype(f32) * flag)
    beta_row_ref[...] = beta_row * flag


def write_memory(flag, mem_out, w_mem, w_beta):
    mems, width = mem_out.shape
    names = ("key", "value", "phi_keys_low", "phi_keys_rest", "delta_low", "beta_row")
    out_shape = [
        shaped((mems, width), f32),
        shaped((mems, width), f32),
        shaped((mems, 3 * width), low_type),
        shaped((mems, 3 * width), low_type),
        shaped((mems, width), low_type),
        shaped((1, mems), f32),
    ]
    outs = pl.pallas_call(
        write_kernel,
        grid=(1,),
        in_specs=[
            pl.BlockSpec(memory_space=pltpu.SMEM),
            whole((mems, width)),
            pl.BlockSpec((width, width), lambda j: (0, 1)),
            pl.BlockSpec((width, width), lambda j: (0, 2)),
            whole((1, width)),
        ],
        out_specs=[result(s.shape) for s in out_shape],
        out_shape=out_shape,
        compiler_params=params(),
        name="write",
    )(flag, mem_out, w_mem, w_mem, w_beta)
    return dict(zip(names, outs))


def write_back_kernel(
    flag_ref,
    mem_out_ref,
    w_key_ref,
    w_value_ref,
    w_beta_ref,
    key_ref,
    value_ref,
    grad_delta_ref,
    grad_phi_ref,
    grad_normal_ref,
    grad_rows_ref,
    grad_w_ref,
    grad_beta_ref,
):
    flag = flag_ref[0]
    width = key_ref.shape[1]
    mem_out = mem_out_ref[...]
    mem_low = low(mem_out)
    w_beta = w_beta_ref[...]
    key = key_ref[...]
    value = value_ref[...]
    beta, _ = beta_parts(mem_out, w_beta)
    softer = softplus(key)
    parts = feature_parts(softer)
    grad_delta = grad_delta_ref[...] * flag
    grad_strength = jnp.sum(grad_delta * value, axis=1, keepdims=True)
    grads = []
    for index, part in enumerate(parts):
        at = slice(index * width, (index + 1) * width)
        grad_normal = grad_normal_ref[:, at] * flag
        grad_strength += jnp.sum(part * grad_normal, axis=1, keepdims=True)
        grads.append(grad_phi_ref[:, at] * flag + beta * grad_normal)
    grad_key = low(feature_back(grads, softer, key))
    grad_value = low(beta * grad_delta)
    grad_logit = grad_strength * beta * (1.0 - beta)
    grad_rows_ref[...] = (
        grad_logit * w_beta + nt(grad_key, w_key_ref[...]) + nt(grad_value, w_value_ref[...])
    )
    grad_beta_ref[...] = jnp.sum(grad_logit * mem_out, axis=0, keepdims=True)
    grad_w_ref[:, :width] = low(tn(mem_low, grad_key))
    grad_w_ref[:, width:] = low(tn(mem_low, grad_value))


def write_back(flag, mem_out, w_mem, w_beta, written, grad_delta, grad_phi, grad_normal):
    mems, width = mem_out.shape
    args = [flag, mem_out, w_mem, w_mem, w_beta, written["key"], written["value"]]
    args += [grad_delta, grad_phi, grad_normal]
    out_shape = [
        shaped((mems, width), f32),
        shaped((width, 2 * width), low_type),
        shaped((1, width), f32),
    ]
    return pl.pallas_call(
        write_back_kernel,
        grid=(1,),
        in_specs=[
            pl.BlockSpec(memory_space=pltpu.SMEM),
            whole((mems, width)),
            pl.BlockSpec((width, width), lambda j: (0, 1)),
            pl.BlockSpec((width, width), lambda j: (0, 2)),
        ]
        + [whole(a.shape) for a in args[4:]],
        out_specs=[result(s.shape) for s in out_shape],
        out_shape=out_shape,
        compiler_params=params(),
        name="write_back",
    )(*args)


def leave_back_kernel(writes, adds, *refs):
    (out_grad_ref, *refs) = refs
    if writes:
        (grad_rows_ref, *refs) = refs
    (
        states_two_ref,
        normed_ref,
        upward_ref,
        attended_ref,
        gains_ref,
        w_out_ref,
        w_up_ref,
        w_down_ref,
        *refs,
    ) = refs
    if adds:
        (up_in_ref, down_in_ref, out_in_ref, *refs) = refs
    (
        grad_states_ref,
        grad_attended_ref,
        grad_up_ref,
        grad_down_ref,
        grad_out_ref,
        grad_gain_ref,
        grad_low_ref,
        sum_ref,
        grad_two_ref,
    ) = refs
    rows, width = normed_ref.shape
    seg_rows = out_grad_ref.shape[0]
    step = pl.program_id(0)

    @pl.when(step == 0)
    def _():
        grad_low_ref[:seg_rows, :] = out_grad_ref[...]
        grad_states_ref[:seg_rows, :] = out_grad_ref[...].astype(f32)
        if writes:
            grad_low_ref[seg_rows:, :] = low(grad_rows_ref[...])
            grad_states_ref[seg_rows:, :] = grad_rows_ref[...]
        else:
            grad_low_ref[seg_rows:, :] = jnp.zeros((rows - seg_rows, width), low_type)
            grad_states_ref[seg_rows:, :] = jnp.zeros((rows - seg_rows, width), f32)
        sum_ref[...] = jnp.zeros_like(sum_ref)

    upward = upward_ref[...]
    square = upward * upward
    bent = jnp.tanh(upward * (gelu_c + gelu_c * gelu_a * square))
    half = 0.5 + 0.5 * bent
    active = upward * half
    slope = half + (active - active * half) * (2.0 * gelu_c + 6.0 * gelu_c * gelu_a * square)
    grad_low = grad_low_ref[...]
    grad_upward = low(nt(grad_low, w_down_ref[...]) * slope)
    grad_down = tn(low(active), grad_low)
    grad_up = tn(normed_ref[...], grad_upward)
    sum_ref[...] += nt(grad_upward, w_up_ref[...])
    if adds:
        grad_down += down_in_ref[...]
        grad_up += up_in_ref[...]
    grad_down_ref[...] = grad_down.astype(grad_down_ref.dtype)
    grad_up_ref[...] = grad_up.astype(grad_up_ref.dtype)

    @pl.when(step == pl.num_programs(0) - 1)
    def _():
        gain = gains_ref[1:2, :]
        grad_gain_ref[...] = jnp.zeros_like(grad_gain_ref)

        def chunk(at):
            unit, inverse = normal_form(states_two_ref[at, :])
            grad = sum_ref[at, :]
            grad_gain_ref[...] += jnp.sum(grad * unit, axis=0, keepdims=True)
            total = grad_states_ref[at, :] + norm_back(grad, unit, inverse, gain)
            grad_states_ref[at, :] = total
            total_low = low(total)
            grad_two_ref[at, :] = total_low
            grad_attended_ref[at, :] = low(nt(total_low, w_out_ref[...]))

        over_rows(rows, chunk)
        grad_out = tn(attended_ref[...], grad_two_ref[...])
        if adds:
            grad_out += out_in_ref[...]
        grad_out_ref[...] = grad_out.astype(grad_out_ref.dtype)


def leave_back(slot, out_grad, grad_rows, kept, gains, w_out, w_up, w_down, sums, grad_type, moved=None):
    _, seg_rows, width = out_grad.shape
    rows = kept["normed_two"].shape[0]
    hidden = w_up.shape[1]
    size = 512 if hidden % 512 == 0 else hidden
    up_spec = pl.BlockSpec((width, size), lambda j: (0, j))
    down_spec = pl.BlockSpec((size, width), lambda j: (j, 0))
    args = [out_grad]
    in_specs = [
        pl.BlockSpec((None, seg_rows, width), lambda j: (slot, 0, 0), pipeline_mode=pl.Buffered(1))
    ]
    if grad_rows is not None:
        args.append(grad_rows)
        in_specs.append(whole(grad_rows.shape))
    args += [kept["states_two"], kept["normed_two"], kept["upward"], kept["attended"]]
    args += [gains, w_out, w_up, w_down]
    in_specs += [
        whole((rows, width)),
        whole((rows, width)),
        pl.BlockSpec((rows, size), lambda j: (0, j)),
        whole((rows, width)),
        whole(gains.shape),
        whole((width, width)),
        up_spec,
        down_spec,
    ]
    if sums is not None:
        args += [sums["up"], sums["down"], sums["out"]]
        in_specs += [up_spec, down_spec, whole((width, width))]
    body = functools.partial(leave_back_kernel, grad_rows is not None, sums is not None)
    out_specs = [
        result((rows, width)),
        result((rows, width)),
        up_spec,
        down_spec,
        result((width, width)),
        result((1, width)),
    ]
    out_shape = [
        shaped((rows, width), f32),
        shaped((rows, width), low_type),
        shaped((width, hidden), grad_type),
        shaped((hidden, width), grad_type),
        shaped((width, width), grad_type),
        shaped((1, width), f32),
    ]
    scratch = [
        pltpu.VMEM((rows, width), low_type),
        pltpu.VMEM((rows, width), f32),
        pltpu.VMEM((rows, width), low_type),
    ]
    extra = {}
    if moved is not None:
        shapes = [m.shape[-2:] for m in moved]
        groups = []
        before = 0
        for a, (_, cols) in enumerate(shapes):
            for at in range(0, cols, width):
                groups.append((a, at, width, 0, before + at, cut(width, (1, 1)), False))
            before += cols
        plan = Reduce(groups, shapes)
        grid = hidden // size
        schedule = {1: (0,), 2: (1,), 3: (2,), 4: (3,), 5: (4,), grid: (5,)}
        counts = (len(args), len(moved), len(out_shape), 1, len(scratch))
        body = functools.partial(carry_kernel, body, plan, counts, schedule, grid)
        args += moved
        in_specs += [ANYWHERE] * len(moved)
        total = (width // DEVICES, before)
        out_specs.append(result(total))
        out_shape.append(shaped(total, f32))
        scratch += plan.scratch()
        extra = dict(collective_id=1, has_side_effects=True)
    return pl.pallas_call(
        body,
        grid=(hidden // size,),
        in_specs=in_specs,
        out_specs=out_specs,
        out_shape=out_shape,
        scratch_shapes=scratch,
        compiler_params=params(**extra),
        cost_estimate=pl.CostEstimate(
            flops=4 * rows * width * (width + 2 * hidden), bytes_accessed=60 * 2**20, transcendentals=0
        ),
        name="leave_back",
    )(*args)


def enter_back_kernel(reads, adds, earlier, *refs):
    (tokens_ref, mem_ref, normed_ref, grad_qkv_ref, grad_states_ref, gains_ref, w_ref, *refs) = refs
    if reads:
        (
            states_ref,
            query_ref,
            match_ref,
            w_query_ref,
            phi_keys_ref,
            phi_rest_ref,
            delta_ref,
            beta_ref,
            *refs,
        ) = refs
    if adds:
        (w_in_ref, *refs) = refs
    if earlier:
        refs = refs[1:]
    (grad_tokens_ref, grad_mem_ref, grad_w_ref, grad_gain_ref, *refs) = refs
    if reads:
        (grad_w_query_ref, grad_delta_ref, grad_phi_ref, grad_normal_ref, *refs) = refs
    (first_ref, sum_ref, *refs) = refs
    rows, width = normed_ref.shape
    seg_rows = tokens_ref.shape[0]
    step = pl.program_id(0)

    @pl.when(step == 0)
    def _():
        load_first(tokens_ref, mem_ref, first_ref)
        sum_ref[...] = jnp.zeros_like(sum_ref)

    grad_part = grad_qkv_ref[0]
    sum_ref[...] += nt(grad_part, w_ref[...])
    grad_w = tn(normed_ref[...], grad_part)
    if adds:
        grad_w += w_in_ref[...]
    grad_w_ref[...] = grad_w.astype(grad_w_ref.dtype)

    @pl.when(step == pl.num_programs(0) - 1)
    def _():
        gain = gains_ref[0:1, :]
        grad_gain_ref[...] = jnp.zeros_like(grad_gain_ref)
        if reads:
            (grad_query_ref, packed_sum_ref, delta_sum_ref) = refs
            packed_sum_ref[...] = jnp.zeros_like(packed_sum_ref)
            delta_sum_ref[...] = jnp.zeros_like(delta_sum_ref)
            mems = delta_ref.shape[0]
            beta = beta_ref[...]
            basis = jnp.concatenate([phi_keys_ref[...], phi_keys_ref[...], phi_rest_ref[...]], axis=0)

        def chunk(at):
            first = first_ref[at, :].astype(f32)
            states = states_ref[at, :] if reads else first
            unit, inverse = normal_form(states)
            grad = sum_ref[at, :]
            grad_gain_ref[...] += jnp.sum(grad * unit, axis=0, keepdims=True)
            total = grad_states_ref[at, :] + norm_back(grad, unit, inverse, gain)
            if reads:
                match = match_ref[at, :]
                below = 1.0 + jnp.sum(match * beta, axis=1, keepdims=True)
                grad_num = low(total / below)
                grad_below = -jnp.sum(total * (states - first), axis=1, keepdims=True) / below
                pulled = nt(grad_num, delta_ref[...])
                spread_below = grad_below * beta
                both_high, both_low = split(pulled + spread_below)
                weights = jnp.concatenate([both_high, both_low, low(spread_below)], axis=1)
                query = query_ref[at, :]
                softer = softplus(query)
                parts = feature_parts(softer)
                grads = []
                packed = jnp.concatenate(
                    list(split(pulled))
                    + [low(jnp.broadcast_to(part, pulled.shape)) for part in (grad_below,)]
                    + [
                        low(
                            jnp.broadcast_to(
                                grad_below - low(grad_below).astype(f32), pulled.shape
                            )
                        )
                    ],
                    axis=1,
                )
                for index, part in enumerate(parts):
                    cols = slice(index * width, (index + 1) * width)
                    grads.append(nn(weights, basis[:, cols]))
                    packed_sum_ref[:, cols] += tn(packed, low(part))
                delta_sum_ref[...] += tn(jnp.concatenate(split(match), axis=1), grad_num)
                grad_query = low(feature_back(grads, softer, query))
                grad_query_ref[at, :] = grad_query
                total += nt(grad_query, w_query_ref[...])
            sum_ref[at, :] = total

        over_rows(rows, chunk)
        grad_tokens_ref[...] = sum_ref[:seg_rows, :]
        grad_mem_ref[...] = sum_ref[seg_rows:, :]
        if reads:
            grad_w_query_ref[...] = low(tn(first_ref[...], grad_query_ref[...]))
            grad_delta_ref[...] = delta_sum_ref[:mems, :] + delta_sum_ref[mems:, :]
            grad_phi_ref[...] = packed_sum_ref[:mems, :] + packed_sum_ref[mems : 2 * mems, :]
            grad_normal_ref[...] = (
                packed_sum_ref[2 * mems : 2 * mems + 1, :]
                + packed_sum_ref[3 * mems : 3 * mems + 1, :]
            )


def enter_back(
    slot, tokens, mem_tokens, kept, grad_qkv, grad_states, gains, w_qkv, w_mem, written, w_sum, earlier, grad_type
):
    slots, seg_rows, width = tokens.shape
    mems = mem_tokens.shape[0]
    rows = seg_rows + mems
    parts = grad_qkv.shape[0]
    reads = written is not None
    args = [tokens, mem_tokens, kept["normed_one"], grad_qkv, grad_states, gains, w_qkv]
    in_specs = [
        pl.BlockSpec((None, seg_rows, width), lambda j: (slot, 0, 0), pipeline_mode=pl.Buffered(1)),
        whole((mems, width)),
        whole((rows, width)),
        pl.BlockSpec((1, rows, width), lambda j: (j, 0, 0)),
        whole((rows, width)),
        whole(gains.shape),
        pl.BlockSpec((width, width), lambda j: (0, j)),
    ]
    scratch = [pltpu.VMEM((rows, width), low_type), pltpu.VMEM((rows, width), f32)]
    if reads:
        more = [written["phi_keys_low"], written["phi_keys_rest"]]
        more += [written["delta_low"], written["beta_row"]]
        args += [kept["states_one"], kept["query"], kept["match"], w_mem] + more
        in_specs += [whole((rows, width)), whole((rows, width)), whole((rows, mems)), whole((width, width))]
        in_specs += [whole(a.shape) for a in more]
        scratch += [
            pltpu.VMEM((rows, width), low_type),
            pltpu.VMEM((4 * mems, 3 * width), f32),
            pltpu.VMEM((2 * mems, width), f32),
        ]
    if w_sum is not None:
        args.append(w_sum)
        in_specs.append(pl.BlockSpec((width, width), lambda j: (0, j)))
    aliases = {}
    if earlier is not None:
        aliases = {len(args): 0}
        args.append(earlier)
        in_specs.append(pl.BlockSpec(memory_space=pl.ANY))
    out_specs = [
        pl.BlockSpec((None, seg_rows, width), lambda j: (slot, 0, 0)),
        result((mems, width)),
        pl.BlockSpec((width, width), lambda j: (0, j)),
        result((1, width)),
    ]
    out_shape = [
        shaped((slots, seg_rows, width), f32),
        shaped((mems, width), f32),
        shaped((width, parts * width), grad_type),
        shaped((1, width), f32),
    ]
    if reads:
        extra = [
            shaped((width, width), low_type),
            shaped((mems, width), f32),
            shaped((mems, 3 * width), f32),
            shaped((1, 3 * width), f32),
        ]
        out_shape += extra
        out_specs += [result(s.shape) for s in extra]
    return pl.pallas_call(
        functools.partial(enter_back_kernel, reads, w_sum is not None, earlier is not None),
        grid=(parts,),
        in_specs=in_specs,
        out_specs=out_specs,
        out_shape=out_shape,
        scratch_shapes=scratch,
        input_output_aliases=aliases,
        compiler_params=params(),
        cost_estimate=pl.CostEstimate(
            flops=4 * rows * width * width * (parts + 1), bytes_accessed=30 * 2**20, transcendentals=0
        ),
        name="enter_back",
    )(*args)


MESH = pl.DeviceIdType.MESH
DEPTH, SIDE = 4, 2
GRID = (DEPTH, SIDE, SIDE, SIDE)
DEVICES = DEPTH * SIDE**3
ORDERS = ("zxy", "zyx", "xyz", "yxz")
sems = pltpu.SemaphoreType.DMA


def my_place():
    wide = lax.axis_index("wide")
    narrow = lax.axis_index("narrow")
    return wide // SIDE, wide % SIDE, narrow // SIDE, narrow % SIDE


def device_at(z, x, y, core):
    return (z * SIDE + x, y * SIDE + core)


def partners(z, x, y, core):
    return {
        "z": [device_at((z + step) % DEPTH, x, y, core) for step in range(1, DEPTH)],
        "x": [device_at(z, 1 - x, y, core)],
        "y": [device_at(z, x, 1 - y, core)],
        "c": [device_at(z, x, y, 1 - core)],
    }


def meet(peers):
    barrier = pltpu.get_barrier_semaphore()
    everyone = [peer for group in peers.values() for peer in group]
    for peer in everyone:
        pl.semaphore_signal(barrier, inc=1, device_id=peer, device_id_type=MESH)
    pl.semaphore_wait(barrier, len(everyone))


def remote(source, target, send, recv, peer):
    return pltpu.make_async_remote_copy(
        src_ref=source,
        dst_ref=target,
        send_sem=send,
        recv_sem=recv,
        device_id=peer,
        device_id_type=MESH,
    )


def slab(ref, place, known, at):
    z, x, y, core = place
    return ref.at[
        slice(None) if "z" in known else z,
        slice(None) if "x" in known else x,
        slice(None) if "y" in known else y,
        slice(None) if "c" in known else core,
        :,
        at,
    ]


def cut(cols, shares):
    unit = cols // 128 // sum(shares)
    pieces = []
    at = 0
    for order, share in zip(ORDERS, shares):
        if share:
            pieces.append((order, at, share * unit * 128))
            at += share * unit * 128
    return pieces


class Gather:
    def __init__(self, groups, lead):
        self.groups = groups
        self.lead = lead
        self.ticks = len(groups) + 3
        self.numbers = {}
        for group, (_, pieces) in enumerate(groups):
            for piece in pieces:
                self.numbers[group, piece] = len(self.numbers)

    def scratch(self):
        count = len(self.numbers)
        return [sems((count,)), sems((count, 6)), sems((count, 6))]

    def bind(self, shards, fulls, scratch):
        self.shards = shards
        self.fulls = fulls
        self.own_sem, self.send_sem, self.recv_sem = scratch
        self.place = my_place()
        self.peers = partners(*self.place)

    def copies(self, index, group):
        a, pieces = self.groups[group]
        made = []
        for piece in pieces:
            order, start, size = piece
            number = self.numbers[group, piece]
            path = order + "c"
            at = pl.ds(start, size)
            target = slab(self.fulls[a], self.place, path[:index], at)
            source = self.shards[a].at[:, at] if index == 0 else target
            if index == 0:
                made.append(pltpu.make_async_copy(source, target, self.own_sem.at[number]))
            for step, peer in enumerate(self.peers[path[index]]):
                slot = index + step if path[index] == "z" else index + 2 * ("z" in path[:index])
                made.append(
                    remote(
                        source,
                        target,
                        self.send_sem.at[number, slot],
                        self.recv_sem.at[number, slot],
                        peer,
                    )
                )
        return made

    def begin(self, index, group):
        for copy in self.copies(index, group):
            copy.start()

    def enter(self):
        meet(self.peers)
        for group in range(min(self.lead, len(self.groups))):
            self.begin(0, group)

    def tick(self, now):
        total = len(self.groups)
        for index in (3, 2, 1, 0):
            group = now - index
            if not 0 <= group < total:
                continue
            for copy in self.copies(index, group):
                copy.wait()
            if index < 3:
                self.begin(index + 1, group)
            if index == 0 and group + self.lead < total:
                self.begin(0, group + self.lead)


class Reduce:
    def __init__(self, groups, shapes, ready=None):
        self.groups = groups
        self.shapes = shapes
        self.ready = ready or {}
        self.ticks = len(groups) + 3
        self.slots = 2
        count = 0
        self.entries = []
        for *_, pieces, _ in groups:
            self.entries.append([(count + i, piece) for i, piece in enumerate(pieces)])
            count += len(pieces)
        self.count = count

    def scratch(self):
        total = len(self.groups)
        made = [sems((total,)), sems((total,)), sems((total,)), sems((self.count, 5)), sems((self.count, 5))]
        for a, _, cols, _, _, pieces, held in self.groups:
            height = self.shapes[a][0]
            full = (DEPTH, SIDE, SIDE, height, cols)
            made.append(pltpu.VMEM(full, low_type))
            if not held:
                made.append(pltpu.VMEM(full, low_type))
            for _, _, size in pieces:
                made.append(pltpu.VMEM((DEPTH, SIDE, height, size), f32))
                made.append(pltpu.VMEM((DEPTH, SIDE, height, size), low_type))
                made.append(pltpu.VMEM((DEPTH, height, size), low_type))
                made.append(pltpu.VMEM((DEPTH - 1, height, size), low_type))
        return made

    def bind(self, partials, totals, scratch):
        self.partials = partials
        self.totals = totals
        self.own_sem, self.core_send, self.core_recv, self.send_sem, self.recv_sem, *scratch = scratch
        self.place = my_place()
        self.peers = partners(*self.place)
        z, x, y, core = self.place
        self.mine = {"x": x, "y": y}
        self.core_in, self.own, self.parts = [], [], {}
        for group, (*_, held) in enumerate(self.groups):
            core_in, *scratch = scratch
            self.core_in.append(core_in)
            if held:
                self.own.append(None)
            else:
                own, *scratch = scratch
                self.own.append(own)
            for number, _ in self.entries[group]:
                self.parts[number] = scratch[:4]
                scratch = scratch[4:]

    def enter(self):
        meet(self.peers)

    def core_copies(self, group):
        a, first, cols, _, _, _, held = self.groups[group]
        at = pl.ds(first, cols)
        core = self.place[3]
        made = [
            remote(
                self.partials[a].at[:, :, :, 1 - core, :, at],
                self.core_in[group],
                self.core_send.at[group],
                self.core_recv.at[group],
                self.peers["c"][0],
            )
        ]
        if not held:
            made.append(
                pltpu.make_async_copy(
                    self.partials[a].at[:, :, :, core, :, at], self.own[group], self.own_sem.at[group]
                )
            )
        return made

    def copies(self, index, group):
        if index == 0:
            return self.core_copies(group)
        made = []
        z = self.place[0]
        for number, (order, start, size) in self.entries[group]:
            kept, in1, in2, in3 = self.parts[number]
            if index == 1:
                axis = order[2]
                far = 1 - self.mine[axis]
                at = pl.ds(start, size)
                core_in = self.core_in[group]
                source = core_in.at[:, :, far, :, at] if axis == "y" else core_in.at[:, far, :, :, at]
                pairs = [(source, in1, self.peers[axis][0], 0)]
            elif index == 2:
                axis = order[1]
                pairs = [(in1.at[:, 1 - self.mine[axis]], in2, self.peers[axis][0], 1)]
            else:
                pairs = [
                    (in2.at[(z + step) % DEPTH], in3.at[step - 1], self.peers["z"][step - 1], 1 + step)
                    for step in range(1, DEPTH)
                ]
            for source, target, peer, slot in pairs:
                made.append(
                    remote(
                        source,
                        target,
                        self.send_sem.at[number, slot],
                        self.recv_sem.at[number, slot],
                        peer,
                    )
                )
        return made

    def begin(self, index, group):
        for copy in self.copies(index, group):
            copy.start()

    def add(self, index, group):
        z, x, y, core = self.place
        a, first, _, out, offset, _, held = self.groups[group]
        core_in = self.core_in[group]
        for number, (order, start, size) in self.entries[group]:
            kept, in1, in2, in3 = self.parts[number]
            at = pl.ds(start, size)
            if index == 0:
                axis = order[2]
                mine = self.mine[axis]

                def spot(step, where):
                    far, side = step // SIDE, step % SIDE
                    return (far, side, where) if axis == "y" else (far, where, side)

                def own_at(place):
                    if held:
                        inside = pl.ds(first + start, size)
                        return self.partials[a][place + (core, slice(None), inside)].astype(f32)
                    return self.own[group][place + (slice(None), at)].astype(f32)

                @pl.loop(0, DEPTH * SIDE)
                def _(step):
                    near = spot(step, mine)
                    away = spot(step, 1 - mine)
                    kept[step // SIDE, step % SIDE] = own_at(near) + core_in[near + (slice(None), at)].astype(f32)
                    moved = own_at(away) + core_in[away + (slice(None), at)].astype(f32)
                    core_in[away + (slice(None), at)] = low(moved)
            elif index == 1:
                mine = self.mine[order[1]]

                @pl.loop(0, DEPTH)
                def _(far):
                    kept[far, mine] += in1[far, mine].astype(f32)
                    in1[far, 1 - mine] = low(kept[far, 1 - mine] + in1[far, 1 - mine].astype(f32))
            elif index == 2:
                mine = self.mine[order[1]]
                kept[z, mine] += in2[z].astype(f32)
                for step in range(1, DEPTH):
                    target = (z + step) % DEPTH
                    in2[target] = low(kept[target, mine] + in2[target].astype(f32))
            else:
                mine = self.mine[order[1]]
                total = kept[z, mine]
                for step in range(DEPTH - 1):
                    total = total + in3[step].astype(f32)
                self.totals[out][:, pl.ds(offset + start, size)] = total

    def tick(self, now):
        total = len(self.groups)
        for index in (3, 2, 1, 0):
            group = now - index
            if not 0 <= group < total:
                continue
            for copy in self.copies(index, group):
                copy.wait()
            self.add(index, group)
            if index < 3:
                self.begin(index + 1, group)


class SmallSum:
    def __init__(self, shape):
        self.shape = shape
        self.ticks = 4

    def scratch(self):
        return [
            pltpu.VMEM((4,) + self.shape, f32),
            pltpu.VMEM((3,) + self.shape, f32),
            pltpu.VMEM((DEPTH,) + self.shape, f32),
            sems((6,)),
            sems((6,)),
        ]

    def bind(self, out, scratch):
        self.out = out
        self.sums, self.arrived, self.along, self.send_sem, self.recv_sem = scratch
        self.place = my_place()
        self.peers = partners(*self.place)

    def copies(self, index):
        if index < 3:
            return [
                remote(
                    self.sums.at[index],
                    self.arrived.at[index],
                    self.send_sem.at[index],
                    self.recv_sem.at[index],
                    self.peers["cyx"[index]][0],
                )
            ]
        return [
            remote(
                self.sums.at[3],
                self.along.at[self.place[0]],
                self.send_sem.at[3 + step],
                self.recv_sem.at[3 + step],
                self.peers["z"][step],
            )
            for step in range(DEPTH - 1)
        ]

    def enter(self, value):
        self.sums[0] = value
        for copy in self.copies(0):
            copy.start()

    def tick(self, index):
        for copy in self.copies(index):
            copy.wait()
        if index < 3:
            self.sums[index + 1] = self.sums[index] + self.arrived[index]
            if index == 2:
                self.along[self.place[0]] = self.sums[3]
            for copy in self.copies(index + 1):
                copy.start()
        else:
            total = self.along[0]
            for far in range(1, DEPTH):
                total = total + self.along[far]
            self.out[...] = total


def slabs(array):
    rows, cols = array.shape
    return array.reshape(GRID + (rows // DEVICES, cols))


def flat(array):
    return array.reshape(DEVICES * array.shape[-2], array.shape[-1])


ANYWHERE = pl.BlockSpec(memory_space=pl.ANY)


def gather_weights(shards):
    return [lax.all_gather(shard, AXES, axis=0, tiled=True) for shard in shards]


def scatter_sums(totals):
    return [
        lax.psum_scatter(total.astype(f32), AXES, scatter_dimension=0, tiled=True)
        for total in totals
    ]


def at_chunk(step, size):
    return pl.ds(pl.multiple_of(step * size, size), size)


def at_step(step, when):
    return lambda body: pl.when(step == when)(body)


def arrive_kernel(plan, seg_rows, schedule, *refs):
    count = len(plan.groups)
    tokens_ref, mem_ref, gains_ref, *refs = refs
    shards, refs = refs[:count], refs[count:]
    normed_ref, qkv_ref, attended_ref, log_ref, *refs = refs
    fulls, refs = refs[:count], refs[count:]
    first_ref, w_ref, w_sem, *refs = refs
    plan.bind(shards, fulls, refs)
    parts, rows, width = qkv_ref.shape
    step = pl.program_id(0)

    @pl.when(step == 0)
    def _():
        plan.enter()
        load_first(tokens_ref, mem_ref, first_ref)

        def chunk(at):
            unit, _ = normal_form(first_ref[at, :].astype(f32))
            normed_ref[at, :] = low(unit * gains_ref[0:1, :])

        over_rows(rows, chunk)

    for when, ticks in schedule.items():

        @pl.when(step == when)
        def _():
            for now in ticks:
                plan.tick(now)

    @pl.when(step == 0)
    def _():
        copy = pltpu.make_async_copy(fulls[0], w_ref, w_sem)
        copy.start()
        copy.wait()

    @pl.when(step < parts)
    def _():
        block = w_ref[..., at_chunk(step, width)].astype(f32).reshape(width, width)
        qkv_ref[step] = low(nn(normed_ref[...], low(block)))

    @pl.when(step >= parts)
    def _():
        attend_kernel(seg_rows, qkv_ref, attended_ref, log_ref, at_chunk(step - parts, PAIR))


def arrive(tokens, mem_tokens, gains, shards, plan, schedule):
    slots, seg_rows, width = tokens.shape
    mems = mem_tokens.shape[0]
    rows = seg_rows + mems
    parts = shards[0].shape[1] // width
    pairs = width // PAIR
    _, lanes = packed_lanes(rows, seg_rows)

    def pair(step):
        return jnp.maximum(step - parts, 0)

    outs = pl.pallas_call(
        functools.partial(arrive_kernel, plan, seg_rows, schedule),
        grid=(parts + pairs,),
        in_specs=[
            pl.BlockSpec((None, seg_rows, width), lambda j: (0, 0, 0), pipeline_mode=pl.Buffered(1)),
            whole((mems, width)),
            whole(gains.shape),
        ]
        + [ANYWHERE] * len(shards),
        out_specs=[
            result((rows, width)),
            result((parts, rows, width)),
            pl.BlockSpec((rows, PAIR), lambda j: (0, pair(j))),
            pl.BlockSpec((1, 1, lanes), lambda j: (pair(j), 0, 0)),
        ]
        + [ANYWHERE] * len(shards),
        out_shape=[
            shaped((rows, width), low_type),
            shaped((parts, rows, width), low_type),
            shaped((rows, width), low_type),
            shaped((pairs, 1, lanes), f32),
        ]
        + [shaped(GRID + shard.shape, low_type) for shard in shards],
        scratch_shapes=[
            pltpu.VMEM((rows, width), low_type),
            pltpu.VMEM(GRID + shards[0].shape, low_type),
            sems,
        ]
        + plan.scratch(),
        compiler_params=params(collective_id=0, has_side_effects=True),
        name="arrive",
    )(tokens, mem_tokens, gains, *shards)
    return outs[:4], [flat(o) for o in outs[4:]]


def carry_kernel(body, plan, counts, schedule, grid, *refs):
    ins, moved, outs, totals, scratch = counts
    parts = []
    for count in (ins, moved, outs, totals, scratch):
        parts.append(refs[:count])
        refs = refs[count:]
    own_in, partials, own_out, total_refs, own_scratch = parts
    plan.bind(partials, total_refs, refs)
    step = pl.program_id(0)

    @pl.when(step == 0)
    def _():
        plan.enter()
        for group in range(len(plan.groups)):
            plan.begin(0, group)

    for when, ticks in schedule.items():
        if when < grid:

            @pl.when(step == when)
            def _():
                for now in ticks:
                    plan.tick(now)

    body(*own_in, *own_out, *own_scratch)

    if grid in schedule:

        @pl.when(step == grid - 1)
        def _():
            for now in schedule[grid]:
                plan.tick(now)


def finish_kernel(plan, small, seg_rows, schedule, counts, *refs):
    (
        qkv_ref,
        grad_ref,
        attended_ref,
        log_ref,
        tokens_ref,
        mem_ref,
        normed_ref,
        gains_ref,
        w_ref,
        w_in_ref,
        small_in_ref,
        grad_states_ref,
        *refs,
    ) = refs
    moved, totals = counts
    partials, refs = refs[:moved], refs[moved:]
    first_ref, *refs = refs
    total_refs, refs = refs[:totals], refs[totals:]
    small_out_ref, keys_sum, values_sum, grad_qkv_ref, w_grad_ref, sum_ref, states_sem, *refs = refs
    kept = len(small.scratch())
    small.bind(small_out_ref, refs[:kept])
    plan.bind(list(partials) + [w_grad_ref], total_refs, refs[kept:])
    rows, width = normed_ref.shape
    parts = grad_qkv_ref.shape[0]
    pairs = width // PAIR
    step = pl.program_id(0)
    late = [g for g, group in enumerate(plan.groups) if group[-1]]
    early = [g for g, group in enumerate(plan.groups) if not group[-1]]
    states_copy = pltpu.make_async_copy(grad_states_ref, first_ref, states_sem)

    @pl.when(step == 0)
    def _():
        plan.enter()
        for group in early:
            plan.begin(0, group)
        states_copy.start()
        sum_ref[...] = jnp.zeros_like(sum_ref)

    for when, ticks in schedule.items():

        @pl.when(step == when)
        def _():
            for now in ticks:
                plan.tick(now)

    @pl.when(step < pairs)
    def _():
        attend_back_kernel(
            seg_rows,
            qkv_ref,
            grad_ref,
            attended_ref,
            log_ref,
            grad_qkv_ref,
            keys_sum,
            values_sum,
            at_chunk(step, PAIR),
        )

    @pl.when((step >= pairs) & (step < pairs + parts))
    def _():
        part = step - pairs
        grad_w = tn(normed_ref[...], grad_qkv_ref[part]) + w_in_ref[...]
        w_grad_ref[..., at_chunk(part, width)] = low(grad_w.reshape(GRID + (width // DEVICES, width)))
        for index, group in enumerate(late):

            @pl.when(part == index)
            def _():
                plan.begin(0, group)

    @pl.when(step >= pairs + parts)
    def _():
        sum_ref[...] += nt(grad_qkv_ref[step - pairs - parts], w_ref[...])

    @pl.when(step == pairs + 2 * parts - 1)
    def _():
        gain = gains_ref[0:1, :]
        states_copy.wait()
        small_out_ref[...] = small_in_ref[...]
        mems = rows - seg_rows

        def back(first, at):
            unit, inverse = normal_form(first)
            grad = sum_ref[at, :]
            small_out_ref[mems : mems + 1, :] += jnp.sum(grad * unit, axis=0, keepdims=True)
            first_ref[at, :] += norm_back(grad, unit, inverse, gain)

        def chunk(at):
            back(tokens_ref[at, :].astype(f32), at)

        over_rows(seg_rows, chunk)
        last = pl.ds(seg_rows, mems)
        back(mem_ref[...].astype(f32), last)
        small_out_ref[:mems, :] += first_ref[last, :]
        small.enter(small_out_ref[...])
        rest = list(range(sum(len(t) for t in schedule.values()), plan.ticks))
        for index in range(max(len(rest), small.ticks)):
            if index < len(rest):
                plan.tick(rest[index])
            if index < small.ticks:
                small.tick(index)


def finish(
    tokens, mem_tokens, kept, grad_attended, grad_states, gains, w_qkv, w_in, small_in, partials, plan, schedule, widths
):
    slots, seg_rows, width = tokens.shape
    mems = mem_tokens.shape[0]
    rows = seg_rows + mems
    qkv = kept["qkv"]
    parts = qkv.shape[0]
    pairs = width // PAIR
    small = SmallSum(small_in.shape)
    logs = kept["logs"]

    def pair(step):
        return jnp.minimum(step, pairs - 1)

    def part(step, start):
        return jnp.clip(step - start, 0, parts - 1)

    column = pl.BlockSpec((rows, PAIR), lambda j: (0, pair(j)))
    outs = pl.pallas_call(
        functools.partial(finish_kernel, plan, small, seg_rows, schedule, (len(partials), len(widths))),
        grid=(pairs + 2 * parts,),
        in_specs=[
            pl.BlockSpec((parts, rows, PAIR), lambda j: (0, 0, pair(j))),
            column,
            column,
            pl.BlockSpec((1,) + logs.shape[1:], lambda j: (pair(j), 0, 0)),
            pl.BlockSpec((None, seg_rows, width), lambda j: (0, 0, 0), pipeline_mode=pl.Buffered(1)),
            whole((mems, width)),
            whole((rows, width)),
            whole(gains.shape),
            pl.BlockSpec((width, width), lambda j: (0, part(j, pairs + parts))),
            pl.BlockSpec((width, width), lambda j: (0, part(j, pairs))),
            whole(small_in.shape),
            ANYWHERE,
        ]
        + [ANYWHERE] * len(partials),
        out_specs=[whole((rows, width))] + [whole(s) for s in widths] + [whole(small_in.shape)],
        out_shape=[shaped((rows, width), f32)]
        + [shaped(s, f32) for s in widths]
        + [shaped(small_in.shape, f32)],
        scratch_shapes=[
            pltpu.VMEM((rows, PAIR), f32),
            pltpu.VMEM((rows, PAIR), f32),
            pltpu.VMEM((parts, rows, width), low_type),
            pltpu.VMEM(GRID + (width // DEVICES, parts * width), low_type),
            pltpu.VMEM((rows, width), f32),
            sems,
        ]
        + small.scratch()
        + plan.scratch(),
        compiler_params=params(collective_id=2, has_side_effects=True),
        name="finish",
    )(
        qkv,
        grad_attended,
        kept["attended"],
        logs,
        tokens,
        mem_tokens,
        kept["normed_one"],
        gains,
        w_qkv,
        w_in,
        small_in,
        grad_states,
        *partials,
    )
    return outs[0], outs[1:-1], outs[-1]


def settle_kernel(count, first_ref, *refs):
    small_ref, *refs = refs
    sums, refs = refs[:count], refs[count + 1 :]
    tokens_ref, mem_ref, gains_ref, beta_ref, *outs = refs
    tokens_ref[...] = first_ref[...]

    @pl.when(pl.program_id(0) == 0)
    def _():
        mems = mem_ref.shape[0]
        mem_ref[...] = small_ref[:mems, :]
        gains_ref[...] = small_ref[mems : mems + 2, :]
        beta_ref[...] = small_ref[mems + 2 : mems + 3, :]
        for source, target in zip(sums, outs):
            target[...] = source[...]


def settle(first, small, sums, grad_tokens, mems):
    slots, seg_rows, width = grad_tokens.shape
    size = 256
    shapes = [(mems, width), (2, width), (1, width)] + [s.shape for s in sums]
    return pl.pallas_call(
        functools.partial(settle_kernel, len(sums)),
        grid=(seg_rows // size,),
        in_specs=[pl.BlockSpec((size, width), lambda j: (j, 0)), whole(small.shape)]
        + [whole(s.shape) for s in sums]
        + [ANYWHERE],
        out_specs=[pl.BlockSpec((None, size, width), lambda j: (0, j, 0))] + [result(s) for s in shapes],
        out_shape=[shaped(grad_tokens.shape, f32)] + [shaped(s, f32) for s in shapes],
        input_output_aliases={2 + len(sums): 0},
        compiler_params=params(),
        name="settle",
    )(first, small, *sums, grad_tokens)


def fast_gather(shards):
    shares = {2304: (8, 8, 1, 1), 768: (3, 3, 0, 0), 3072: (10, 10, 2, 2)}
    groups = []
    for a, shard in enumerate(shards):
        rows, cols = shard.shape
        groups.append((a, cut(cols, (2, 2, 1, 1) if rows > 48 else shares.get(cols, (1, 1)))))
    return Gather(groups, 1)


def on_device(
    fast, tokens, item_ids, w_mem, w_qkv, w_out, w_up, w_down, mem_tokens, gains, w_beta, out_grad
):
    slots, seg_rows, width = tokens.shape
    mems = mem_tokens.shape[0]
    gains = gains.astype(f32)
    w_beta = w_beta.astype(f32).reshape(1, width)
    shards = [w_qkv, w_out, w_up, w_down, w_mem]
    if fast:
        schedule = {0: (0, 1, 2, 3), 4: (4,), 6: (5,), 8: (6, 7)}
        arrived, fulls = arrive(tokens, mem_tokens, gains, shards, fast_gather(shards), schedule)
    else:
        fulls = gather_weights(shards)
    w_qkv, w_out, w_up, w_down, w_mem = fulls
    same_item = jnp.where(item_ids[1:] == item_ids[:-1], 1.0, 0.0).astype(f32)
    kept_all = []
    written = [None] * (slots + 1)
    out = None
    for slot in range(slots):
        kept = {}
        start = (tokens, mem_tokens)
        if fast and slot == 0:
            kept["normed_one"], kept["qkv"], kept["attended"], kept["logs"] = arrived
        else:
            entered = enter_segment(slot, tokens, mem_tokens, gains, w_qkv, w_mem, written[slot])
            kept["normed_one"], kept["qkv"] = entered[:2]
            if written[slot] is not None:
                kept["states_one"], kept["query"], kept["match"] = entered[2:]
                start = kept["states_one"]
            kept["attended"], kept["logs"] = attend(kept["qkv"], seg_rows)
        out, mem_out, kept["states_two"], kept["normed_two"], kept["upward"] = leave_segment(
            slot, slots, seg_rows, start, kept["attended"], gains, w_out, w_up, w_down, out
        )
        kept["mem_out"] = mem_out
        if slot + 1 < slots:
            written[slot + 1] = write_memory(same_item[slot : slot + 1], mem_out, w_mem, w_beta)
        kept_all.append(kept)

    sums = None
    qkv_sum = None
    grad_tokens = None
    grad_mem_tokens = 0.0
    gain_one_sum = 0.0
    gain_two_sum = 0.0
    grad_beta = 0.0
    pulled = None
    for slot in reversed(range(slots)):
        kept = kept_all[slot]
        last = slot == 0
        grad_type = low_type if last else f32
        grad_rows = None
        mem_plan = None
        if slot + 1 < slots:
            grad_rows, w_pair_sum, grad_beta_part = write_back(
                same_item[slot : slot + 1], kept["mem_out"], w_mem, w_beta, written[slot + 1], *pulled
            )
            grad_beta += grad_beta_part
            if fast and last:
                mem_plan = [slabs(w_query_sum), slabs(w_pair_sum)]
        left = leave_back(
            slot, out_grad, grad_rows, kept, gains, w_out, w_up, w_down, sums, grad_type, mem_plan
        )
        grad_states, grad_attended, up_sum, down_sum, out_sum, gain_two, *mem_total = left
        gain_two_sum += gain_two
        sums = {"up": up_sum, "down": down_sum, "out": out_sum}
        if fast and last:
            break
        grad_qkv = attend_back(kept["qkv"], grad_attended, kept["attended"], kept["logs"], seg_rows)
        grad_tokens, grad_mem, qkv_sum, gain_one, *extra = enter_back(
            slot,
            tokens,
            mem_tokens,
            kept,
            grad_qkv,
            grad_states,
            gains,
            w_qkv,
            w_mem,
            written[slot],
            qkv_sum,
            grad_tokens,
            grad_type,
        )
        if written[slot] is not None:
            w_query_sum, *pulled = extra
        grad_mem_tokens += grad_mem
        gain_one_sum += gain_one
    if fast:
        small = jnp.concatenate([grad_mem_tokens, gain_one_sum, gain_two_sum, grad_beta], axis=0)
        small = jnp.pad(small, ((0, -small.shape[0] % 8), (0, 0)))
        partials = [slabs(down_sum), slabs(up_sum), slabs(out_sum)]
        shapes = [p.shape[-2:] for p in partials] + [(width // DEVICES, w_qkv.shape[1])]
        half = shapes[1][1] // 2
        groups = [(0, 0, width, 0, 0, cut(width, (1, 1)), False)]
        groups += [(1, at, half, 1, at, cut(half, (1, 1)), False) for at in (0, half)]
        groups += [(2, 0, width, 2, 0, cut(width, (1, 1)), False)]
        groups += [
            (3, at, width, 3, at, cut(width, (1, 1)), True) for at in range(0, shapes[3][1], width)
        ]
        plan = Reduce(groups, shapes)
        schedule = {1: (0,), 4: (1,), 6: (2,), 9: (3,)}
        first, (down_total, up_total, out_total, qkv_total), small = finish(
            tokens,
            mem_tokens,
            kept,
            grad_attended,
            grad_states,
            gains,
            w_qkv,
            qkv_sum,
            small,
            partials,
            plan,
            schedule,
            shapes,
        )
        totals = [mem_total[0], qkv_total, out_total, up_total, down_total]
        grad_tokens, grad_mem_tokens, grad_gains, grad_beta, *totals = settle(
            first, small, totals, grad_tokens, mems
        )
        return (out, grad_tokens, *totals, grad_mem_tokens, grad_gains, grad_beta.reshape(width))
    mem_sum = jnp.concatenate([w_query_sum, w_pair_sum], axis=1)
    grad_gains = jnp.concatenate([gain_one_sum, gain_two_sum], axis=0)
    summed = scatter_sums([mem_sum, qkv_sum, sums["out"], sums["up"], sums["down"]])
    small = lax.psum((grad_mem_tokens, grad_gains, grad_beta.reshape(width)), AXES)
    return (out, grad_tokens, *summed, *small)


def solution(mesh):
    split_rows = P(AXES, None)
    split_items = P(AXES, None, None)
    in_specs = (
        split_items,
        P(AXES),
        split_rows,
        split_rows,
        split_rows,
        split_rows,
        split_rows,
        P(),
        P(),
        P(),
        split_items,
    )
    out_specs = (
        split_items,
        split_items,
        split_rows,
        split_rows,
        split_rows,
        split_rows,
        split_rows,
        P(),
        P(),
        P(),
    )
    fast = mesh.shape["wide"] == DEPTH * SIDE and mesh.shape["narrow"] == SIDE * SIDE
    return jax.shard_map(
        functools.partial(on_device, fast), mesh=mesh, in_specs=in_specs, out_specs=out_specs, check_vma=False
    )
```

```python
import functools

import jax
import jax.numpy as jnp
from jax import lax
from jax.experimental import pallas as pl
from jax.experimental.pallas import tpu as pltpu
from jax.sharding import PartitionSpec as P

HD = 64
PAIR = 2 * HD
AXES = ("wide", "narrow")
eps_norm = 1e-05
score_scale = 0.125
gelu_c = 0.7978845608028654
gelu_a = 0.044715
f32 = jnp.float32
low_type = jnp.bfloat16
MIB = 2**20
ANYWHERE = pl.BlockSpec(memory_space=pl.ANY)


def nn(left, right):
    return lax.dot_general(left, right, (((1,), (0,)), ((), ())), preferred_element_type=f32)


def nt(left, right):
    return lax.dot_general(left, right, (((1,), (1,)), ((), ())), preferred_element_type=f32)


def tn(left, right):
    return lax.dot_general(left, right, (((0,), (0,)), ((), ())), preferred_element_type=f32)


def low(values):
    return values.astype(low_type)


def split(values):
    high = low(values)
    return high, low(values - high.astype(f32))


def row_chunk(rows):
    for count in (208, 256, 128, 80, 64, 16):
        if rows % count == 0:
            return count
    return rows


def over_rows(rows, body):
    count = row_chunk(rows)

    @pl.loop(0, rows // count)
    def _(step):
        body(pl.ds(pl.multiple_of(step * count, count), count))


def normal_form(values):
    average = jnp.mean(values, axis=-1, keepdims=True)
    centered = values - average
    spread = jnp.mean(centered * centered, axis=-1, keepdims=True)
    inverse = lax.rsqrt(spread + eps_norm)
    return centered * inverse, inverse


def norm_back(grad, unit, inverse, gain):
    scaled = grad * gain
    mean_grad = jnp.mean(scaled, axis=-1, keepdims=True)
    mean_unit = jnp.mean(scaled * unit, axis=-1, keepdims=True)
    return inverse * (scaled - mean_grad - unit * mean_unit)


def softplus(values):
    return jnp.maximum(values, 0.0) + jnp.log1p(jnp.exp(-jnp.abs(values)))


def feature_parts(softer):
    return [softer * pltpu.roll(softer, offset, 1) for offset in (1, 2, 3)]


def feature_back(grads, softer, values):
    width = softer.shape[1]
    total = None
    for offset, grad in zip((1, 2, 3), grads):
        term = grad * pltpu.roll(softer, offset, 1) + pltpu.roll(grad * softer, width - offset, 1)
        total = term if total is None else total + term
    return total * jax.nn.sigmoid(values)


def whole(shape, memory=None):
    zeros = (0,) * len(shape)
    return pl.BlockSpec(shape, lambda *_: zeros, pipeline_mode=pl.Buffered(1))


def result(shape):
    zeros = (0,) * len(shape)
    return pl.BlockSpec(shape, lambda *_: zeros)


def params(mib=60, **extra):
    return pltpu.CompilerParams(vmem_limit_bytes=mib * MIB, **extra)


def shaped(shape, dtype):
    return jax.ShapeDtypeStruct(shape, dtype)


def load_first(tokens_ref, mem_ref, first_ref):
    seg_rows = tokens_ref.shape[0]
    first_ref[:seg_rows, :] = tokens_ref[...]
    first_ref[seg_rows:, :] = mem_ref[...]


def enter_kernel(tokens_ref, mem_ref, gains_ref, w_ref, normed_ref, qkv_ref, first_ref):
    @pl.when(pl.program_id(0) == 0)
    def _():
        load_first(tokens_ref, mem_ref, first_ref)

        def chunk(at):
            unit, _ = normal_form(first_ref[at, :].astype(f32))
            normed_ref[at, :] = low(unit * gains_ref[0:1, :])

        over_rows(first_ref.shape[0], chunk)

    qkv_ref[0] = low(nn(normed_ref[...], w_ref[...]))


def enter_read_kernel(
    tokens_ref,
    mem_ref,
    gains_ref,
    w_ref,
    w_query_ref,
    phi_keys_ref,
    delta_ref,
    beta_ref,
    normed_ref,
    qkv_ref,
    states_ref,
    query_ref,
    match_ref,
    first_ref,
):
    @pl.when(pl.program_id(0) == 0)
    def _():
        load_first(tokens_ref, mem_ref, first_ref)
        width = first_ref.shape[1]
        delta_twice = jnp.concatenate([delta_ref[...], delta_ref[...]], axis=0)

        def chunk(at):
            first = first_ref[at, :]
            query = nn(first, w_query_ref[...])
            query_ref[at, :] = query
            parts = feature_parts(softplus(query))
            match = None
            for index, part in enumerate(parts):
                term = nt(low(part), phi_keys_ref[:, index * width : (index + 1) * width])
                match = term if match is None else match + term
            match_ref[at, :] = match
            numerator = nn(jnp.concatenate(split(match), axis=1), delta_twice)
            below = 1.0 + jnp.sum(match * beta_ref[...], axis=1, keepdims=True)
            states = first.astype(f32) + numerator / below
            states_ref[at, :] = states
            unit, _ = normal_form(states)
            normed_ref[at, :] = low(unit * gains_ref[0:1, :])

        over_rows(first_ref.shape[0], chunk)

    qkv_ref[0] = low(nn(normed_ref[...], w_ref[...]))


def enter_segment(slot, tokens, mem_tokens, gains, w_qkv, w_mem, written):
    slots, seg_rows, width = tokens.shape
    mems = mem_tokens.shape[0]
    rows = seg_rows + mems
    parts = w_qkv.shape[1] // width
    in_specs = [
        pl.BlockSpec((None, seg_rows, width), lambda j: (slot, 0, 0), pipeline_mode=pl.Buffered(1)),
        whole((mems, width)),
        whole(gains.shape),
        pl.BlockSpec((width, width), lambda j: (0, j)),
    ]
    out_shape = [shaped((rows, width), low_type), shaped((parts, rows, width), low_type)]
    out_specs = [
        result((rows, width)),
        pl.BlockSpec((1, rows, width), lambda j: (j, 0, 0)),
    ]
    args = [tokens, mem_tokens, gains, w_qkv]
    body = enter_kernel
    macs = rows * width * width * parts
    if written is not None:
        body = enter_read_kernel
        args += [w_mem, written["phi_keys_low"], written["delta_low"], written["beta_row"]]
        in_specs += [whole((width, width))] + [whole(a.shape) for a in args[5:]]
        out_shape += [
            shaped((rows, width), f32),
            shaped((rows, width), f32),
            shaped((rows, mems), f32),
        ]
        out_specs += [result((rows, width)), result((rows, width)), result((rows, mems))]
        macs += rows * width * width
    return pl.pallas_call(
        body,
        grid=(parts,),
        in_specs=in_specs,
        out_specs=out_specs,
        out_shape=out_shape,
        scratch_shapes=[pltpu.VMEM((rows, width), low_type)],
        compiler_params=params(24),
        cost_estimate=pl.CostEstimate(
            flops=2 * macs, bytes_accessed=20 * 2**20, transcendentals=0
        ),
        name="enter_read" if written is not None else "enter",
    )(*args)


def query_blocks(rows, seg_rows):
    step = 256 if seg_rows % 256 == 0 else seg_rows
    blocks = [(at, step) for at in range(0, seg_rows, step)]
    return blocks + [(seg_rows, rows - seg_rows)]


def packed_lanes(rows, seg_rows):
    places = []
    at = 0
    for _, count in query_blocks(rows, seg_rows):
        places.append(at)
        at += -(-2 * count // 128) * 128
    return places, at


def stack_heads(block):
    lanes = lax.broadcasted_iota(jnp.int32, block.shape, 1)
    zero = jnp.zeros_like(block)
    return jnp.concatenate(
        [jnp.where(lanes < HD, block, zero), jnp.where(lanes < HD, zero, block)], axis=0
    )


def merge_heads(stacked):
    count = stacked.shape[0] // 2
    lanes = lax.broadcasted_iota(jnp.int32, (count, stacked.shape[1]), 1)
    return jnp.where(lanes < HD, stacked[:count], stacked[count:])


def as_row(column):
    count = column.shape[0]
    return jnp.transpose(jnp.broadcast_to(column, (count, 128)))[0:1, :]


def attend_kernel(seg_rows, qkv_ref, attended_ref, log_ref, lanes=slice(None)):
    rows = qkv_ref.shape[1]
    places, _ = packed_lanes(rows, seg_rows)
    for (start, count), place in zip(query_blocks(rows, seg_rows), places):
        reach = start + count
        queries = stack_heads(qkv_ref[0, start:reach, lanes] * score_scale)
        raw = nt(queries, qkv_ref[1, :reach, lanes])
        place_of = lax.broadcasted_iota(jnp.int32, (2 * count, count), 0)
        place_of = jnp.where(place_of < count, place_of, place_of - count)
        allowed = place_of >= lax.broadcasted_iota(jnp.int32, (2 * count, count), 1)
        edge = jnp.where(allowed, raw[:, start:], -1e30)
        masked = jnp.concatenate([raw[:, :start], edge], axis=1) if start else edge
        peak = jnp.max(masked, axis=1, keepdims=True)
        grown = jnp.exp(masked - peak)
        total = jnp.sum(grown, axis=1, keepdims=True)
        probs = low(grown * (1.0 / total))
        mixed = merge_heads(nn(probs, qkv_ref[2, :reach, lanes]))
        attended_ref[start:reach, :] = low(mixed)
        log_row = as_row(peak + jnp.log(total))
        log_ref[0, 0:1, place : place + 2 * count] = log_row


def attend(qkv, seg_rows):
    parts, rows, width = qkv.shape
    _, lanes = packed_lanes(rows, seg_rows)
    pairs = width // PAIR
    return pl.pallas_call(
        functools.partial(attend_kernel, seg_rows),
        grid=(pairs,),
        in_specs=[pl.BlockSpec((parts, rows, PAIR), lambda h: (0, 0, h))],
        out_specs=[
            pl.BlockSpec((rows, PAIR), lambda h: (0, h)),
            pl.BlockSpec((1, 1, lanes), lambda h: (h, 0, 0)),
        ],
        out_shape=[shaped((rows, width), low_type), shaped((pairs, 1, lanes), f32)],
        compiler_params=params(10),
        cost_estimate=pl.CostEstimate(
            flops=4 * rows * rows * width, bytes_accessed=7 * 2**20, transcendentals=0
        ),
        name="attend",
    )(qkv)


def attend_back_kernel(
    seg_rows,
    qkv_ref,
    grad_ref,
    attended_ref,
    log_ref,
    out_ref,
    keys_sum,
    values_sum,
    lanes=slice(None),
):
    rows = qkv_ref.shape[1]
    places, _ = packed_lanes(rows, seg_rows)
    ones = jnp.ones((8, PAIR), f32)
    blocks = list(zip(query_blocks(rows, seg_rows), places))
    for order, ((start, count), place) in enumerate(reversed(blocks)):
        reach = start + count
        queries = stack_heads(qkv_ref[0, start:reach, :] * score_scale)
        grads = stack_heads(grad_ref[start:reach, :])
        mixed = attended_ref[start:reach, :].astype(f32)
        both = jnp.concatenate([mixed, mixed], axis=0) * grads.astype(f32)
        inner = lax.dot_general(
            ones,
            both,
            (((1,), (1,)), ((), ())),
            precision=lax.Precision.HIGHEST,
            preferred_element_type=f32,
        )[0:1, :]
        keys = qkv_ref[1, :reach, :]
        raw = nt(keys, queries)
        log_row = log_ref[0, 0:1, place : place + 2 * count]
        probs = jnp.exp(raw - log_row)
        place_of = lax.broadcasted_iota(jnp.int32, (count, 2 * count), 1)
        place_of = jnp.where(place_of < count, place_of, place_of - count)
        allowed = place_of >= lax.broadcasted_iota(jnp.int32, (count, 2 * count), 0)
        edge = jnp.where(allowed, probs[start:], 0.0)
        probs = jnp.concatenate([probs[:start], edge], axis=0) if start else edge
        grad_probs = nt(qkv_ref[2, :reach, :], grads)
        grad_raw = low(probs * (grad_probs - inner))
        value_part = nn(low(probs), grads)
        key_part = nn(grad_raw, queries)
        if order == 0:
            values_sum[...] = value_part
            keys_sum[...] = key_part
        else:
            values_sum[:reach, :] += value_part
            keys_sum[:reach, :] += key_part
        out_ref[0, start:reach, lanes] = low(merge_heads(tn(grad_raw, keys)) * score_scale)
    out_ref[1, :, lanes] = low(keys_sum[...])
    out_ref[2, :, lanes] = low(values_sum[...])


def attend_back(qkv, grad_attended, attended, logs, seg_rows):
    parts, rows, width = qkv.shape
    pairs = width // PAIR
    column = pl.BlockSpec((rows, PAIR), lambda h: (0, h))
    three = pl.BlockSpec((parts, rows, PAIR), lambda h: (0, 0, h))
    return pl.pallas_call(
        functools.partial(attend_back_kernel, seg_rows),
        grid=(pairs,),
        in_specs=[
            three,
            column,
            column,
            pl.BlockSpec((1,) + logs.shape[1:], lambda h: (h, 0, 0)),
        ],
        out_specs=three,
        out_shape=shaped((parts, rows, width), low_type),
        scratch_shapes=[pltpu.VMEM((rows, PAIR), f32), pltpu.VMEM((rows, PAIR), f32)],
        compiler_params=params(12),
        cost_estimate=pl.CostEstimate(
            flops=10 * rows * rows * width, bytes_accessed=13 * 2**20, transcendentals=0
        ),
        name="attend_back",
    )(qkv, grad_attended, attended, logs)


def leave_kernel(
    reads, earlier, *refs
):
    if reads:
        (states_one_ref, *refs) = refs
    else:
        (tokens_ref, mem_ref, *refs) = refs
    (attended_ref, gains_ref, w_out_ref, w_up_ref, w_down_ref, *refs) = refs
    if earlier:
        refs = refs[1:]
    (out_ref, mem_out_ref, states_two_ref, normed_ref, upward_ref, sum_ref, *scratch) = refs
    rows, width = attended_ref.shape
    seg_rows = out_ref.shape[0]
    step = pl.program_id(0)

    @pl.when(step == 0)
    def _():
        if not reads:
            load_first(tokens_ref, mem_ref, scratch[0])

        def chunk(at):
            source = states_one_ref if reads else scratch[0]
            states = source[at, :].astype(f32) + nn(attended_ref[at, :], w_out_ref[...])
            states_two_ref[at, :] = states
            unit, _ = normal_form(states)
            normed_ref[at, :] = low(unit * gains_ref[1:2, :])
            sum_ref[at, :] = states

        over_rows(rows, chunk)

    def chunk(at):
        upward = nn(normed_ref[at, :], w_up_ref[...])
        upward_ref[at, :] = upward
        bent = jnp.tanh(upward * (gelu_c + gelu_c * gelu_a * (upward * upward)))
        active = low(upward * (0.5 + 0.5 * bent))
        sum_ref[at, :] += nn(active, w_down_ref[...])

    chunk(pl.ds(0, rows))

    @pl.when(step == pl.num_programs(0) - 1)
    def _():
        out_ref[...] = low(sum_ref[:seg_rows, :])
        mem_out_ref[...] = sum_ref[seg_rows:, :]


def leave_segment(slot, slots, seg_rows, start, attended, gains, w_out, w_up, w_down, earlier):
    rows, width = attended.shape
    hidden = w_up.shape[1]
    size = 512 if hidden % 512 == 0 else hidden
    reads = not isinstance(start, tuple)
    args = []
    in_specs = []
    scratch = [pltpu.VMEM((rows, width), f32)]
    if reads:
        args.append(start)
        in_specs.append(whole((rows, width)))
    else:
        tokens, mem_tokens = start
        args += [tokens, mem_tokens]
        in_specs += [
            pl.BlockSpec((None, seg_rows, width), lambda j: (slot, 0, 0), pipeline_mode=pl.Buffered(1)),
            whole(mem_tokens.shape),
        ]
        scratch.append(pltpu.VMEM((rows, width), low_type))
    args += [attended, gains, w_out, w_up, w_down]
    in_specs += [
        whole((rows, width)),
        whole(gains.shape),
        whole((width, width)),
        pl.BlockSpec((width, size), lambda j: (0, j)),
        pl.BlockSpec((size, width), lambda j: (j, 0)),
    ]
    aliases = {}
    if earlier is not None:
        aliases = {len(args): 0}
        args.append(earlier)
        in_specs.append(pl.BlockSpec(memory_space=pl.ANY))
    return pl.pallas_call(
        functools.partial(leave_kernel, reads, earlier is not None),
        grid=(hidden // size,),
        in_specs=in_specs,
        out_specs=[
            pl.BlockSpec((None, seg_rows, width), lambda j: (slot, 0, 0)),
            result((rows - seg_rows, width)),
            result((rows, width)),
            result((rows, width)),
            pl.BlockSpec((rows, size), lambda j: (0, j)),
        ],
        out_shape=[
            shaped((slots, seg_rows, width), low_type),
            shaped((rows - seg_rows, width), f32),
            shaped((rows, width), f32),
            shaped((rows, width), low_type),
            shaped((rows, hidden), f32),
        ],
        scratch_shapes=scratch,
        input_output_aliases=aliases,
        compiler_params=params(40),
        cost_estimate=pl.CostEstimate(
            flops=2 * rows * width * (width + 2 * hidden), bytes_accessed=36 * 2**20, transcendentals=0
        ),
        name="leave",
    )(*args)


def beta_parts(mem_out, w_beta):
    column = jnp.sum(mem_out * w_beta, axis=1, keepdims=True)
    row = lax.dot_general(
        w_beta,
        mem_out,
        (((1,), (1,)), ((), ())),
        precision=lax.Precision.HIGHEST,
        preferred_element_type=f32,
    )
    return jax.nn.sigmoid(column), jax.nn.sigmoid(row)


def write_kernel(
    flag_ref,
    mem_out_ref,
    w_key_ref,
    w_value_ref,
    w_beta_ref,
    key_ref,
    value_ref,
    phi_ref,
    phi_rest_ref,
    delta_ref,
    beta_row_ref,
):
    flag = flag_ref[0]
    width = key_ref.shape[1]
    mem_out = mem_out_ref[...]
    mem_low = low(mem_out)
    key = nn(mem_low, w_key_ref[...])
    value = nn(mem_low, w_value_ref[...])
    key_ref[...] = key
    value_ref[...] = value
    for index, part in enumerate(feature_parts(softplus(key))):
        high, rest = split(part)
        phi_ref[:, index * width : (index + 1) * width] = high
        phi_rest_ref[:, index * width : (index + 1) * width] = rest
    beta, beta_row = beta_parts(mem_out, w_beta_ref[...])
    delta_ref[...] = low(low(beta * value).astype(f32) * flag)
    beta_row_ref[...] = beta_row * flag


def write_memory(flag, mem_out, w_mem, w_beta):
    mems, width = mem_out.shape
    names = ("key", "value", "phi_keys_low", "phi_keys_rest", "delta_low", "beta_row")
    out_shape = [
        shaped((mems, width), f32),
        shaped((mems, width), f32),
        shaped((mems, 3 * width), low_type),
        shaped((mems, 3 * width), low_type),
        shaped((mems, width), low_type),
        shaped((1, mems), f32),
    ]
    outs = pl.pallas_call(
        write_kernel,
        grid=(1,),
        in_specs=[
            pl.BlockSpec(memory_space=pltpu.SMEM),
            whole((mems, width)),
            pl.BlockSpec((width, width), lambda j: (0, 1)),
            pl.BlockSpec((width, width), lambda j: (0, 2)),
            whole((1, width)),
        ],
        out_specs=[result(s.shape) for s in out_shape],
        out_shape=out_shape,
        compiler_params=params(10),
        name="write",
    )(flag, mem_out, w_mem, w_mem, w_beta)
    return dict(zip(names, outs))


def write_back_kernel(
    flag_ref,
    mem_out_ref,
    w_key_ref,
    w_value_ref,
    w_beta_ref,
    key_ref,
    value_ref,
    grad_delta_ref,
    grad_phi_ref,
    grad_normal_ref,
    grad_rows_ref,
    grad_w_ref,
    grad_beta_ref,
):
    flag = flag_ref[0]
    width = key_ref.shape[1]
    mem_out = mem_out_ref[...]
    mem_low = low(mem_out)
    w_beta = w_beta_ref[...]
    key = key_ref[...]
    value = value_ref[...]
    beta, _ = beta_parts(mem_out, w_beta)
    softer = softplus(key)
    parts = feature_parts(softer)
    grad_delta = grad_delta_ref[...] * flag
    grad_strength = jnp.sum(grad_delta * value, axis=1, keepdims=True)
    grads = []
    for index, part in enumerate(parts):
        at = slice(index * width, (index + 1) * width)
        grad_normal = grad_normal_ref[:, at] * flag
        grad_strength += jnp.sum(part * grad_normal, axis=1, keepdims=True)
        grads.append(grad_phi_ref[:, at] * flag + beta * grad_normal)
    grad_key = low(feature_back(grads, softer, key))
    grad_value = low(beta * grad_delta)
    grad_logit = grad_strength * beta * (1.0 - beta)
    grad_rows_ref[...] = (
        grad_logit * w_beta + nt(grad_key, w_key_ref[...]) + nt(grad_value, w_value_ref[...])
    )
    grad_beta_ref[...] = jnp.sum(grad_logit * mem_out, axis=0, keepdims=True)
    grad_w_ref[:, :width] = low(tn(mem_low, grad_key))
    grad_w_ref[:, width:] = low(tn(mem_low, grad_value))


def write_back(flag, mem_out, w_mem, w_beta, written, grad_delta, grad_phi, grad_normal):
    mems, width = mem_out.shape
    args = [flag, mem_out, w_mem, w_mem, w_beta, written["key"], written["value"]]
    args += [grad_delta, grad_phi, grad_normal]
    out_shape = [
        shaped((mems, width), f32),
        shaped((width, 2 * width), low_type),
        shaped((1, width), f32),
    ]
    return pl.pallas_call(
        write_back_kernel,
        grid=(1,),
        in_specs=[
            pl.BlockSpec(memory_space=pltpu.SMEM),
            whole((mems, width)),
            pl.BlockSpec((width, width), lambda j: (0, 1)),
            pl.BlockSpec((width, width), lambda j: (0, 2)),
        ]
        + [whole(a.shape) for a in args[4:]],
        out_specs=[result(s.shape) for s in out_shape],
        out_shape=out_shape,
        compiler_params=params(12),
        name="write_back",
    )(*args)


def leave_back_kernel(writes, adds, *refs):
    (out_grad_ref, *refs) = refs
    if writes:
        (grad_rows_ref, *refs) = refs
    (
        states_two_ref,
        normed_ref,
        upward_ref,
        attended_ref,
        gains_ref,
        w_out_ref,
        w_up_ref,
        w_down_ref,
        *refs,
    ) = refs
    if adds:
        (up_in_ref, down_in_ref, out_in_ref, *refs) = refs
    (
        grad_states_ref,
        grad_attended_ref,
        grad_up_ref,
        grad_down_ref,
        grad_out_ref,
        grad_gain_ref,
        grad_low_ref,
        sum_ref,
        grad_two_ref,
    ) = refs
    rows, width = normed_ref.shape
    seg_rows = out_grad_ref.shape[0]
    step = pl.program_id(0)

    @pl.when(step == 0)
    def _():
        grad_low_ref[:seg_rows, :] = out_grad_ref[...]
        grad_states_ref[:seg_rows, :] = out_grad_ref[...].astype(f32)
        if writes:
            grad_low_ref[seg_rows:, :] = low(grad_rows_ref[...])
            grad_states_ref[seg_rows:, :] = grad_rows_ref[...]
        else:
            grad_low_ref[seg_rows:, :] = jnp.zeros((rows - seg_rows, width), low_type)
            grad_states_ref[seg_rows:, :] = jnp.zeros((rows - seg_rows, width), f32)
        sum_ref[...] = jnp.zeros_like(sum_ref)

    upward = upward_ref[...]
    square = upward * upward
    bent = jnp.tanh(upward * (gelu_c + gelu_c * gelu_a * square))
    half = 0.5 + 0.5 * bent
    active = upward * half
    slope = half + (active - active * half) * (2.0 * gelu_c + 6.0 * gelu_c * gelu_a * square)
    grad_low = grad_low_ref[...]
    grad_upward = low(nt(grad_low, w_down_ref[...]) * slope)
    grad_down = tn(low(active), grad_low)
    grad_up = tn(normed_ref[...], grad_upward)
    sum_ref[...] += nt(grad_upward, w_up_ref[...])
    if adds:
        grad_down += down_in_ref[...]
        grad_up += up_in_ref[...]
    grad_down_ref[...] = grad_down.astype(grad_down_ref.dtype)
    grad_up_ref[...] = grad_up.astype(grad_up_ref.dtype)

    @pl.when(step == pl.num_programs(0) - 1)
    def _():
        gain = gains_ref[1:2, :]
        grad_gain_ref[...] = jnp.zeros_like(grad_gain_ref)

        def chunk(at):
            unit, inverse = normal_form(states_two_ref[at, :])
            grad = sum_ref[at, :]
            grad_gain_ref[...] += jnp.sum(grad * unit, axis=0, keepdims=True)
            total = grad_states_ref[at, :] + norm_back(grad, unit, inverse, gain)
            grad_states_ref[at, :] = total
            total_low = low(total)
            grad_two_ref[at, :] = total_low
            grad_attended_ref[at, :] = low(nt(total_low, w_out_ref[...]))

        over_rows(rows, chunk)
        grad_out = tn(attended_ref[...], grad_two_ref[...])
        if adds:
            grad_out += out_in_ref[...]
        grad_out_ref[...] = grad_out.astype(grad_out_ref.dtype)


def leave_back(slot, out_grad, grad_rows, kept, gains, w_out, w_up, w_down, sums, grad_type, moved=None):
    _, seg_rows, width = out_grad.shape
    rows = kept["normed_two"].shape[0]
    hidden = w_up.shape[1]
    size = 512 if hidden % 512 == 0 else hidden
    up_spec = pl.BlockSpec((width, size), lambda j: (0, j))
    down_spec = pl.BlockSpec((size, width), lambda j: (j, 0))
    args = [out_grad]
    in_specs = [
        pl.BlockSpec((None, seg_rows, width), lambda j: (slot, 0, 0), pipeline_mode=pl.Buffered(1))
    ]
    if grad_rows is not None:
        args.append(grad_rows)
        in_specs.append(whole(grad_rows.shape))
    args += [kept["states_two"], kept["normed_two"], kept["upward"], kept["attended"]]
    args += [gains, w_out, w_up, w_down]
    in_specs += [
        whole((rows, width)),
        whole((rows, width)),
        pl.BlockSpec((rows, size), lambda j: (0, j)),
        whole((rows, width)),
        whole(gains.shape),
        whole((width, width)),
        up_spec,
        down_spec,
    ]
    if sums is not None:
        args += [sums["up"], sums["down"], sums["out"]]
        in_specs += [up_spec, down_spec, whole((width, width))]
    body = functools.partial(leave_back_kernel, grad_rows is not None, sums is not None)
    out_specs = [
        result((rows, width)),
        result((rows, width)),
        up_spec,
        down_spec,
        result((width, width)),
        result((1, width)),
    ]
    out_shape = [
        shaped((rows, width), f32),
        shaped((rows, width), low_type),
        shaped((width, hidden), grad_type),
        shaped((hidden, width), grad_type),
        shaped((width, width), grad_type),
        shaped((1, width), f32),
    ]
    scratch = [
        pltpu.VMEM((rows, width), low_type),
        pltpu.VMEM((rows, width), f32),
        pltpu.VMEM((rows, width), low_type),
    ]
    extra = {}
    if moved is not None:
        shapes = [m.shape[-2:] for m in moved]
        groups = []
        before = 0
        for a, (_, cols) in enumerate(shapes):
            for at in range(0, cols, width):
                groups.append((a, at, width, 0, before + at, cut(width, (1, 1)), False))
            before += cols
        plan = Reduce(groups, shapes)
        grid = hidden // size
        schedule = {1: (0,), 2: (1,), 3: (2,), 4: (3,), 5: (4,), grid: (5,)}
        counts = (len(args), len(moved), len(out_shape), 1, len(scratch))
        body = functools.partial(carry_kernel, body, plan, counts, schedule, grid)
        args += moved
        in_specs += [ANYWHERE] * len(moved)
        total = (width // DEVICES, before)
        out_specs.append(result(total))
        out_shape.append(shaped(total, f32))
        scratch += plan.scratch()
        extra = dict(collective_id=1, has_side_effects=True)
    return pl.pallas_call(
        body,
        grid=(hidden // size,),
        in_specs=in_specs,
        out_specs=out_specs,
        out_shape=out_shape,
        scratch_shapes=scratch,
        compiler_params=params(**extra),
        cost_estimate=pl.CostEstimate(
            flops=4 * rows * width * (width + 2 * hidden), bytes_accessed=60 * 2**20, transcendentals=0
        ),
        name="leave_back",
    )(*args)


def leave_both_kernel(reads, adds, *refs):
    if reads:
        (states_one_ref, *refs) = refs
    else:
        (tokens_ref, mem_ref, *refs) = refs
    (attended_ref, out_grad_ref, gains_ref, w_out_ref, w_up_ref, w_down_ref, *refs) = refs
    if adds:
        refs = refs[1:]
    (
        out_ref,
        grad_states_ref,
        grad_attended_ref,
        grad_up_ref,
        grad_down_ref,
        grad_out_ref,
        grad_gain_ref,
        states_two_ref,
        normed_ref,
        forward_ref,
        backward_ref,
        grad_low_ref,
        *scratch,
    ) = refs
    rows, width = attended_ref.shape
    seg_rows = out_grad_ref.shape[0]
    step = pl.program_id(0)

    @pl.when(step == 0)
    def _():
        if not reads:
            load_first(tokens_ref, mem_ref, scratch[0])
        grad_low_ref[:seg_rows, :] = out_grad_ref[...]
        grad_low_ref[seg_rows:, :] = jnp.zeros((rows - seg_rows, width), low_type)

        def chunk(at):
            source = states_one_ref if reads else scratch[0]
            states = source[at, :].astype(f32) + nn(attended_ref[at, :], w_out_ref[...])
            states_two_ref[at, :] = states
            unit, _ = normal_form(states)
            normed_ref[at, :] = low(unit * gains_ref[1:2, :])
            forward_ref[at, :] = states
            backward_ref[at, :] = jnp.zeros_like(states)

        over_rows(rows, chunk)

    normed = normed_ref[...]
    grad_low = grad_low_ref[...]
    upward = nn(normed, w_up_ref[...])
    grad_active = nt(grad_low, w_down_ref[...])
    active, slope = gelu_parts(upward)
    active = low(active)
    grad_upward = low(grad_active * slope)
    forward_ref[...] += nn(active, w_down_ref[...])
    backward_ref[...] += nt(grad_upward, w_up_ref[...])
    grad_down = tn(active, grad_low)
    grad_up = tn(normed, grad_upward)
    grad_down_ref[...] = grad_down.astype(grad_down_ref.dtype)
    grad_up_ref[...] = grad_up.astype(grad_up_ref.dtype)

    @pl.when(step == pl.num_programs(0) - 1)
    def _():
        gain = gains_ref[1:2, :]
        grad_gain_ref[...] = jnp.zeros_like(grad_gain_ref)

        def chunk(at):
            unit, inverse = normal_form(states_two_ref[at, :])
            grad = backward_ref[at, :]
            grad_gain_ref[...] += jnp.sum(grad * unit, axis=0, keepdims=True)
            total = grad_low_ref[at, :].astype(f32) + norm_back(grad, unit, inverse, gain)
            grad_states_ref[at, :] = total
            total_low = low(total)
            normed_ref[at, :] = total_low
            grad_attended_ref[at, :] = low(nt(total_low, w_out_ref[...]))

        over_rows(rows, chunk)
        grad_out = tn(attended_ref[...], normed_ref[...])
        grad_out_ref[...] = grad_out.astype(grad_out_ref.dtype)
        out_ref[...] = low(forward_ref[:seg_rows, :])


def gelu_parts(upward):
    square = upward * upward
    bent = jnp.tanh(upward * (gelu_c + gelu_c * gelu_a * square))
    half = 0.5 + 0.5 * bent
    active = upward * half
    slope = half + (active - active * half) * (2.0 * gelu_c + 6.0 * gelu_c * gelu_a * square)
    return active, slope


def leave_both(slot, start, attended, out_grad, gains, w_out, w_up, w_down, earlier, grad_type):
    slots, seg_rows, width = out_grad.shape
    rows = attended.shape[0]
    mems = rows - seg_rows
    hidden = w_up.shape[1]
    size = 512 if hidden % 512 == 0 else hidden
    reads = not isinstance(start, tuple)
    args = []
    in_specs = []
    scratch = [
        pltpu.VMEM((rows, width), f32),
        pltpu.VMEM((rows, width), low_type),
        pltpu.VMEM((rows, width), f32),
        pltpu.VMEM((rows, width), f32),
        pltpu.VMEM((rows, width), low_type),
    ]
    segment = pl.BlockSpec((None, seg_rows, width), lambda j: (slot, 0, 0), pipeline_mode=pl.Buffered(1))
    if reads:
        args.append(start)
        in_specs.append(whole((rows, width)))
    else:
        args += list(start)
        in_specs += [segment, whole((mems, width))]
        scratch.append(pltpu.VMEM((rows, width), low_type))
    up_spec = pl.BlockSpec((width, size), lambda j: (0, j))
    down_spec = pl.BlockSpec((size, width), lambda j: (j, 0))
    args += [attended, out_grad, gains, w_out, w_up, w_down]
    in_specs += [
        whole((rows, width)),
        segment,
        whole(gains.shape),
        whole((width, width)),
        up_spec,
        down_spec,
    ]
    aliases = {}
    if earlier is not None:
        args.append(earlier)
        in_specs.append(ANYWHERE)
        aliases = {len(args) - 1: 0}
    outs = pl.pallas_call(
        functools.partial(leave_both_kernel, reads, earlier is not None),
        grid=(hidden // size,),
        in_specs=in_specs,
        out_specs=[
            segment,
            whole((rows, width)),
            whole((rows, width)),
            up_spec,
            down_spec,
            whole((width, width)),
            whole((1, width)),
        ],
        out_shape=[
            shaped((slots, seg_rows, width), low_type),
            shaped((rows, width), f32),
            shaped((rows, width), low_type),
            shaped((width, hidden), grad_type),
            shaped((hidden, width), grad_type),
            shaped((width, width), grad_type),
            shaped((1, width), f32),
        ],
        scratch_shapes=scratch,
        input_output_aliases=aliases,
        compiler_params=params(50),
        cost_estimate=pl.CostEstimate(
            flops=6 * rows * width * (width + 2 * hidden), bytes_accessed=60 * 2**20, transcendentals=0
        ),
        name="leave_both",
    )(*args)
    names = ("block_out", "grad_states", "grad_attended", "up", "down", "out", "gain_two")
    return dict(zip(names, outs))


def enter_back_kernel(reads, adds, earlier, *refs):
    (tokens_ref, mem_ref, normed_ref, grad_qkv_ref, grad_states_ref, gains_ref, w_ref, *refs) = refs
    if reads:
        (
            states_ref,
            query_ref,
            match_ref,
            w_query_ref,
            phi_keys_ref,
            phi_rest_ref,
            delta_ref,
            beta_ref,
            *refs,
        ) = refs
    if adds:
        (w_in_ref, *refs) = refs
    if earlier:
        refs = refs[1:]
    (grad_tokens_ref, grad_mem_ref, grad_w_ref, grad_gain_ref, *refs) = refs
    if reads:
        (grad_w_query_ref, grad_delta_ref, grad_phi_ref, grad_normal_ref, *refs) = refs
    (first_ref, sum_ref, *refs) = refs
    rows, width = normed_ref.shape
    seg_rows = tokens_ref.shape[0]
    step = pl.program_id(0)

    @pl.when(step == 0)
    def _():
        load_first(tokens_ref, mem_ref, first_ref)
        sum_ref[...] = jnp.zeros_like(sum_ref)

    grad_part = grad_qkv_ref[0]
    sum_ref[...] += nt(grad_part, w_ref[...])
    grad_w = tn(normed_ref[...], grad_part)
    if adds:
        grad_w += w_in_ref[...]
    grad_w_ref[...] = grad_w.astype(grad_w_ref.dtype)

    @pl.when(step == pl.num_programs(0) - 1)
    def _():
        gain = gains_ref[0:1, :]
        grad_gain_ref[...] = jnp.zeros_like(grad_gain_ref)
        if reads:
            (grad_query_ref, packed_sum_ref, delta_sum_ref) = refs
            packed_sum_ref[...] = jnp.zeros_like(packed_sum_ref)
            delta_sum_ref[...] = jnp.zeros_like(delta_sum_ref)
            mems = delta_ref.shape[0]
            beta = beta_ref[...]
            basis = jnp.concatenate([phi_keys_ref[...], phi_keys_ref[...], phi_rest_ref[...]], axis=0)

        def chunk(at):
            first = first_ref[at, :].astype(f32)
            states = states_ref[at, :] if reads else first
            unit, inverse = normal_form(states)
            grad = sum_ref[at, :]
            grad_gain_ref[...] += jnp.sum(grad * unit, axis=0, keepdims=True)
            total = grad_states_ref[at, :] + norm_back(grad, unit, inverse, gain)
            if reads:
                match = match_ref[at, :]
                below = 1.0 + jnp.sum(match * beta, axis=1, keepdims=True)
                grad_num = low(total / below)
                grad_below = -jnp.sum(total * (states - first), axis=1, keepdims=True) / below
                pulled = nt(grad_num, delta_ref[...])
                spread_below = grad_below * beta
                both_high, both_low = split(pulled + spread_below)
                weights = jnp.concatenate([both_high, both_low, low(spread_below)], axis=1)
                query = query_ref[at, :]
                softer = softplus(query)
                parts = feature_parts(softer)
                grads = []
                packed = jnp.concatenate(
                    list(split(pulled))
                    + [low(jnp.broadcast_to(part, pulled.shape)) for part in (grad_below,)]
                    + [
                        low(
                            jnp.broadcast_to(
                                grad_below - low(grad_below).astype(f32), pulled.shape
                            )
                        )
                    ],
                    axis=1,
                )
                for index, part in enumerate(parts):
                    cols = slice(index * width, (index + 1) * width)
                    grads.append(nn(weights, basis[:, cols]))
                    packed_sum_ref[:, cols] += tn(packed, low(part))
                delta_sum_ref[...] += tn(jnp.concatenate(split(match), axis=1), grad_num)
                grad_query = low(feature_back(grads, softer, query))
                grad_query_ref[at, :] = grad_query
                total += nt(grad_query, w_query_ref[...])
            sum_ref[at, :] = total

        over_rows(rows, chunk)
        grad_tokens_ref[...] = sum_ref[:seg_rows, :]
        grad_mem_ref[...] = sum_ref[seg_rows:, :]
        if reads:
            grad_w_query_ref[...] = low(tn(first_ref[...], grad_query_ref[...]))
            grad_delta_ref[...] = delta_sum_ref[:mems, :] + delta_sum_ref[mems:, :]
            grad_phi_ref[...] = packed_sum_ref[:mems, :] + packed_sum_ref[mems : 2 * mems, :]
            grad_normal_ref[...] = (
                packed_sum_ref[2 * mems : 2 * mems + 1, :]
                + packed_sum_ref[3 * mems : 3 * mems + 1, :]
            )


def enter_back(
    slot, tokens, mem_tokens, kept, grad_qkv, grad_states, gains, w_qkv, w_mem, written, w_sum, earlier, grad_type
):
    slots, seg_rows, width = tokens.shape
    mems = mem_tokens.shape[0]
    rows = seg_rows + mems
    parts = grad_qkv.shape[0]
    reads = written is not None
    args = [tokens, mem_tokens, kept["normed_one"], grad_qkv, grad_states, gains, w_qkv]
    in_specs = [
        pl.BlockSpec((None, seg_rows, width), lambda j: (slot, 0, 0), pipeline_mode=pl.Buffered(1)),
        whole((mems, width)),
        whole((rows, width)),
        pl.BlockSpec((1, rows, width), lambda j: (j, 0, 0)),
        whole((rows, width)),
        whole(gains.shape),
        pl.BlockSpec((width, width), lambda j: (0, j)),
    ]
    scratch = [pltpu.VMEM((rows, width), low_type), pltpu.VMEM((rows, width), f32)]
    if reads:
        more = [written["phi_keys_low"], written["phi_keys_rest"]]
        more += [written["delta_low"], written["beta_row"]]
        args += [kept["states_one"], kept["query"], kept["match"], w_mem] + more
        in_specs += [whole((rows, width)), whole((rows, width)), whole((rows, mems)), whole((width, width))]
        in_specs += [whole(a.shape) for a in more]
        scratch += [
            pltpu.VMEM((rows, width), low_type),
            pltpu.VMEM((4 * mems, 3 * width), f32),
            pltpu.VMEM((2 * mems, width), f32),
        ]
    if w_sum is not None:
        args.append(w_sum)
        in_specs.append(pl.BlockSpec((width, width), lambda j: (0, j)))
    aliases = {}
    if earlier is not None:
        aliases = {len(args): 0}
        args.append(earlier)
        in_specs.append(pl.BlockSpec(memory_space=pl.ANY))
    out_specs = [
        pl.BlockSpec((None, seg_rows, width), lambda j: (slot, 0, 0)),
        result((mems, width)),
        pl.BlockSpec((width, width), lambda j: (0, j)),
        result((1, width)),
    ]
    out_shape = [
        shaped((slots, seg_rows, width), f32),
        shaped((mems, width), f32),
        shaped((width, parts * width), grad_type),
        shaped((1, width), f32),
    ]
    if reads:
        extra = [
            shaped((width, width), low_type),
            shaped((mems, width), f32),
            shaped((mems, 3 * width), f32),
            shaped((1, 3 * width), f32),
        ]
        out_shape += extra
        out_specs += [result(s.shape) for s in extra]
    return pl.pallas_call(
        functools.partial(enter_back_kernel, reads, w_sum is not None, earlier is not None),
        grid=(parts,),
        in_specs=in_specs,
        out_specs=out_specs,
        out_shape=out_shape,
        scratch_shapes=scratch,
        input_output_aliases=aliases,
        compiler_params=params(36),
        cost_estimate=pl.CostEstimate(
            flops=4 * rows * width * width * (parts + 1), bytes_accessed=30 * 2**20, transcendentals=0
        ),
        name="enter_back",
    )(*args)


MESH = pl.DeviceIdType.MESH
DEPTH, SIDE = 4, 2
GRID = (DEPTH, SIDE, SIDE, SIDE)
DEVICES = DEPTH * SIDE**3
ORDERS = ("zxy", "zyx", "xyz", "yxz")
sems = pltpu.SemaphoreType.DMA


def my_place():
    wide = lax.axis_index("wide")
    narrow = lax.axis_index("narrow")
    return wide // SIDE, wide % SIDE, narrow // SIDE, narrow % SIDE


def device_at(z, x, y, core):
    return (z * SIDE + x, y * SIDE + core)


def partners(z, x, y, core):
    return {
        "z": [device_at((z + step) % DEPTH, x, y, core) for step in range(1, DEPTH)],
        "x": [device_at(z, 1 - x, y, core)],
        "y": [device_at(z, x, 1 - y, core)],
        "c": [device_at(z, x, y, 1 - core)],
    }


def meet(peers):
    barrier = pltpu.get_barrier_semaphore()
    everyone = [peer for group in peers.values() for peer in group]
    for peer in everyone:
        pl.semaphore_signal(barrier, inc=1, device_id=peer, device_id_type=MESH)
    pl.semaphore_wait(barrier, len(everyone))


def remote(source, target, send, recv, peer):
    return pltpu.make_async_remote_copy(
        src_ref=source,
        dst_ref=target,
        send_sem=send,
        recv_sem=recv,
        device_id=peer,
        device_id_type=MESH,
    )


def slab(ref, place, known, at):
    z, x, y, core = place
    return ref.at[
        slice(None) if "z" in known else z,
        slice(None) if "x" in known else x,
        slice(None) if "y" in known else y,
        slice(None) if "c" in known else core,
        :,
        at,
    ]


def cut(cols, shares):
    unit = cols // 128 // sum(shares)
    pieces = []
    at = 0
    for order, share in zip(ORDERS, shares):
        if share:
            pieces.append((order, at, share * unit * 128))
            at += share * unit * 128
    return pieces


class Gather:
    def __init__(self, groups, lead):
        self.groups = groups
        self.lead = lead
        self.ticks = len(groups) + 3
        self.numbers = {}
        for group, (_, pieces) in enumerate(groups):
            for piece in pieces:
                self.numbers[group, piece] = len(self.numbers)

    def scratch(self):
        count = len(self.numbers)
        return [sems((count,)), sems((count, 6)), sems((count, 6))]

    def bind(self, shards, fulls, scratch):
        self.shards = shards
        self.fulls = fulls
        self.own_sem, self.send_sem, self.recv_sem = scratch
        self.place = my_place()
        self.peers = partners(*self.place)

    def copies(self, index, group):
        a, pieces = self.groups[group]
        made = []
        for piece in pieces:
            order, start, size = piece
            number = self.numbers[group, piece]
            path = order + "c"
            at = pl.ds(start, size)
            target = slab(self.fulls[a], self.place, path[:index], at)
            source = self.shards[a].at[:, at] if index == 0 else target
            if index == 0:
                made.append(pltpu.make_async_copy(source, target, self.own_sem.at[number]))
            for step, peer in enumerate(self.peers[path[index]]):
                slot = index + step if path[index] == "z" else index + 2 * ("z" in path[:index])
                made.append(
                    remote(
                        source,
                        target,
                        self.send_sem.at[number, slot],
                        self.recv_sem.at[number, slot],
                        peer,
                    )
                )
        return made

    def begin(self, index, group):
        for copy in self.copies(index, group):
            copy.start()

    def enter(self):
        meet(self.peers)
        for group in range(min(self.lead, len(self.groups))):
            self.begin(0, group)

    def tick(self, now):
        total = len(self.groups)
        for index in (3, 2, 1, 0):
            group = now - index
            if not 0 <= group < total:
                continue
            for copy in self.copies(index, group):
                copy.wait()
            if index < 3:
                self.begin(index + 1, group)
            if index == 0 and group + self.lead < total:
                self.begin(0, group + self.lead)


class Reduce:
    def __init__(self, groups, shapes, ready=None):
        self.groups = groups
        self.shapes = shapes
        self.ready = ready or {}
        self.ticks = len(groups) + 3
        self.slots = 2
        count = 0
        self.entries = []
        for *_, pieces, _ in groups:
            self.entries.append([(count + i, piece) for i, piece in enumerate(pieces)])
            count += len(pieces)
        self.count = count

    def scratch(self):
        total = len(self.groups)
        made = [sems((total,)), sems((total,)), sems((total,)), sems((self.count, 5)), sems((self.count, 5))]
        for a, _, cols, _, _, pieces, held in self.groups:
            height = self.shapes[a][0]
            full = (DEPTH, SIDE, SIDE, height, cols)
            made.append(pltpu.VMEM(full, low_type))
            if not held:
                made.append(pltpu.VMEM(full, low_type))
            for _, _, size in pieces:
                made.append(pltpu.VMEM((DEPTH, SIDE, height, size), f32))
                made.append(pltpu.VMEM((DEPTH, SIDE, height, size), low_type))
                made.append(pltpu.VMEM((DEPTH, height, size), low_type))
                made.append(pltpu.VMEM((DEPTH - 1, height, size), low_type))
        return made

    def bind(self, partials, totals, scratch):
        self.partials = partials
        self.totals = totals
        self.own_sem, self.core_send, self.core_recv, self.send_sem, self.recv_sem, *scratch = scratch
        self.place = my_place()
        self.peers = partners(*self.place)
        z, x, y, core = self.place
        self.mine = {"x": x, "y": y}
        self.core_in, self.own, self.parts = [], [], {}
        for group, (*_, held) in enumerate(self.groups):
            core_in, *scratch = scratch
            self.core_in.append(core_in)
            if held:
                self.own.append(None)
            else:
                own, *scratch = scratch
                self.own.append(own)
            for number, _ in self.entries[group]:
                self.parts[number] = scratch[:4]
                scratch = scratch[4:]

    def enter(self):
        meet(self.peers)

    def core_copies(self, group):
        a, first, cols, _, _, _, held = self.groups[group]
        at = pl.ds(first, cols)
        core = self.place[3]
        made = [
            remote(
                self.partials[a].at[:, :, :, 1 - core, :, at],
                self.core_in[group],
                self.core_send.at[group],
                self.core_recv.at[group],
                self.peers["c"][0],
            )
        ]
        if not held:
            made.append(
                pltpu.make_async_copy(
                    self.partials[a].at[:, :, :, core, :, at], self.own[group], self.own_sem.at[group]
                )
            )
        return made

    def copies(self, index, group):
        if index == 0:
            return self.core_copies(group)
        made = []
        z = self.place[0]
        for number, (order, start, size) in self.entries[group]:
            kept, in1, in2, in3 = self.parts[number]
            if index == 1:
                axis = order[2]
                far = 1 - self.mine[axis]
                at = pl.ds(start, size)
                core_in = self.core_in[group]
                source = core_in.at[:, :, far, :, at] if axis == "y" else core_in.at[:, far, :, :, at]
                pairs = [(source, in1, self.peers[axis][0], 0)]
            elif index == 2:
                axis = order[1]
                pairs = [(in1.at[:, 1 - self.mine[axis]], in2, self.peers[axis][0], 1)]
            else:
                pairs = [
                    (in2.at[(z + step) % DEPTH], in3.at[step - 1], self.peers["z"][step - 1], 1 + step)
                    for step in range(1, DEPTH)
                ]
            for source, target, peer, slot in pairs:
                made.append(
                    remote(
                        source,
                        target,
                        self.send_sem.at[number, slot],
                        self.recv_sem.at[number, slot],
                        peer,
                    )
                )
        return made

    def begin(self, index, group):
        for copy in self.copies(index, group):
            copy.start()

    def add(self, index, group):
        z, x, y, core = self.place
        a, first, _, out, offset, _, held = self.groups[group]
        core_in = self.core_in[group]
        for number, (order, start, size) in self.entries[group]:
            kept, in1, in2, in3 = self.parts[number]
            at = pl.ds(start, size)
            if index == 0:
                axis = order[2]
                mine = self.mine[axis]

                def spot(step, where):
                    far, side = step // SIDE, step % SIDE
                    return (far, side, where) if axis == "y" else (far, where, side)

                def own_at(place):
                    if held:
                        inside = pl.ds(first + start, size)
                        return self.partials[a][place + (core, slice(None), inside)].astype(f32)
                    return self.own[group][place + (slice(None), at)].astype(f32)

                @pl.loop(0, DEPTH * SIDE)
                def _(step):
                    near = spot(step, mine)
                    away = spot(step, 1 - mine)
                    kept[step // SIDE, step % SIDE] = own_at(near) + core_in[near + (slice(None), at)].astype(f32)
                    moved = own_at(away) + core_in[away + (slice(None), at)].astype(f32)
                    core_in[away + (slice(None), at)] = low(moved)
            elif index == 1:
                mine = self.mine[order[1]]

                @pl.loop(0, DEPTH)
                def _(far):
                    kept[far, mine] += in1[far, mine].astype(f32)
                    in1[far, 1 - mine] = low(kept[far, 1 - mine] + in1[far, 1 - mine].astype(f32))
            elif index == 2:
                mine = self.mine[order[1]]
                kept[z, mine] += in2[z].astype(f32)
                for step in range(1, DEPTH):
                    target = (z + step) % DEPTH
                    in2[target] = low(kept[target, mine] + in2[target].astype(f32))
            else:
                mine = self.mine[order[1]]
                total = kept[z, mine]
                for step in range(DEPTH - 1):
                    total = total + in3[step].astype(f32)
                self.totals[out][:, pl.ds(offset + start, size)] = total

    def tick(self, now):
        total = len(self.groups)
        for index in (3, 2, 1, 0):
            group = now - index
            if not 0 <= group < total:
                continue
            for copy in self.copies(index, group):
                copy.wait()
            self.add(index, group)
            if index < 3:
                self.begin(index + 1, group)


class SmallSum:
    def __init__(self, shape):
        self.shape = shape
        self.ticks = 4

    def scratch(self):
        return [
            pltpu.VMEM((4,) + self.shape, f32),
            pltpu.VMEM((3,) + self.shape, f32),
            pltpu.VMEM((DEPTH,) + self.shape, f32),
            sems((6,)),
            sems((6,)),
        ]

    def bind(self, out, scratch):
        self.out = out
        self.sums, self.arrived, self.along, self.send_sem, self.recv_sem = scratch
        self.place = my_place()
        self.peers = partners(*self.place)

    def copies(self, index):
        if index < 3:
            return [
                remote(
                    self.sums.at[index],
                    self.arrived.at[index],
                    self.send_sem.at[index],
                    self.recv_sem.at[index],
                    self.peers["cyx"[index]][0],
                )
            ]
        return [
            remote(
                self.sums.at[3],
                self.along.at[self.place[0]],
                self.send_sem.at[3 + step],
                self.recv_sem.at[3 + step],
                self.peers["z"][step],
            )
            for step in range(DEPTH - 1)
        ]

    def enter(self, value):
        self.sums[0] = value
        for copy in self.copies(0):
            copy.start()

    def tick(self, index):
        for copy in self.copies(index):
            copy.wait()
        if index < 3:
            self.sums[index + 1] = self.sums[index] + self.arrived[index]
            if index == 2:
                self.along[self.place[0]] = self.sums[3]
            for copy in self.copies(index + 1):
                copy.start()
        else:
            total = self.along[0]
            for far in range(1, DEPTH):
                total = total + self.along[far]
            self.out[...] = total


def slabs(array):
    rows, cols = array.shape
    return array.reshape(GRID + (rows // DEVICES, cols))


def flat(array):
    return array.reshape(DEVICES * array.shape[-2], array.shape[-1])


def gather_weights(shards):
    return [lax.all_gather(shard, AXES, axis=0, tiled=True) for shard in shards]


def scatter_sums(totals):
    return [
        lax.psum_scatter(total.astype(f32), AXES, scatter_dimension=0, tiled=True)
        for total in totals
    ]


def at_chunk(step, size):
    return pl.ds(pl.multiple_of(step * size, size), size)


def at_step(step, when):
    return lambda body: pl.when(step == when)(body)


def arrive_kernel(plan, seg_rows, schedule, *refs):
    count = len(plan.groups)
    tokens_ref, mem_ref, gains_ref, *refs = refs
    shards, refs = refs[:count], refs[count:]
    normed_ref, qkv_ref, attended_ref, log_ref, *refs = refs
    fulls, refs = refs[:count], refs[count:]
    first_ref, w_ref, w_sem, *refs = refs
    plan.bind(shards, fulls, refs)
    parts, rows, width = qkv_ref.shape
    step = pl.program_id(0)

    @pl.when(step == 0)
    def _():
        plan.enter()
        load_first(tokens_ref, mem_ref, first_ref)

        def chunk(at):
            unit, _ = normal_form(first_ref[at, :].astype(f32))
            normed_ref[at, :] = low(unit * gains_ref[0:1, :])

        over_rows(rows, chunk)

    for when, ticks in schedule.items():

        @pl.when(step == when)
        def _():
            for now in ticks:
                plan.tick(now)

    @pl.when(step == 0)
    def _():
        copy = pltpu.make_async_copy(fulls[0], w_ref, w_sem)
        copy.start()
        copy.wait()

    @pl.when(step < parts)
    def _():
        block = w_ref[..., at_chunk(step, width)].astype(f32).reshape(width, width)
        qkv_ref[step] = low(nn(normed_ref[...], low(block)))

    @pl.when(step >= parts)
    def _():
        attend_kernel(seg_rows, qkv_ref, attended_ref, log_ref, at_chunk(step - parts, PAIR))


def arrive(tokens, mem_tokens, gains, shards, plan, schedule):
    slots, seg_rows, width = tokens.shape
    mems = mem_tokens.shape[0]
    rows = seg_rows + mems
    parts = shards[0].shape[1] // width
    pairs = width // PAIR
    _, lanes = packed_lanes(rows, seg_rows)

    def pair(step):
        return jnp.maximum(step - parts, 0)

    outs = pl.pallas_call(
        functools.partial(arrive_kernel, plan, seg_rows, schedule),
        grid=(parts + pairs,),
        in_specs=[
            pl.BlockSpec((None, seg_rows, width), lambda j: (0, 0, 0), pipeline_mode=pl.Buffered(1)),
            whole((mems, width)),
            whole(gains.shape),
        ]
        + [ANYWHERE] * len(shards),
        out_specs=[
            result((rows, width)),
            result((parts, rows, width)),
            pl.BlockSpec((rows, PAIR), lambda j: (0, pair(j))),
            pl.BlockSpec((1, 1, lanes), lambda j: (pair(j), 0, 0)),
        ]
        + [ANYWHERE] * len(shards),
        out_shape=[
            shaped((rows, width), low_type),
            shaped((parts, rows, width), low_type),
            shaped((rows, width), low_type),
            shaped((pairs, 1, lanes), f32),
        ]
        + [shaped(GRID + shard.shape, low_type) for shard in shards],
        scratch_shapes=[
            pltpu.VMEM((rows, width), low_type),
            pltpu.VMEM(GRID + shards[0].shape, low_type),
            sems,
        ]
        + plan.scratch(),
        compiler_params=params(collective_id=0, has_side_effects=True),
        name="arrive",
    )(tokens, mem_tokens, gains, *shards)
    return outs[:4], [flat(o) for o in outs[4:]]


def carry_kernel(body, plan, counts, schedule, grid, *refs):
    ins, moved, outs, totals, scratch = counts
    parts = []
    for count in (ins, moved, outs, totals, scratch):
        parts.append(refs[:count])
        refs = refs[count:]
    own_in, partials, own_out, total_refs, own_scratch = parts
    plan.bind(partials, total_refs, refs)
    step = pl.program_id(0)

    @pl.when(step == 0)
    def _():
        plan.enter()
        for group in range(len(plan.groups)):
            plan.begin(0, group)

    for when, ticks in schedule.items():
        if when < grid:

            @pl.when(step == when)
            def _():
                for now in ticks:
                    plan.tick(now)

    body(*own_in, *own_out, *own_scratch)

    if grid in schedule:

        @pl.when(step == grid - 1)
        def _():
            for now in schedule[grid]:
                plan.tick(now)


def finish_kernel(plan, small, seg_rows, schedule, counts, *refs):
    (
        qkv_ref,
        grad_ref,
        attended_ref,
        log_ref,
        tokens_ref,
        mem_ref,
        normed_ref,
        gains_ref,
        w_ref,
        w_in_ref,
        small_in_ref,
        grad_states_ref,
        *refs,
    ) = refs
    moved, totals = counts
    partials, refs = refs[:moved], refs[moved:]
    first_ref, *refs = refs
    total_refs, refs = refs[:totals], refs[totals:]
    small_out_ref, keys_sum, values_sum, grad_qkv_ref, w_grad_ref, sum_ref, states_sem, *refs = refs
    kept = len(small.scratch())
    small.bind(small_out_ref, refs[:kept])
    plan.bind(list(partials) + [w_grad_ref], total_refs, refs[kept:])
    rows, width = normed_ref.shape
    parts = grad_qkv_ref.shape[0]
    pairs = width // PAIR
    step = pl.program_id(0)
    late = [g for g, group in enumerate(plan.groups) if group[-1]]
    early = [g for g, group in enumerate(plan.groups) if not group[-1]]
    states_copy = pltpu.make_async_copy(grad_states_ref, first_ref, states_sem)

    @pl.when(step == 0)
    def _():
        plan.enter()
        for group in early:
            plan.begin(0, group)
        states_copy.start()
        sum_ref[...] = jnp.zeros_like(sum_ref)

    for when, ticks in schedule.items():

        @pl.when(step == when)
        def _():
            for now in ticks:
                plan.tick(now)

    @pl.when(step < pairs)
    def _():
        attend_back_kernel(
            seg_rows,
            qkv_ref,
            grad_ref,
            attended_ref,
            log_ref,
            grad_qkv_ref,
            keys_sum,
            values_sum,
            at_chunk(step, PAIR),
        )

    @pl.when((step >= pairs) & (step < pairs + parts))
    def _():
        part = step - pairs
        grad_w = tn(normed_ref[...], grad_qkv_ref[part]) + w_in_ref[...]
        w_grad_ref[..., at_chunk(part, width)] = low(grad_w.reshape(GRID + (width // DEVICES, width)))
        for index, group in enumerate(late):

            @pl.when(part == index)
            def _():
                plan.begin(0, group)

    @pl.when(step >= pairs + parts)
    def _():
        sum_ref[...] += nt(grad_qkv_ref[step - pairs - parts], w_ref[...])

    @pl.when(step == pairs + 2 * parts - 1)
    def _():
        gain = gains_ref[0:1, :]
        states_copy.wait()
        small_out_ref[...] = small_in_ref[...]
        mems = rows - seg_rows

        def back(first, at):
            unit, inverse = normal_form(first)
            grad = sum_ref[at, :]
            small_out_ref[mems : mems + 1, :] += jnp.sum(grad * unit, axis=0, keepdims=True)
            first_ref[at, :] += norm_back(grad, unit, inverse, gain)

        def chunk(at):
            back(tokens_ref[at, :].astype(f32), at)

        over_rows(seg_rows, chunk)
        last = pl.ds(seg_rows, mems)
        back(mem_ref[...].astype(f32), last)
        small_out_ref[:mems, :] += first_ref[last, :]
        small.enter(small_out_ref[...])
        rest = list(range(sum(len(t) for t in schedule.values()), plan.ticks))
        for index in range(max(len(rest), small.ticks)):
            if index < len(rest):
                plan.tick(rest[index])
            if index < small.ticks:
                small.tick(index)


def finish(
    tokens, mem_tokens, kept, grad_attended, grad_states, gains, w_qkv, w_in, small_in, partials, plan, schedule, widths
):
    slots, seg_rows, width = tokens.shape
    mems = mem_tokens.shape[0]
    rows = seg_rows + mems
    qkv = kept["qkv"]
    parts = qkv.shape[0]
    pairs = width // PAIR
    small = SmallSum(small_in.shape)
    logs = kept["logs"]

    def pair(step):
        return jnp.minimum(step, pairs - 1)

    def part(step, start):
        return jnp.clip(step - start, 0, parts - 1)

    column = pl.BlockSpec((rows, PAIR), lambda j: (0, pair(j)))
    outs = pl.pallas_call(
        functools.partial(finish_kernel, plan, small, seg_rows, schedule, (len(partials), len(widths))),
        grid=(pairs + 2 * parts,),
        in_specs=[
            pl.BlockSpec((parts, rows, PAIR), lambda j: (0, 0, pair(j))),
            column,
            column,
            pl.BlockSpec((1,) + logs.shape[1:], lambda j: (pair(j), 0, 0)),
            pl.BlockSpec((None, seg_rows, width), lambda j: (0, 0, 0), pipeline_mode=pl.Buffered(1)),
            whole((mems, width)),
            whole((rows, width)),
            whole(gains.shape),
            pl.BlockSpec((width, width), lambda j: (0, part(j, pairs + parts))),
            pl.BlockSpec((width, width), lambda j: (0, part(j, pairs))),
            whole(small_in.shape),
            ANYWHERE,
        ]
        + [ANYWHERE] * len(partials),
        out_specs=[whole((rows, width))] + [whole(s) for s in widths] + [whole(small_in.shape)],
        out_shape=[shaped((rows, width), f32)]
        + [shaped(s, f32) for s in widths]
        + [shaped(small_in.shape, f32)],
        scratch_shapes=[
            pltpu.VMEM((rows, PAIR), f32),
            pltpu.VMEM((rows, PAIR), f32),
            pltpu.VMEM((parts, rows, width), low_type),
            pltpu.VMEM(GRID + (width // DEVICES, parts * width), low_type),
            pltpu.VMEM((rows, width), f32),
            sems,
        ]
        + small.scratch()
        + plan.scratch(),
        compiler_params=params(collective_id=2, has_side_effects=True),
        name="finish",
    )(
        qkv,
        grad_attended,
        kept["attended"],
        logs,
        tokens,
        mem_tokens,
        kept["normed_one"],
        gains,
        w_qkv,
        w_in,
        small_in,
        grad_states,
        *partials,
    )
    return outs[0], outs[1:-1], outs[-1]


def settle_kernel(count, first_ref, *refs):
    small_ref, *refs = refs
    sums, refs = refs[:count], refs[count + 1 :]
    tokens_ref, mem_ref, gains_ref, beta_ref, *outs = refs
    tokens_ref[...] = first_ref[...]

    @pl.when(pl.program_id(0) == 0)
    def _():
        mems = mem_ref.shape[0]
        mem_ref[...] = small_ref[:mems, :]
        gains_ref[...] = small_ref[mems : mems + 2, :]
        beta_ref[...] = small_ref[mems + 2 : mems + 3, :]
        for source, target in zip(sums, outs):
            target[...] = source[...]


def settle(first, small, sums, grad_tokens, mems):
    slots, seg_rows, width = grad_tokens.shape
    size = 256
    shapes = [(mems, width), (2, width), (1, width)] + [s.shape for s in sums]
    return pl.pallas_call(
        functools.partial(settle_kernel, len(sums)),
        grid=(seg_rows // size,),
        in_specs=[pl.BlockSpec((size, width), lambda j: (j, 0)), whole(small.shape)]
        + [whole(s.shape) for s in sums]
        + [ANYWHERE],
        out_specs=[pl.BlockSpec((None, size, width), lambda j: (0, j, 0))] + [result(s) for s in shapes],
        out_shape=[shaped(grad_tokens.shape, f32)] + [shaped(s, f32) for s in shapes],
        input_output_aliases={2 + len(sums): 0},
        compiler_params=params(10),
        name="settle",
    )(first, small, *sums, grad_tokens)


def fast_gather(shards):
    shares = {2304: (8, 8, 1, 1), 768: (3, 3, 0, 0), 3072: (10, 10, 2, 2)}
    groups = []
    for a, shard in enumerate(shards):
        rows, cols = shard.shape
        groups.append((a, cut(cols, (2, 2, 1, 1) if rows > 48 else shares.get(cols, (1, 1)))))
    return Gather(groups, 1)


def on_device(
    fast, tokens, item_ids, w_mem, w_qkv, w_out, w_up, w_down, mem_tokens, gains, w_beta, out_grad
):
    slots, seg_rows, width = tokens.shape
    mems = mem_tokens.shape[0]
    gains = gains.astype(f32)
    w_beta = w_beta.astype(f32).reshape(1, width)
    shards = [w_qkv, w_out, w_up, w_down, w_mem]
    if fast:
        schedule = {0: (0, 1, 2, 3), 4: (4,), 6: (5,), 8: (6, 7)}
        arrived, fulls = arrive(tokens, mem_tokens, gains, shards, fast_gather(shards), schedule)
    else:
        fulls = gather_weights(shards)
    w_qkv, w_out, w_up, w_down, w_mem = fulls
    same_item = jnp.where(item_ids[1:] == item_ids[:-1], 1.0, 0.0).astype(f32)
    kept_all = []
    written = [None] * (slots + 1)
    out = None
    for slot in range(slots):
        kept = {}
        start = (tokens, mem_tokens)
        if fast and slot == 0:
            kept["normed_one"], kept["qkv"], kept["attended"], kept["logs"] = arrived
        else:
            entered = enter_segment(slot, tokens, mem_tokens, gains, w_qkv, w_mem, written[slot])
            kept["normed_one"], kept["qkv"] = entered[:2]
            if written[slot] is not None:
                kept["states_one"], kept["query"], kept["match"] = entered[2:]
                start = kept["states_one"]
            kept["attended"], kept["logs"] = attend(kept["qkv"], seg_rows)
        if slot + 1 == slots:
            both = leave_both(slot, start, kept["attended"], out_grad, gains, w_out, w_up, w_down, out, f32)
            out = both["block_out"]
        else:
            out, mem_out, kept["states_two"], kept["normed_two"], kept["upward"] = leave_segment(
                slot, slots, seg_rows, start, kept["attended"], gains, w_out, w_up, w_down, out
            )
            kept["mem_out"] = mem_out
            written[slot + 1] = write_memory(same_item[slot : slot + 1], mem_out, w_mem, w_beta)
        kept_all.append(kept)

    sums = None
    qkv_sum = None
    grad_tokens = None
    grad_mem_tokens = 0.0
    gain_one_sum = 0.0
    gain_two_sum = 0.0
    grad_beta = 0.0
    pulled = None
    for slot in reversed(range(slots)):
        kept = kept_all[slot]
        last = slot == 0
        grad_type = low_type if last else f32
        grad_rows = None
        mem_plan = None
        if slot + 1 < slots:
            grad_rows, w_pair_sum, grad_beta_part = write_back(
                same_item[slot : slot + 1], kept["mem_out"], w_mem, w_beta, written[slot + 1], *pulled
            )
            grad_beta += grad_beta_part
            if fast and last:
                mem_plan = [slabs(w_query_sum), slabs(w_pair_sum)]
            left = leave_back(
                slot, out_grad, grad_rows, kept, gains, w_out, w_up, w_down, sums, grad_type, mem_plan
            )
        else:
            left = [both[name] for name in ("grad_states", "grad_attended", "up", "down", "out", "gain_two")]
        grad_states, grad_attended, up_sum, down_sum, out_sum, gain_two, *mem_total = left
        gain_two_sum += gain_two
        sums = {"up": up_sum, "down": down_sum, "out": out_sum}
        if fast and last:
            break
        grad_qkv = attend_back(kept["qkv"], grad_attended, kept["attended"], kept["logs"], seg_rows)
        grad_tokens, grad_mem, qkv_sum, gain_one, *extra = enter_back(
            slot,
            tokens,
            mem_tokens,
            kept,
            grad_qkv,
            grad_states,
            gains,
            w_qkv,
            w_mem,
            written[slot],
            qkv_sum,
            grad_tokens,
            grad_type,
        )
        if written[slot] is not None:
            w_query_sum, *pulled = extra
        grad_mem_tokens += grad_mem
        gain_one_sum += gain_one
    if fast:
        small = jnp.concatenate([grad_mem_tokens, gain_one_sum, gain_two_sum, grad_beta], axis=0)
        small = jnp.pad(small, ((0, -small.shape[0] % 8), (0, 0)))
        partials = [slabs(down_sum), slabs(up_sum), slabs(out_sum)]
        shapes = [p.shape[-2:] for p in partials] + [(width // DEVICES, w_qkv.shape[1])]
        half = shapes[1][1] // 2
        groups = [(0, 0, width, 0, 0, cut(width, (1, 1)), False)]
        groups += [(1, at, half, 1, at, cut(half, (1, 1)), False) for at in (0, half)]
        groups += [(2, 0, width, 2, 0, cut(width, (1, 1)), False)]
        groups += [
            (3, at, width, 3, at, cut(width, (1, 1)), True) for at in range(0, shapes[3][1], width)
        ]
        plan = Reduce(groups, shapes)
        schedule = {1: (0,), 4: (1,), 6: (2,), 9: (3,)}
        first, (down_total, up_total, out_total, qkv_total), small = finish(
            tokens,
            mem_tokens,
            kept,
            grad_attended,
            grad_states,
            gains,
            w_qkv,
            qkv_sum,
            small,
            partials,
            plan,
            schedule,
            shapes,
        )
        totals = [mem_total[0], qkv_total, out_total, up_total, down_total]
        grad_tokens, grad_mem_tokens, grad_gains, grad_beta, *totals = settle(
            first, small, totals, grad_tokens, mems
        )
        return (out, grad_tokens, *totals, grad_mem_tokens, grad_gains, grad_beta.reshape(width))
    mem_sum = jnp.concatenate([w_query_sum, w_pair_sum], axis=1)
    grad_gains = jnp.concatenate([gain_one_sum, gain_two_sum], axis=0)
    summed = scatter_sums([mem_sum, qkv_sum, sums["out"], sums["up"], sums["down"]])
    small = lax.psum((grad_mem_tokens, grad_gains, grad_beta.reshape(width)), AXES)
    return (out, grad_tokens, *summed, *small)


def solution(mesh):
    split_rows = P(AXES, None)
    split_items = P(AXES, None, None)
    in_specs = (
        split_items,
        P(AXES),
        split_rows,
        split_rows,
        split_rows,
        split_rows,
        split_rows,
        P(),
        P(),
        P(),
        split_items,
    )
    out_specs = (
        split_items,
        split_items,
        split_rows,
        split_rows,
        split_rows,
        split_rows,
        split_rows,
        P(),
        P(),
        P(),
    )
    fast = mesh.shape["wide"] == DEPTH * SIDE and mesh.shape["narrow"] == SIDE * SIDE
    return jax.shard_map(
        functools.partial(on_device, fast), mesh=mesh, in_specs=in_specs, out_specs=out_specs, check_vma=False
    )
```

```python
import functools

import jax
import jax.numpy as jnp
from jax import lax
from jax.experimental import pallas as pl
from jax.experimental.pallas import tpu as pltpu
from jax.sharding import PartitionSpec as P

HD = 64
PAIR = 2 * HD
AXES = ("wide", "narrow")
eps_norm = 1e-05
score_scale = 0.125
gelu_c = 0.7978845608028654
gelu_a = 0.044715
f32 = jnp.float32
low_type = jnp.bfloat16
MIB = 2**20
ANYWHERE = pl.BlockSpec(memory_space=pl.ANY)


def nn(left, right):
    return lax.dot_general(left, right, (((1,), (0,)), ((), ())), preferred_element_type=f32)


def nt(left, right):
    return lax.dot_general(left, right, (((1,), (1,)), ((), ())), preferred_element_type=f32)


def tn(left, right):
    return lax.dot_general(left, right, (((0,), (0,)), ((), ())), preferred_element_type=f32)


def low(values):
    return values.astype(low_type)


def split(values):
    high = low(values)
    return high, low(values - high.astype(f32))


def row_chunk(rows):
    for count in (208, 256, 128, 80, 64, 16):
        if rows % count == 0:
            return count
    return rows


def over_rows(rows, body, at_once=True):
    if at_once:
        body(pl.ds(0, rows))
        return
    count = row_chunk(rows)

    @pl.loop(0, rows // count)
    def _(step):
        body(pl.ds(pl.multiple_of(step * count, count), count))


def normal_form(values):
    average = jnp.mean(values, axis=-1, keepdims=True)
    centered = values - average
    spread = jnp.mean(centered * centered, axis=-1, keepdims=True)
    inverse = lax.rsqrt(spread + eps_norm)
    return centered * inverse, inverse


def norm_back(grad, unit, inverse, gain):
    scaled = grad * gain
    mean_grad = jnp.mean(scaled, axis=-1, keepdims=True)
    mean_unit = jnp.mean(scaled * unit, axis=-1, keepdims=True)
    return inverse * (scaled - mean_grad - unit * mean_unit)


def softplus(values):
    return jnp.maximum(values, 0.0) + jnp.log1p(jnp.exp(-jnp.abs(values)))


def feature_parts(softer):
    return [softer * pltpu.roll(softer, offset, 1) for offset in (1, 2, 3)]


def feature_back(grads, softer, values):
    width = softer.shape[1]
    total = None
    for offset, grad in zip((1, 2, 3), grads):
        term = grad * pltpu.roll(softer, offset, 1) + pltpu.roll(grad * softer, width - offset, 1)
        total = term if total is None else total + term
    return total * jax.nn.sigmoid(values)


def whole(shape, memory=None):
    zeros = (0,) * len(shape)
    return pl.BlockSpec(shape, lambda *_: zeros, pipeline_mode=pl.Buffered(1))


def result(shape):
    zeros = (0,) * len(shape)
    return pl.BlockSpec(shape, lambda *_: zeros)


def params(mib=60, **extra):
    return pltpu.CompilerParams(vmem_limit_bytes=mib * MIB, **extra)


def shaped(shape, dtype):
    return jax.ShapeDtypeStruct(shape, dtype)


def load_first(tokens_ref, mem_ref, first_ref):
    seg_rows = tokens_ref.shape[0]
    first_ref[:seg_rows, :] = tokens_ref[...]
    first_ref[seg_rows:, :] = mem_ref[...]


def enter_kernel(tokens_ref, mem_ref, gains_ref, w_ref, normed_ref, qkv_ref, first_ref):
    @pl.when(pl.program_id(0) == 0)
    def _():
        load_first(tokens_ref, mem_ref, first_ref)

        def chunk(at):
            unit, _ = normal_form(first_ref[at, :].astype(f32))
            normed_ref[at, :] = low(unit * gains_ref[0:1, :].astype(f32))

        over_rows(first_ref.shape[0], chunk)

    qkv_ref[0] = low(nn(normed_ref[...], w_ref[...]))


def enter_read_kernel(
    tokens_ref,
    mem_ref,
    gains_ref,
    w_ref,
    w_query_ref,
    phi_keys_ref,
    delta_ref,
    beta_ref,
    normed_ref,
    qkv_ref,
    states_ref,
    query_ref,
    match_ref,
    first_ref,
):
    @pl.when(pl.program_id(0) == 0)
    def _():
        load_first(tokens_ref, mem_ref, first_ref)
        width = first_ref.shape[1]
        delta_twice = jnp.concatenate([delta_ref[...], delta_ref[...]], axis=0)

        def chunk(at):
            first = first_ref[at, :]
            query = nn(first, w_query_ref[...])
            query_ref[at, :] = query
            parts = feature_parts(softplus(query))
            match = None
            for index, part in enumerate(parts):
                term = nt(low(part), phi_keys_ref[:, index * width : (index + 1) * width])
                match = term if match is None else match + term
            match_ref[at, :] = match
            numerator = nn(jnp.concatenate(split(match), axis=1), delta_twice)
            below = 1.0 + jnp.sum(match * beta_ref[...], axis=1, keepdims=True)
            states = first.astype(f32) + numerator / below
            states_ref[at, :] = states
            unit, _ = normal_form(states)
            normed_ref[at, :] = low(unit * gains_ref[0:1, :].astype(f32))

        over_rows(first_ref.shape[0], chunk)

    qkv_ref[0] = low(nn(normed_ref[...], w_ref[...]))


def enter_segment(slot, tokens, mem_tokens, gains, w_qkv, w_mem, written):
    slots, seg_rows, width = tokens.shape
    mems = mem_tokens.shape[0]
    rows = seg_rows + mems
    parts = w_qkv.shape[1] // width
    in_specs = [
        pl.BlockSpec((None, seg_rows, width), lambda j: (slot, 0, 0), pipeline_mode=pl.Buffered(1)),
        whole((mems, width)),
        whole(gains.shape),
        pl.BlockSpec((width, width), lambda j: (0, j)),
    ]
    out_shape = [shaped((rows, width), low_type), shaped((parts, rows, width), low_type)]
    out_specs = [
        result((rows, width)),
        pl.BlockSpec((1, rows, width), lambda j: (j, 0, 0)),
    ]
    args = [tokens, mem_tokens, gains, w_qkv]
    body = enter_kernel
    macs = rows * width * width * parts
    if written is not None:
        body = enter_read_kernel
        args += [w_mem, written["phi_keys_low"], written["delta_low"], written["beta_row"]]
        in_specs += [whole((width, width))] + [whole(a.shape) for a in args[5:]]
        out_shape += [
            shaped((rows, width), f32),
            shaped((rows, width), f32),
            shaped((rows, mems), f32),
        ]
        out_specs += [result((rows, width)), result((rows, width)), result((rows, mems))]
        macs += rows * width * width
    return pl.pallas_call(
        body,
        grid=(parts,),
        in_specs=in_specs,
        out_specs=out_specs,
        out_shape=out_shape,
        scratch_shapes=[pltpu.VMEM((rows, width), low_type)],
        compiler_params=params(24),
        cost_estimate=pl.CostEstimate(
            flops=2 * macs, bytes_accessed=20 * 2**20, transcendentals=0
        ),
        name="enter_read" if written is not None else "enter",
    )(*args)


def query_blocks(rows, seg_rows):
    step = 256 if seg_rows % 256 == 0 else seg_rows
    blocks = [(at, step) for at in range(0, seg_rows, step)]
    return blocks + [(seg_rows, rows - seg_rows)]


def packed_lanes(rows, seg_rows):
    places = []
    at = 0
    for _, count in query_blocks(rows, seg_rows):
        places.append(at)
        at += -(-2 * count // 128) * 128
    return places, at


def stack_heads(block):
    lanes = lax.broadcasted_iota(jnp.int32, block.shape, 1)
    zero = jnp.zeros_like(block)
    return jnp.concatenate(
        [jnp.where(lanes < HD, block, zero), jnp.where(lanes < HD, zero, block)], axis=0
    )


def merge_heads(stacked):
    count = stacked.shape[0] // 2
    lanes = lax.broadcasted_iota(jnp.int32, (count, stacked.shape[1]), 1)
    return jnp.where(lanes < HD, stacked[:count], stacked[count:])


def as_row(column):
    count = column.shape[0]
    return jnp.transpose(jnp.broadcast_to(column, (count, 128)))[0:1, :]


def attend_kernel(
    seg_rows, qkv_ref, attended_ref, log_ref, lanes=slice(None), pair=0
):
    rows = qkv_ref.shape[1]
    places, _ = packed_lanes(rows, seg_rows)
    for (start, count), place in zip(query_blocks(rows, seg_rows), places):
        reach = start + count
        queries = stack_heads(qkv_ref[0, start:reach, lanes] * score_scale)
        raw = nt(queries, qkv_ref[1, :reach, lanes])
        place_of = lax.broadcasted_iota(jnp.int32, (2 * count, count), 0)
        place_of = jnp.where(place_of < count, place_of, place_of - count)
        allowed = place_of >= lax.broadcasted_iota(jnp.int32, (2 * count, count), 1)
        edge = jnp.where(allowed, raw[:, start:], -1e30)
        masked = jnp.concatenate([raw[:, :start], edge], axis=1) if start else edge
        peak = jnp.max(masked, axis=1, keepdims=True)
        grown = jnp.exp(masked - peak)
        total = jnp.sum(grown, axis=1, keepdims=True)
        probs = low(grown * (1.0 / total))
        mixed = merge_heads(nn(probs, qkv_ref[2, :reach, lanes]))
        attended_ref[start:reach, lanes] = low(mixed)
        log_row = as_row(peak + jnp.log(total))
        log_ref[pair, 0:1, place : place + 2 * count] = log_row


def attend(qkv, seg_rows):
    parts, rows, width = qkv.shape
    _, lanes = packed_lanes(rows, seg_rows)
    pairs = width // PAIR
    return pl.pallas_call(
        functools.partial(attend_kernel, seg_rows),
        grid=(pairs,),
        in_specs=[pl.BlockSpec((parts, rows, PAIR), lambda h: (0, 0, h))],
        out_specs=[
            pl.BlockSpec((rows, PAIR), lambda h: (0, h)),
            pl.BlockSpec((1, 1, lanes), lambda h: (h, 0, 0)),
        ],
        out_shape=[shaped((rows, width), low_type), shaped((pairs, 1, lanes), f32)],
        compiler_params=params(10),
        cost_estimate=pl.CostEstimate(
            flops=4 * rows * rows * width, bytes_accessed=7 * 2**20, transcendentals=0
        ),
        name="attend",
    )(qkv)


def attend_back_kernel(
    seg_rows,
    qkv_ref,
    grad_ref,
    attended_ref,
    log_ref,
    out_ref,
    keys_sum,
    values_sum,
    lanes=slice(None),
):
    rows = qkv_ref.shape[1]
    places, _ = packed_lanes(rows, seg_rows)
    ones = jnp.ones((8, PAIR), f32)
    blocks = list(zip(query_blocks(rows, seg_rows), places))
    for order, ((start, count), place) in enumerate(reversed(blocks)):
        reach = start + count
        queries = stack_heads(qkv_ref[0, start:reach, :] * score_scale)
        grads = stack_heads(grad_ref[start:reach, :])
        mixed = attended_ref[start:reach, :].astype(f32)
        both = jnp.concatenate([mixed, mixed], axis=0) * grads.astype(f32)
        inner = lax.dot_general(
            ones,
            both,
            (((1,), (1,)), ((), ())),
            precision=lax.Precision.HIGHEST,
            preferred_element_type=f32,
        )[0:1, :]
        keys = qkv_ref[1, :reach, :]
        raw = nt(keys, queries)
        log_row = log_ref[0, 0:1, place : place + 2 * count]
        probs = jnp.exp(raw - log_row)
        place_of = lax.broadcasted_iota(jnp.int32, (count, 2 * count), 1)
        place_of = jnp.where(place_of < count, place_of, place_of - count)
        allowed = place_of >= lax.broadcasted_iota(jnp.int32, (count, 2 * count), 0)
        edge = jnp.where(allowed, probs[start:], 0.0)
        probs = jnp.concatenate([probs[:start], edge], axis=0) if start else edge
        grad_probs = nt(qkv_ref[2, :reach, :], grads)
        grad_raw = low(probs * (grad_probs - inner))
        value_part = nn(low(probs), grads)
        key_part = nn(grad_raw, queries)
        if order == 0:
            values_sum[...] = value_part
            keys_sum[...] = key_part
        else:
            values_sum[:reach, :] += value_part
            keys_sum[:reach, :] += key_part
        out_ref[0, start:reach, lanes] = low(merge_heads(tn(grad_raw, keys)) * score_scale)
    out_ref[1, :, lanes] = low(keys_sum[...])
    out_ref[2, :, lanes] = low(values_sum[...])


def attend_back(qkv, grad_attended, attended, logs, seg_rows):
    parts, rows, width = qkv.shape
    pairs = width // PAIR
    column = pl.BlockSpec((rows, PAIR), lambda h: (0, h))
    three = pl.BlockSpec((parts, rows, PAIR), lambda h: (0, 0, h))
    return pl.pallas_call(
        functools.partial(attend_back_kernel, seg_rows),
        grid=(pairs,),
        in_specs=[
            three,
            column,
            column,
            pl.BlockSpec((1,) + logs.shape[1:], lambda h: (h, 0, 0)),
        ],
        out_specs=three,
        out_shape=shaped((parts, rows, width), low_type),
        scratch_shapes=[pltpu.VMEM((rows, PAIR), f32), pltpu.VMEM((rows, PAIR), f32)],
        compiler_params=params(12),
        cost_estimate=pl.CostEstimate(
            flops=10 * rows * rows * width, bytes_accessed=13 * 2**20, transcendentals=0
        ),
        name="attend_back",
    )(qkv, grad_attended, attended, logs)


def leave_kernel(
    reads, earlier, *refs
):
    if reads:
        (states_one_ref, *refs) = refs
    else:
        (tokens_ref, mem_ref, *refs) = refs
    (attended_ref, gains_ref, w_out_ref, w_up_ref, w_down_ref, *refs) = refs
    if earlier:
        refs = refs[1:]
    (out_ref, mem_out_ref, states_two_ref, normed_ref, upward_ref, sum_ref, *scratch) = refs
    rows, width = attended_ref.shape
    seg_rows = out_ref.shape[0]
    step = pl.program_id(0)

    @pl.when(step == 0)
    def _():
        if not reads:
            load_first(tokens_ref, mem_ref, scratch[0])

        def chunk(at):
            source = states_one_ref if reads else scratch[0]
            states = source[at, :].astype(f32) + nn(attended_ref[at, :], w_out_ref[...])
            states_two_ref[at, :] = states
            unit, _ = normal_form(states)
            normed_ref[at, :] = low(unit * gains_ref[1:2, :].astype(f32))
            sum_ref[at, :] = states

        over_rows(rows, chunk)

    def chunk(at):
        upward = nn(normed_ref[at, :], w_up_ref[...])
        upward_ref[at, :] = upward
        bent = jnp.tanh(upward * (gelu_c + gelu_c * gelu_a * (upward * upward)))
        active = low(upward * (0.5 + 0.5 * bent))
        sum_ref[at, :] += nn(active, w_down_ref[...])

    chunk(pl.ds(0, rows))

    @pl.when(step == pl.num_programs(0) - 1)
    def _():
        out_ref[...] = low(sum_ref[:seg_rows, :])
        mem_out_ref[...] = sum_ref[seg_rows:, :]


def leave_segment(slot, slots, seg_rows, start, attended, gains, w_out, w_up, w_down, earlier):
    rows, width = attended.shape
    hidden = w_up.shape[1]
    size = 512 if hidden % 512 == 0 else hidden
    reads = not isinstance(start, tuple)
    args = []
    in_specs = []
    scratch = [pltpu.VMEM((rows, width), f32)]
    if reads:
        args.append(start)
        in_specs.append(whole((rows, width)))
    else:
        tokens, mem_tokens = start
        args += [tokens, mem_tokens]
        in_specs += [
            pl.BlockSpec((None, seg_rows, width), lambda j: (slot, 0, 0), pipeline_mode=pl.Buffered(1)),
            whole(mem_tokens.shape),
        ]
        scratch.append(pltpu.VMEM((rows, width), low_type))
    args += [attended, gains, w_out, w_up, w_down]
    in_specs += [
        whole((rows, width)),
        whole(gains.shape),
        whole((width, width)),
        pl.BlockSpec((width, size), lambda j: (0, j)),
        pl.BlockSpec((size, width), lambda j: (j, 0)),
    ]
    aliases = {}
    if earlier is not None:
        aliases = {len(args): 0}
        args.append(earlier)
        in_specs.append(pl.BlockSpec(memory_space=pl.ANY))
    return pl.pallas_call(
        functools.partial(leave_kernel, reads, earlier is not None),
        grid=(hidden // size,),
        in_specs=in_specs,
        out_specs=[
            pl.BlockSpec((None, seg_rows, width), lambda j: (slot, 0, 0)),
            result((rows - seg_rows, width)),
            result((rows, width)),
            result((rows, width)),
            pl.BlockSpec((rows, size), lambda j: (0, j)),
        ],
        out_shape=[
            shaped((slots, seg_rows, width), low_type),
            shaped((rows - seg_rows, width), f32),
            shaped((rows, width), f32),
            shaped((rows, width), low_type),
            shaped((rows, hidden), f32),
        ],
        scratch_shapes=scratch,
        input_output_aliases=aliases,
        compiler_params=params(40),
        cost_estimate=pl.CostEstimate(
            flops=2 * rows * width * (width + 2 * hidden), bytes_accessed=36 * 2**20, transcendentals=0
        ),
        name="leave",
    )(*args)


def beta_parts(mem_out, w_beta):
    column = jnp.sum(mem_out * w_beta, axis=1, keepdims=True)
    row = lax.dot_general(
        w_beta,
        mem_out,
        (((1,), (1,)), ((), ())),
        precision=lax.Precision.HIGHEST,
        preferred_element_type=f32,
    )
    return jax.nn.sigmoid(column), jax.nn.sigmoid(row)


def write_kernel(
    slot,
    flag_ref,
    mem_out_ref,
    w_key_ref,
    w_value_ref,
    w_beta_ref,
    key_ref,
    value_ref,
    phi_ref,
    phi_rest_ref,
    delta_ref,
    beta_row_ref,
):
    flag = jnp.where(flag_ref[slot + 1] == flag_ref[slot], 1.0, 0.0).astype(f32)
    width = key_ref.shape[1]
    mem_out = mem_out_ref[...]
    mem_low = low(mem_out)
    key = nn(mem_low, w_key_ref[...])
    value = nn(mem_low, w_value_ref[...])
    key_ref[...] = key
    value_ref[...] = value
    for index, part in enumerate(feature_parts(softplus(key))):
        high, rest = split(part)
        phi_ref[:, index * width : (index + 1) * width] = high
        phi_rest_ref[:, index * width : (index + 1) * width] = rest
    beta, beta_row = beta_parts(mem_out, w_beta_ref[...].astype(f32))
    delta_ref[...] = low(low(beta * value).astype(f32) * flag)
    beta_row_ref[...] = beta_row * flag


def write_memory(slot, flag, mem_out, w_mem, w_beta):
    mems, width = mem_out.shape
    names = ("key", "value", "phi_keys_low", "phi_keys_rest", "delta_low", "beta_row")
    out_shape = [
        shaped((mems, width), f32),
        shaped((mems, width), f32),
        shaped((mems, 3 * width), low_type),
        shaped((mems, 3 * width), low_type),
        shaped((mems, width), low_type),
        shaped((1, mems), f32),
    ]
    outs = pl.pallas_call(
        functools.partial(write_kernel, slot),
        grid=(1,),
        in_specs=[
            pl.BlockSpec(memory_space=pltpu.SMEM),
            whole((mems, width)),
            pl.BlockSpec((width, width), lambda j: (0, 1)),
            pl.BlockSpec((width, width), lambda j: (0, 2)),
            whole((1, width)),
        ],
        out_specs=[result(s.shape) for s in out_shape],
        out_shape=out_shape,
        compiler_params=params(10),
        name="write",
    )(flag, mem_out, w_mem, w_mem, w_beta)
    return dict(zip(names, outs))


def write_back_kernel(
    slot,
    flag_ref,
    mem_out_ref,
    w_key_ref,
    w_value_ref,
    w_beta_ref,
    key_ref,
    value_ref,
    grad_delta_ref,
    grad_phi_ref,
    grad_normal_ref,
    grad_rows_ref,
    grad_w_ref,
    grad_beta_ref,
):
    flag = jnp.where(flag_ref[slot + 1] == flag_ref[slot], 1.0, 0.0).astype(f32)
    width = key_ref.shape[1]
    mem_out = mem_out_ref[...]
    mem_low = low(mem_out)
    w_beta = w_beta_ref[...].astype(f32)
    key = key_ref[...]
    value = value_ref[...]
    beta, _ = beta_parts(mem_out, w_beta)
    softer = softplus(key)
    parts = feature_parts(softer)
    grad_delta = grad_delta_ref[...] * flag
    grad_strength = jnp.sum(grad_delta * value, axis=1, keepdims=True)
    grads = []
    for index, part in enumerate(parts):
        at = slice(index * width, (index + 1) * width)
        grad_normal = grad_normal_ref[:, at] * flag
        grad_strength += jnp.sum(part * grad_normal, axis=1, keepdims=True)
        grads.append(grad_phi_ref[:, at] * flag + beta * grad_normal)
    grad_key = low(feature_back(grads, softer, key))
    grad_value = low(beta * grad_delta)
    grad_logit = grad_strength * beta * (1.0 - beta)
    grad_rows_ref[...] = (
        grad_logit * w_beta + nt(grad_key, w_key_ref[...]) + nt(grad_value, w_value_ref[...])
    )
    grad_beta_ref[...] = jnp.sum(grad_logit * mem_out, axis=0, keepdims=True)
    grad_w_ref[:, :width] = low(tn(mem_low, grad_key))
    grad_w_ref[:, width:] = low(tn(mem_low, grad_value))


def write_back(slot, flag, mem_out, w_mem, w_beta, written, grad_delta, grad_phi, grad_normal):
    mems, width = mem_out.shape
    args = [flag, mem_out, w_mem, w_mem, w_beta, written["key"], written["value"]]
    args += [grad_delta, grad_phi, grad_normal]
    out_shape = [
        shaped((mems, width), f32),
        shaped((width, 2 * width), low_type),
        shaped((1, width), f32),
    ]
    return pl.pallas_call(
        functools.partial(write_back_kernel, slot),
        grid=(1,),
        in_specs=[
            pl.BlockSpec(memory_space=pltpu.SMEM),
            whole((mems, width)),
            pl.BlockSpec((width, width), lambda j: (0, 1)),
            pl.BlockSpec((width, width), lambda j: (0, 2)),
        ]
        + [whole(a.shape) for a in args[4:]],
        out_specs=[result(s.shape) for s in out_shape],
        out_shape=out_shape,
        compiler_params=params(12),
        name="write_back",
    )(*args)


def leave_back_kernel(writes, adds, *refs):
    (out_grad_ref, *refs) = refs
    if writes:
        (grad_rows_ref, *refs) = refs
    (
        states_two_ref,
        normed_ref,
        upward_ref,
        attended_ref,
        gains_ref,
        w_out_ref,
        w_up_ref,
        w_down_ref,
        *refs,
    ) = refs
    if adds:
        (up_in_ref, down_in_ref, out_in_ref, *refs) = refs
    (
        grad_states_ref,
        grad_attended_ref,
        grad_up_ref,
        grad_down_ref,
        grad_out_ref,
        grad_gain_ref,
        grad_low_ref,
        sum_ref,
        grad_two_ref,
    ) = refs
    rows, width = normed_ref.shape
    seg_rows = out_grad_ref.shape[0]
    step = pl.program_id(0)

    @pl.when(step == 0)
    def _():
        grad_low_ref[:seg_rows, :] = out_grad_ref[...]
        grad_states_ref[:seg_rows, :] = out_grad_ref[...].astype(f32)
        if writes:
            grad_low_ref[seg_rows:, :] = low(grad_rows_ref[...])
            grad_states_ref[seg_rows:, :] = grad_rows_ref[...]
        else:
            grad_low_ref[seg_rows:, :] = jnp.zeros((rows - seg_rows, width), low_type)
            grad_states_ref[seg_rows:, :] = jnp.zeros((rows - seg_rows, width), f32)
        sum_ref[...] = jnp.zeros_like(sum_ref)

    upward = upward_ref[...]
    square = upward * upward
    bent = jnp.tanh(upward * (gelu_c + gelu_c * gelu_a * square))
    half = 0.5 + 0.5 * bent
    active = upward * half
    slope = half + (active - active * half) * (2.0 * gelu_c + 6.0 * gelu_c * gelu_a * square)
    grad_low = grad_low_ref[...]
    grad_upward = low(nt(grad_low, w_down_ref[...]) * slope)
    grad_down = tn(low(active), grad_low)
    grad_up = tn(normed_ref[...], grad_upward)
    sum_ref[...] += nt(grad_upward, w_up_ref[...])
    if adds:
        grad_down += down_in_ref[...]
        grad_up += up_in_ref[...]
    grad_down_ref[...] = grad_down.astype(grad_down_ref.dtype)
    grad_up_ref[...] = grad_up.astype(grad_up_ref.dtype)

    @pl.when(step == pl.num_programs(0) - 1)
    def _():
        gain = gains_ref[1:2, :].astype(f32)
        grad_gain_ref[...] = jnp.zeros_like(grad_gain_ref)

        def chunk(at):
            unit, inverse = normal_form(states_two_ref[at, :])
            grad = sum_ref[at, :]
            grad_gain_ref[...] += jnp.sum(grad * unit, axis=0, keepdims=True)
            total = grad_states_ref[at, :] + norm_back(grad, unit, inverse, gain)
            grad_states_ref[at, :] = total
            total_low = low(total)
            grad_two_ref[at, :] = total_low
            grad_attended_ref[at, :] = low(nt(total_low, w_out_ref[...]))

        over_rows(rows, chunk)
        grad_out = tn(attended_ref[...], grad_two_ref[...])
        if adds:
            grad_out += out_in_ref[...]
        grad_out_ref[...] = grad_out.astype(grad_out_ref.dtype)


def leave_back(slot, out_grad, grad_rows, kept, gains, w_out, w_up, w_down, sums, grad_type, moved=None):
    _, seg_rows, width = out_grad.shape
    rows = kept["normed_two"].shape[0]
    hidden = w_up.shape[1]
    size = 512 if hidden % 512 == 0 else hidden
    up_spec = pl.BlockSpec((width, size), lambda j: (0, j))
    down_spec = pl.BlockSpec((size, width), lambda j: (j, 0))
    args = [out_grad]
    in_specs = [
        pl.BlockSpec((None, seg_rows, width), lambda j: (slot, 0, 0), pipeline_mode=pl.Buffered(1))
    ]
    if grad_rows is not None:
        args.append(grad_rows)
        in_specs.append(whole(grad_rows.shape))
    args += [kept["states_two"], kept["normed_two"], kept["upward"], kept["attended"]]
    args += [gains, w_out, w_up, w_down]
    in_specs += [
        whole((rows, width)),
        whole((rows, width)),
        pl.BlockSpec((rows, size), lambda j: (0, j)),
        whole((rows, width)),
        whole(gains.shape),
        whole((width, width)),
        up_spec,
        down_spec,
    ]
    if sums is not None:
        args += [sums["up"], sums["down"], sums["out"]]
        in_specs += [up_spec, down_spec, whole((width, width))]
    body = functools.partial(leave_back_kernel, grad_rows is not None, sums is not None)
    out_specs = [
        result((rows, width)),
        result((rows, width)),
        up_spec,
        down_spec,
        result((width, width)),
        result((1, width)),
    ]
    out_shape = [
        shaped((rows, width), f32),
        shaped((rows, width), low_type),
        shaped((width, hidden), grad_type),
        shaped((hidden, width), grad_type),
        shaped((width, width), grad_type),
        shaped((1, width), f32),
    ]
    scratch = [
        pltpu.VMEM((rows, width), low_type),
        pltpu.VMEM((rows, width), f32),
        pltpu.VMEM((rows, width), low_type),
    ]
    extra = {}
    if moved is not None:
        shapes = [m.shape[-2:] for m in moved]
        groups = []
        before = 0
        for a, (_, cols) in enumerate(shapes):
            for at in range(0, cols, width):
                groups.append((a, at, width, 0, before + at, cut(width, (1, 1)), False))
            before += cols
        plan = Reduce(groups, shapes, event_order(len(groups), 2))
        grid = hidden // size
        schedule = spread(plan.order, {1: (0, 1), 2: (1, 0), 3: (1, 1), 4: (1, 2), 5: (2, 2), grid: (3, 2)})
        counts = (len(args), len(moved), len(out_shape), 1, len(scratch))
        body = functools.partial(carry_kernel, body, plan, counts, schedule, grid)
        args += moved
        in_specs += [ANYWHERE] * len(moved)
        total = (width // DEVICES, before)
        out_specs.append(result(total))
        out_shape.append(shaped(total, f32))
        scratch += plan.scratch()
        extra = dict(collective_id=1, has_side_effects=True)
    return pl.pallas_call(
        body,
        grid=(hidden // size,),
        in_specs=in_specs,
        out_specs=out_specs,
        out_shape=out_shape,
        scratch_shapes=scratch,
        compiler_params=params(**extra),
        cost_estimate=pl.CostEstimate(
            flops=4 * rows * width * (width + 2 * hidden), bytes_accessed=60 * 2**20, transcendentals=0
        ),
        name="leave_back",
    )(*args)


def leave_both_kernel(reads, adds, *refs):
    if reads:
        (states_one_ref, *refs) = refs
    else:
        (tokens_ref, mem_ref, *refs) = refs
    (attended_ref, out_grad_ref, gains_ref, w_out_ref, w_up_ref, w_down_ref, *refs) = refs
    if adds:
        refs = refs[1:]
    (
        out_ref,
        grad_states_ref,
        grad_attended_ref,
        grad_up_ref,
        grad_down_ref,
        grad_out_ref,
        grad_gain_ref,
        states_two_ref,
        normed_ref,
        forward_ref,
        backward_ref,
        grad_low_ref,
        *scratch,
    ) = refs
    rows, width = attended_ref.shape
    seg_rows = out_grad_ref.shape[0]
    step = pl.program_id(0)

    @pl.when(step == 0)
    def _():
        if not reads:
            load_first(tokens_ref, mem_ref, scratch[0])
        grad_low_ref[:seg_rows, :] = out_grad_ref[...]
        grad_low_ref[seg_rows:, :] = jnp.zeros((rows - seg_rows, width), low_type)

        def chunk(at):
            source = states_one_ref if reads else scratch[0]
            states = source[at, :].astype(f32) + nn(attended_ref[at, :], w_out_ref[...])
            states_two_ref[at, :] = states
            unit, _ = normal_form(states)
            normed_ref[at, :] = low(unit * gains_ref[1:2, :].astype(f32))
            forward_ref[at, :] = states
            backward_ref[at, :] = jnp.zeros_like(states)

        over_rows(rows, chunk)

    normed = normed_ref[...]
    grad_low = grad_low_ref[...]
    upward = nn(normed, w_up_ref[...])
    grad_active = nt(grad_low, w_down_ref[...])
    active, slope = gelu_parts(upward)
    active = low(active)
    grad_upward = low(grad_active * slope)
    forward_ref[...] += nn(active, w_down_ref[...])
    backward_ref[...] += nt(grad_upward, w_up_ref[...])
    grad_down = tn(active, grad_low)
    grad_up = tn(normed, grad_upward)
    grad_down_ref[...] = grad_down.astype(grad_down_ref.dtype)
    grad_up_ref[...] = grad_up.astype(grad_up_ref.dtype)

    @pl.when(step == pl.num_programs(0) - 1)
    def _():
        gain = gains_ref[1:2, :].astype(f32)
        grad_gain_ref[...] = jnp.zeros_like(grad_gain_ref)

        def chunk(at):
            unit, inverse = normal_form(states_two_ref[at, :])
            grad = backward_ref[at, :]
            grad_gain_ref[...] += jnp.sum(grad * unit, axis=0, keepdims=True)
            total = grad_low_ref[at, :].astype(f32) + norm_back(grad, unit, inverse, gain)
            grad_states_ref[at, :] = total
            total_low = low(total)
            normed_ref[at, :] = total_low
            grad_attended_ref[at, :] = low(nt(total_low, w_out_ref[...]))

        over_rows(rows, chunk)
        grad_out = tn(attended_ref[...], normed_ref[...])
        grad_out_ref[...] = grad_out.astype(grad_out_ref.dtype)
        out_ref[...] = low(forward_ref[:seg_rows, :])


def gelu_parts(upward):
    square = upward * upward
    bent = jnp.tanh(upward * (gelu_c + gelu_c * gelu_a * square))
    half = 0.5 + 0.5 * bent
    active = upward * half
    slope = half + (active - active * half) * (2.0 * gelu_c + 6.0 * gelu_c * gelu_a * square)
    return active, slope


def leave_both(slot, start, attended, out_grad, gains, w_out, w_up, w_down, earlier, grad_type):
    slots, seg_rows, width = out_grad.shape
    rows = attended.shape[0]
    mems = rows - seg_rows
    hidden = w_up.shape[1]
    size = 512 if hidden % 512 == 0 else hidden
    reads = not isinstance(start, tuple)
    args = []
    in_specs = []
    scratch = [
        pltpu.VMEM((rows, width), f32),
        pltpu.VMEM((rows, width), low_type),
        pltpu.VMEM((rows, width), f32),
        pltpu.VMEM((rows, width), f32),
        pltpu.VMEM((rows, width), low_type),
    ]
    segment = pl.BlockSpec((None, seg_rows, width), lambda j: (slot, 0, 0), pipeline_mode=pl.Buffered(1))
    if reads:
        args.append(start)
        in_specs.append(whole((rows, width)))
    else:
        args += list(start)
        in_specs += [segment, whole((mems, width))]
        scratch.append(pltpu.VMEM((rows, width), low_type))
    up_spec = pl.BlockSpec((width, size), lambda j: (0, j))
    down_spec = pl.BlockSpec((size, width), lambda j: (j, 0))
    args += [attended, out_grad, gains, w_out, w_up, w_down]
    in_specs += [
        whole((rows, width)),
        segment,
        whole(gains.shape),
        whole((width, width)),
        up_spec,
        down_spec,
    ]
    aliases = {}
    if earlier is not None:
        args.append(earlier)
        in_specs.append(ANYWHERE)
        aliases = {len(args) - 1: 0}
    outs = pl.pallas_call(
        functools.partial(leave_both_kernel, reads, earlier is not None),
        grid=(hidden // size,),
        in_specs=in_specs,
        out_specs=[
            segment,
            whole((rows, width)),
            whole((rows, width)),
            up_spec,
            down_spec,
            whole((width, width)),
            whole((1, width)),
        ],
        out_shape=[
            shaped((slots, seg_rows, width), low_type),
            shaped((rows, width), f32),
            shaped((rows, width), low_type),
            shaped((width, hidden), grad_type),
            shaped((hidden, width), grad_type),
            shaped((width, width), grad_type),
            shaped((1, width), f32),
        ],
        scratch_shapes=scratch,
        input_output_aliases=aliases,
        compiler_params=params(50),
        cost_estimate=pl.CostEstimate(
            flops=6 * rows * width * (width + 2 * hidden), bytes_accessed=60 * 2**20, transcendentals=0
        ),
        name="leave_both",
    )(*args)
    names = ("block_out", "grad_states", "grad_attended", "up", "down", "out", "gain_two")
    return dict(zip(names, outs))


def enter_back_kernel(reads, adds, earlier, *refs):
    (tokens_ref, mem_ref, normed_ref, grad_qkv_ref, grad_states_ref, gains_ref, w_ref, *refs) = refs
    if reads:
        (
            states_ref,
            query_ref,
            match_ref,
            w_query_ref,
            phi_keys_ref,
            phi_rest_ref,
            delta_ref,
            beta_ref,
            *refs,
        ) = refs
    if adds:
        (w_in_ref, *refs) = refs
    if earlier:
        refs = refs[1:]
    (grad_tokens_ref, grad_mem_ref, grad_w_ref, grad_gain_ref, *refs) = refs
    if reads:
        (grad_w_query_ref, grad_delta_ref, grad_phi_ref, grad_normal_ref, *refs) = refs
    (first_ref, sum_ref, *refs) = refs
    rows, width = normed_ref.shape
    seg_rows = tokens_ref.shape[0]
    step = pl.program_id(0)

    @pl.when(step == 0)
    def _():
        load_first(tokens_ref, mem_ref, first_ref)
        sum_ref[...] = jnp.zeros_like(sum_ref)

    grad_part = grad_qkv_ref[0]
    sum_ref[...] += nt(grad_part, w_ref[...])
    grad_w = tn(normed_ref[...], grad_part)
    if adds:
        grad_w += w_in_ref[...]
    grad_w_ref[...] = grad_w.astype(grad_w_ref.dtype)

    @pl.when(step == pl.num_programs(0) - 1)
    def _():
        gain = gains_ref[0:1, :].astype(f32)
        grad_gain_ref[...] = jnp.zeros_like(grad_gain_ref)
        if reads:
            (grad_query_ref, packed_sum_ref, delta_sum_ref) = refs
            packed_sum_ref[...] = jnp.zeros_like(packed_sum_ref)
            delta_sum_ref[...] = jnp.zeros_like(delta_sum_ref)
            mems = delta_ref.shape[0]
            beta = beta_ref[...]
            basis = jnp.concatenate([phi_keys_ref[...], phi_keys_ref[...], phi_rest_ref[...]], axis=0)

        def chunk(at):
            first = first_ref[at, :].astype(f32)
            states = states_ref[at, :] if reads else first
            unit, inverse = normal_form(states)
            grad = sum_ref[at, :]
            grad_gain_ref[...] += jnp.sum(grad * unit, axis=0, keepdims=True)
            total = grad_states_ref[at, :] + norm_back(grad, unit, inverse, gain)
            if reads:
                match = match_ref[at, :]
                below = 1.0 + jnp.sum(match * beta, axis=1, keepdims=True)
                grad_num = low(total / below)
                grad_below = -jnp.sum(total * (states - first), axis=1, keepdims=True) / below
                pulled = nt(grad_num, delta_ref[...])
                spread_below = grad_below * beta
                both_high, both_low = split(pulled + spread_below)
                weights = jnp.concatenate([both_high, both_low, low(spread_below)], axis=1)
                query = query_ref[at, :]
                softer = softplus(query)
                parts = feature_parts(softer)
                grads = []
                packed = jnp.concatenate(
                    list(split(pulled))
                    + [low(jnp.broadcast_to(part, pulled.shape)) for part in (grad_below,)]
                    + [
                        low(
                            jnp.broadcast_to(
                                grad_below - low(grad_below).astype(f32), pulled.shape
                            )
                        )
                    ],
                    axis=1,
                )
                for index, part in enumerate(parts):
                    cols = slice(index * width, (index + 1) * width)
                    grads.append(nn(weights, basis[:, cols]))
                    packed_sum_ref[:, cols] += tn(packed, low(part))
                delta_sum_ref[...] += tn(jnp.concatenate(split(match), axis=1), grad_num)
                grad_query = low(feature_back(grads, softer, query))
                grad_query_ref[at, :] = grad_query
                total += nt(grad_query, w_query_ref[...])
            sum_ref[at, :] = total

        over_rows(rows, chunk, False)
        grad_tokens_ref[...] = sum_ref[:seg_rows, :]
        grad_mem_ref[...] = sum_ref[seg_rows:, :]
        if reads:
            grad_w_query_ref[...] = low(tn(first_ref[...], grad_query_ref[...]))
            grad_delta_ref[...] = delta_sum_ref[:mems, :] + delta_sum_ref[mems:, :]
            grad_phi_ref[...] = packed_sum_ref[:mems, :] + packed_sum_ref[mems : 2 * mems, :]
            grad_normal_ref[...] = (
                packed_sum_ref[2 * mems : 2 * mems + 1, :]
                + packed_sum_ref[3 * mems : 3 * mems + 1, :]
            )


def enter_back(
    slot, tokens, mem_tokens, kept, grad_qkv, grad_states, gains, w_qkv, w_mem, written, w_sum, earlier, grad_type
):
    slots, seg_rows, width = tokens.shape
    mems = mem_tokens.shape[0]
    rows = seg_rows + mems
    parts = grad_qkv.shape[0]
    reads = written is not None
    args = [tokens, mem_tokens, kept["normed_one"], grad_qkv, grad_states, gains, w_qkv]
    in_specs = [
        pl.BlockSpec((None, seg_rows, width), lambda j: (slot, 0, 0), pipeline_mode=pl.Buffered(1)),
        whole((mems, width)),
        whole((rows, width)),
        pl.BlockSpec((1, rows, width), lambda j: (j, 0, 0)),
        whole((rows, width)),
        whole(gains.shape),
        pl.BlockSpec((width, width), lambda j: (0, j)),
    ]
    scratch = [pltpu.VMEM((rows, width), low_type), pltpu.VMEM((rows, width), f32)]
    if reads:
        more = [written["phi_keys_low"], written["phi_keys_rest"]]
        more += [written["delta_low"], written["beta_row"]]
        args += [kept["states_one"], kept["query"], kept["match"], w_mem] + more
        in_specs += [whole((rows, width)), whole((rows, width)), whole((rows, mems)), whole((width, width))]
        in_specs += [whole(a.shape) for a in more]
        scratch += [
            pltpu.VMEM((rows, width), low_type),
            pltpu.VMEM((4 * mems, 3 * width), f32),
            pltpu.VMEM((2 * mems, width), f32),
        ]
    if w_sum is not None:
        args.append(w_sum)
        in_specs.append(pl.BlockSpec((width, width), lambda j: (0, j)))
    aliases = {}
    if earlier is not None:
        aliases = {len(args): 0}
        args.append(earlier)
        in_specs.append(pl.BlockSpec(memory_space=pl.ANY))
    out_specs = [
        pl.BlockSpec((None, seg_rows, width), lambda j: (slot, 0, 0)),
        result((mems, width)),
        pl.BlockSpec((width, width), lambda j: (0, j)),
        result((1, width)),
    ]
    out_shape = [
        shaped((slots, seg_rows, width), f32),
        shaped((mems, width), f32),
        shaped((width, parts * width), grad_type),
        shaped((1, width), f32),
    ]
    if reads:
        extra = [
            shaped((width, width), low_type),
            shaped((mems, width), f32),
            shaped((mems, 3 * width), f32),
            shaped((1, 3 * width), f32),
        ]
        out_shape += extra
        out_specs += [result(s.shape) for s in extra]
    return pl.pallas_call(
        functools.partial(enter_back_kernel, reads, w_sum is not None, earlier is not None),
        grid=(parts,),
        in_specs=in_specs,
        out_specs=out_specs,
        out_shape=out_shape,
        scratch_shapes=scratch,
        input_output_aliases=aliases,
        compiler_params=params(36),
        cost_estimate=pl.CostEstimate(
            flops=4 * rows * width * width * (parts + 1), bytes_accessed=30 * 2**20, transcendentals=0
        ),
        name="enter_back",
    )(*args)


MESH = pl.DeviceIdType.MESH
DEPTH, SIDE = 4, 2


def events(*numbers):
    return [divmod(number, 10) if number >= 0 else -1 - number for number in numbers]


ARRIVE_ORDER = events(
    0, 1, 10, 11, 20, 21, 2, 3, 30, 31, 12, 4, 13, 5, 22, 14, 23, 15, 32, 24, 6, 33, 25, 7, 34,
    35, 16, 17, 26, 27, 36, 37
)
ARRIVE_STEPS = {0: (3, 1), 1: (0, 4), 2: (0, 5), 3: (1, 4), 4: (1, 5), 6: (0, 6), 8: (0, 7)}
ARRIVE_STEPS.update({9: (3, 5), 10: (1, 7), 11: (2, 7), 12: (3, 6)})
FINISH_ORDER = events(
    0, 1, 10, 2, 11, 3, 20, 12, 4, 21, 13, 5, 30, 22, 14, 31, 23, 15, 6, 32, 24, 7, 33, 25, 8,
    16, 34, 17, 35, 18, 26, 36, 27, 37, 28, 38
)
FINISH_STEPS = {1: (0, 1), 2: (0, 2), 3: (0, 3), 4: (0, 4), 5: (0, 5), 6: (1, 4)}
FINISH_STEPS.update({7: (0, 6), 8: (0, 7), 9: (0, 8), 10: (3, 4), 11: (3, 5)})
FINISH_TAIL = events(
    -1, 18, 26, -2, 36, 27, -3, 37, 28, -4, 38
)
GRID = (DEPTH, SIDE, SIDE, SIDE)
DEVICES = DEPTH * SIDE**3
ORDERS = ("zxy", "zyx", "xyz", "yxz")
sems = pltpu.SemaphoreType.DMA


def my_place():
    wide = lax.axis_index("wide")
    narrow = lax.axis_index("narrow")
    return wide // SIDE, wide % SIDE, narrow // SIDE, narrow % SIDE


def device_at(z, x, y, core):
    return (z * SIDE + x, y * SIDE + core)


def partners(z, x, y, core):
    return {
        "z": [device_at((z + step) % DEPTH, x, y, core) for step in range(1, DEPTH)],
        "x": [device_at(z, 1 - x, y, core)],
        "y": [device_at(z, x, 1 - y, core)],
        "c": [device_at(z, x, y, 1 - core)],
    }


def meet(peers):
    barrier = pltpu.get_barrier_semaphore()
    everyone = [peer for group in peers.values() for peer in group]
    for peer in everyone:
        pl.semaphore_signal(barrier, inc=1, device_id=peer, device_id_type=MESH)
    pl.semaphore_wait(barrier, len(everyone))


def remote(source, target, send, recv, peer):
    return pltpu.make_async_remote_copy(
        src_ref=source,
        dst_ref=target,
        send_sem=send,
        recv_sem=recv,
        device_id=peer,
        device_id_type=MESH,
    )


def slab(ref, place, known, at):
    z, x, y, core = place
    return ref.at[
        slice(None) if "z" in known else z,
        slice(None) if "x" in known else x,
        slice(None) if "y" in known else y,
        slice(None) if "c" in known else core,
        :,
        at,
    ]


def cut(cols, shares):
    unit = cols // 128 // sum(shares)
    pieces = []
    at = 0
    for order, share in zip(ORDERS, shares):
        if share:
            pieces.append((order, at, share * unit * 128))
            at += share * unit * 128
    return pieces


def event_order(total, lanes):
    order = []
    for now in range(-(-total // lanes) + 3):
        for lane in range(lanes):
            for index in (3, 2, 1, 0):
                group = (now - index) * lanes + lane
                if now >= index and group < total:
                    order.append((index, group))
    return order


def spread(order, last):
    schedule = {}
    done = 0
    for step, event in last.items():
        until = order.index(event) + 1
        schedule[step] = tuple(range(done, until))
        done = until
    return schedule


class Gather:
    def __init__(self, groups, order, lead):
        self.groups = groups
        self.lead = lead
        self.order = order
        self.ticks = len(self.order)
        self.numbers = {}
        for group, (_, pieces) in enumerate(groups):
            for piece in pieces:
                self.numbers[group, piece] = len(self.numbers)

    def scratch(self):
        count = len(self.numbers)
        return [sems((count,)), sems((count, 6)), sems((count, 6))]

    def bind(self, shards, fulls, scratch):
        self.shards = shards
        self.fulls = fulls
        self.own_sem, self.send_sem, self.recv_sem = scratch
        self.place = my_place()
        self.peers = partners(*self.place)

    def copies(self, index, group):
        a, pieces = self.groups[group]
        made = []
        for piece in pieces:
            order, start, size = piece
            number = self.numbers[group, piece]
            path = order + "c"
            at = pl.ds(start, size)
            target = slab(self.fulls[a], self.place, path[:index], at)
            source = self.shards[a].at[:, at] if index == 0 else target
            if index == 0:
                made.append(pltpu.make_async_copy(source, target, self.own_sem.at[number]))
            for step, peer in enumerate(self.peers[path[index]]):
                slot = index + step if path[index] == "z" else index + 2 * ("z" in path[:index])
                made.append(
                    remote(
                        source,
                        target,
                        self.send_sem.at[number, slot],
                        self.recv_sem.at[number, slot],
                        peer,
                    )
                )
        return made

    def begin(self, index, group):
        for copy in self.copies(index, group):
            copy.start()

    def enter(self):
        meet(self.peers)
        for group in range(min(self.lead, len(self.groups))):
            self.begin(0, group)

    def tick(self, now):
        index, group = self.order[now]
        for copy in self.copies(index, group):
            copy.wait()
        if index < 3:
            self.begin(index + 1, group)
        if index == 0 and group + self.lead < len(self.groups):
            self.begin(0, group + self.lead)


class Reduce:
    def __init__(self, groups, shapes, order):
        self.groups = groups
        self.shapes = shapes
        self.order = order
        self.ticks = len(self.order)
        count = 0
        self.entries = []
        for *_, pieces, _ in groups:
            self.entries.append([(count + i, piece) for i, piece in enumerate(pieces)])
            count += len(pieces)
        self.count = count

    def scratch(self):
        total = len(self.groups)
        made = [sems((total,)), sems((total,)), sems((total,)), sems((self.count, 5)), sems((self.count, 5))]
        for a, _, cols, _, _, pieces, held in self.groups:
            height = self.shapes[a][0]
            full = (DEPTH, SIDE, SIDE, height, cols)
            made.append(pltpu.VMEM(full, low_type))
            if not held:
                made.append(pltpu.VMEM(full, low_type))
            for _, _, size in pieces:
                made.append(pltpu.VMEM((DEPTH, SIDE, height, size), f32))
                made.append(pltpu.VMEM((DEPTH, SIDE, height, size), low_type))
                made.append(pltpu.VMEM((DEPTH, height, size), low_type))
                made.append(pltpu.VMEM((DEPTH - 1, height, size), low_type))
        return made

    def bind(self, partials, totals, scratch):
        self.partials = partials
        self.totals = totals
        self.own_sem, self.core_send, self.core_recv, self.send_sem, self.recv_sem, *scratch = scratch
        self.place = my_place()
        self.peers = partners(*self.place)
        z, x, y, core = self.place
        self.mine = {"x": x, "y": y}
        self.core_in, self.own, self.parts = [], [], {}
        for group, (*_, held) in enumerate(self.groups):
            core_in, *scratch = scratch
            self.core_in.append(core_in)
            if held:
                self.own.append(None)
            else:
                own, *scratch = scratch
                self.own.append(own)
            for number, _ in self.entries[group]:
                self.parts[number] = scratch[:4]
                scratch = scratch[4:]

    def enter(self):
        meet(self.peers)

    def core_copies(self, group):
        a, first, cols, _, _, _, held = self.groups[group]
        at = pl.ds(first, cols)
        core = self.place[3]
        made = [
            remote(
                self.partials[a].at[:, :, :, 1 - core, :, at],
                self.core_in[group],
                self.core_send.at[group],
                self.core_recv.at[group],
                self.peers["c"][0],
            )
        ]
        if not held:
            made.append(
                pltpu.make_async_copy(
                    self.partials[a].at[:, :, :, core, :, at], self.own[group], self.own_sem.at[group]
                )
            )
        return made

    def copies(self, index, group):
        if index == 0:
            return self.core_copies(group)
        made = []
        z = self.place[0]
        for number, (order, start, size) in self.entries[group]:
            kept, in1, in2, in3 = self.parts[number]
            if index == 1:
                axis = order[2]
                far = 1 - self.mine[axis]
                at = pl.ds(start, size)
                core_in = self.core_in[group]
                source = core_in.at[:, :, far, :, at] if axis == "y" else core_in.at[:, far, :, :, at]
                pairs = [(source, in1, self.peers[axis][0], 0)]
            elif index == 2:
                axis = order[1]
                pairs = [(in1.at[:, 1 - self.mine[axis]], in2, self.peers[axis][0], 1)]
            else:
                pairs = [
                    (in2.at[(z + step) % DEPTH], in3.at[step - 1], self.peers["z"][step - 1], 1 + step)
                    for step in range(1, DEPTH)
                ]
            for source, target, peer, slot in pairs:
                made.append(
                    remote(
                        source,
                        target,
                        self.send_sem.at[number, slot],
                        self.recv_sem.at[number, slot],
                        peer,
                    )
                )
        return made

    def begin(self, index, group):
        for copy in self.copies(index, group):
            copy.start()

    def add(self, index, group):
        z, x, y, core = self.place
        a, first, _, out, offset, _, held = self.groups[group]
        core_in = self.core_in[group]
        for number, (order, start, size) in self.entries[group]:
            kept, in1, in2, in3 = self.parts[number]
            at = pl.ds(start, size)
            if index == 0:
                axis = order[2]
                mine = self.mine[axis]

                def spot(step, where):
                    far, side = step // SIDE, step % SIDE
                    return (far, side, where) if axis == "y" else (far, where, side)

                def own_at(place):
                    if held:
                        inside = pl.ds(first + start, size)
                        return self.partials[a][place + (core, slice(None), inside)].astype(f32)
                    return self.own[group][place + (slice(None), at)].astype(f32)

                @pl.loop(0, DEPTH * SIDE)
                def _(step):
                    near = spot(step, mine)
                    away = spot(step, 1 - mine)
                    kept[step // SIDE, step % SIDE] = own_at(near) + core_in[near + (slice(None), at)].astype(f32)
                    moved = own_at(away) + core_in[away + (slice(None), at)].astype(f32)
                    core_in[away + (slice(None), at)] = low(moved)
            elif index == 1:
                mine = self.mine[order[1]]

                @pl.loop(0, DEPTH)
                def _(far):
                    kept[far, mine] += in1[far, mine].astype(f32)
                    in1[far, 1 - mine] = low(kept[far, 1 - mine] + in1[far, 1 - mine].astype(f32))
            elif index == 2:
                mine = self.mine[order[1]]
                kept[z, mine] += in2[z].astype(f32)
                for step in range(1, DEPTH):
                    target = (z + step) % DEPTH
                    in2[target] = low(kept[target, mine] + in2[target].astype(f32))
            else:
                mine = self.mine[order[1]]
                total = kept[z, mine]
                for step in range(DEPTH - 1):
                    total = total + in3[step].astype(f32)
                self.totals[out][:, pl.ds(offset + start, size)] = total

    def tick(self, now):
        index, group = self.order[now]
        for copy in self.copies(index, group):
            copy.wait()
        self.add(index, group)
        if index < 3:
            self.begin(index + 1, group)


class SmallSum:
    def __init__(self, shape):
        self.shape = shape
        self.ticks = 4

    def scratch(self):
        return [
            pltpu.VMEM((4,) + self.shape, f32),
            pltpu.VMEM((3,) + self.shape, f32),
            pltpu.VMEM((DEPTH,) + self.shape, f32),
            sems((6,)),
            sems((6,)),
        ]

    def bind(self, out, scratch):
        self.out = out
        self.sums, self.arrived, self.along, self.send_sem, self.recv_sem = scratch
        self.place = my_place()
        self.peers = partners(*self.place)

    def copies(self, index):
        if index < 3:
            return [
                remote(
                    self.sums.at[index],
                    self.arrived.at[index],
                    self.send_sem.at[index],
                    self.recv_sem.at[index],
                    self.peers["cyx"[index]][0],
                )
            ]
        return [
            remote(
                self.sums.at[3],
                self.along.at[self.place[0]],
                self.send_sem.at[3 + step],
                self.recv_sem.at[3 + step],
                self.peers["z"][step],
            )
            for step in range(DEPTH - 1)
        ]

    def enter(self, value):
        self.sums[0] = value
        for copy in self.copies(0):
            copy.start()

    def tick(self, index):
        for copy in self.copies(index):
            copy.wait()
        if index < 3:
            self.sums[index + 1] = self.sums[index] + self.arrived[index]
            if index == 2:
                self.along[self.place[0]] = self.sums[3]
            for copy in self.copies(index + 1):
                copy.start()
        else:
            total = self.along[0]
            for far in range(1, DEPTH):
                total = total + self.along[far]
            self.out[...] = total


def slabs(array):
    rows, cols = array.shape
    return array.reshape(GRID + (rows // DEVICES, cols))


def flat(array):
    return array.reshape(DEVICES * array.shape[-2], array.shape[-1])


def gather_weights(shards):
    return [lax.all_gather(shard, AXES, axis=0, tiled=True) for shard in shards]


def scatter_sums(totals):
    return [
        lax.psum_scatter(total.astype(f32), AXES, scatter_dimension=0, tiled=True)
        for total in totals
    ]


def at_chunk(step, size):
    return pl.ds(pl.multiple_of(step * size, size), size)


def at_step(step, when):
    return lambda body: pl.when(step == when)(body)


def slab_rows(values):
    return low(values.astype(f32).reshape(-1, values.shape[-1]))


def arrive_kernel(plan, seg_rows, schedule, hidden_size, *refs):
    count = 5
    tokens_ref, mem_ref, gains_ref, *refs = refs
    shards, refs = refs[:count], refs[count:]
    (
        normed_ref,
        qkv_ref,
        attended_ref,
        log_ref,
        out_ref,
        mem_out_ref,
        states_two_ref,
        normed_two_ref,
        upward_ref,
        *refs,
    ) = refs
    fulls, refs = refs[:count], refs[count:]
    w_qkv_full, w_out_full, w_up_full, w_down_full, _ = fulls
    (
        first_ref,
        w_ref,
        w_out_slabs,
        w_out_ref,
        w_up_ref,
        w_down_ref,
        sum_ref,
        w_sem,
        up_sem,
        down_sem,
        *refs,
    ) = refs
    plan.bind(shards, fulls, refs)
    parts, rows, width = qkv_ref.shape
    pairs = width // PAIR
    leave_at = parts + pairs
    step = pl.program_id(0)
    chunk_now = step - leave_at

    @pl.when(step == 0)
    def _():
        plan.enter()
        load_first(tokens_ref, mem_ref, first_ref)

        def chunk(at):
            unit, _ = normal_form(first_ref[at, :].astype(f32))
            normed_ref[at, :] = low(unit * gains_ref[0:1, :].astype(f32))

        over_rows(rows, chunk)

    for when, ticks in schedule.items():

        @pl.when(step == when)
        def _():
            for now in ticks:
                plan.tick(now)

    @pl.when(step == 0)
    def _():
        copy = pltpu.make_async_copy(w_qkv_full, w_ref, w_sem)
        copy.start()
        copy.wait()

    @pl.when(step < parts)
    def _():
        block = slab_rows(w_ref[..., at_chunk(step, width)])
        qkv_ref[step] = low(nn(normed_ref[...], block))

    @pl.when((step >= parts) & (step < leave_at))
    def _():
        attend_kernel(
            seg_rows, qkv_ref, attended_ref, log_ref, at_chunk(step - parts, PAIR), step - parts
        )

    def hidden_copies(index):
        slot = lax.rem(index, 2)
        return [
            pltpu.make_async_copy(
                w_up_full.at[..., at_chunk(index, hidden_size)], w_up_ref.at[slot], up_sem.at[slot]
            ),
            pltpu.make_async_copy(w_down_full.at[index], w_down_ref.at[slot], down_sem.at[slot]),
        ]

    @pl.when(step == leave_at)
    def _():
        copy = pltpu.make_async_copy(w_out_full, w_out_slabs, w_sem)
        copy.start()
        for other in hidden_copies(chunk_now):
            other.start()
        copy.wait()
        w_out_ref[...] = slab_rows(w_out_slabs[...])

        def chunk(at):
            states = first_ref[at, :].astype(f32) + nn(attended_ref[at, :], w_out_ref[...])
            states_two_ref[at, :] = states
            unit, _ = normal_form(states)
            normed_two_ref[at, :] = low(unit * gains_ref[1:2, :].astype(f32))
            sum_ref[at, :] = states

        over_rows(rows, chunk)

    @pl.when(step >= leave_at)
    def _():
        for copy in hidden_copies(chunk_now):
            copy.wait()

        @pl.when(step + 1 < pl.num_programs(0))
        def _():
            for copy in hidden_copies(chunk_now + 1):
                copy.start()

        slot = lax.rem(chunk_now, 2)
        upward = nn(normed_two_ref[...], slab_rows(w_up_ref[slot]))
        upward_ref[...] = upward
        bent = jnp.tanh(upward * (gelu_c + gelu_c * gelu_a * (upward * upward)))
        active = low(upward * (0.5 + 0.5 * bent))
        down = w_down_ref[slot]
        sum_ref[...] += nn(active, down.reshape(hidden_size, width))

    @pl.when(step == pl.num_programs(0) - 1)
    def _():
        out_ref[...] = low(sum_ref[:seg_rows, :])
        mem_out_ref[...] = sum_ref[seg_rows:, :]
        for now in range(sum(len(t) for t in schedule.values()), plan.ticks):
            plan.tick(now)


def arrive(tokens, mem_tokens, gains, shards, plan, schedule):
    slots, seg_rows, width = tokens.shape
    mems = mem_tokens.shape[0]
    rows = seg_rows + mems
    parts = shards[0].shape[1] // width
    pairs = width // PAIR
    hidden = shards[2].shape[1]
    size = hidden // DEPTH
    lanes = packed_lanes(rows, seg_rows)[1]
    tall = shards[3].shape[0]
    segment = pl.BlockSpec((None, seg_rows, width), lambda j: (0, 0, 0), pipeline_mode=pl.Buffered(1))
    outs = pl.pallas_call(
        functools.partial(arrive_kernel, plan, seg_rows, schedule, size),
        grid=(parts + pairs + DEPTH,),
        in_specs=[segment, whole((mems, width)), whole(gains.shape)] + [ANYWHERE] * len(shards),
        out_specs=[
            whole((rows, width)),
            whole((parts, rows, width)),
            whole((rows, width)),
            whole((pairs, 1, lanes)),
            segment,
            whole((mems, width)),
            whole((rows, width)),
            whole((rows, width)),
            pl.BlockSpec((rows, size), lambda j: (0, jnp.maximum(j - parts - pairs, 0))),
        ]
        + [ANYWHERE] * len(shards),
        out_shape=[
            shaped((rows, width), low_type),
            shaped((parts, rows, width), low_type),
            shaped((rows, width), low_type),
            shaped((pairs, 1, lanes), f32),
            shaped((slots, seg_rows, width), low_type),
            shaped((mems, width), f32),
            shaped((rows, width), f32),
            shaped((rows, width), low_type),
            shaped((rows, hidden), f32),
        ]
        + [shaped(GRID + shard.shape, low_type) for shard in shards],
        scratch_shapes=[
            pltpu.VMEM((rows, width), low_type),
            pltpu.VMEM(GRID + shards[0].shape, low_type),
            pltpu.VMEM(GRID + shards[1].shape, low_type),
            pltpu.VMEM((width, width), low_type),
            pltpu.VMEM((2,) + GRID + (shards[2].shape[0], size), low_type),
            pltpu.VMEM((2,) + GRID[1:] + (tall, width), low_type),
            pltpu.VMEM((rows, width), f32),
            sems,
            sems((2,)),
            sems((2,)),
        ]
        + plan.scratch(),
        compiler_params=params(collective_id=0, has_side_effects=True),
        name="arrive",
    )(tokens, mem_tokens, gains, *shards)
    return outs[:9], [flat(o) for o in outs[9:]]


def carry_kernel(body, plan, counts, schedule, grid, *refs):
    ins, moved, outs, totals, scratch = counts
    parts = []
    for count in (ins, moved, outs, totals, scratch):
        parts.append(refs[:count])
        refs = refs[count:]
    own_in, partials, own_out, total_refs, own_scratch = parts
    plan.bind(partials, total_refs, refs)
    step = pl.program_id(0)

    @pl.when(step == 0)
    def _():
        plan.enter()
        for group in range(len(plan.groups)):
            plan.begin(0, group)

    for when, ticks in schedule.items():
        if when < grid:

            @pl.when(step == when)
            def _():
                for now in ticks:
                    plan.tick(now)

    body(*own_in, *own_out, *own_scratch)

    if grid in schedule:

        @pl.when(step == grid - 1)
        def _():
            for now in schedule[grid]:
                plan.tick(now)


def finish_kernel(plan, small, seg_rows, schedule, counts, *refs):
    (
        qkv_ref,
        grad_ref,
        attended_ref,
        log_ref,
        tokens_ref,
        mem_ref,
        normed_ref,
        gains_ref,
        w_ref,
        w_in_ref,
        small_in_ref,
        grad_states_ref,
        *refs,
    ) = refs
    moved, totals = counts
    partials, refs = refs[:moved], refs[moved:]
    first_ref, *refs = refs
    total_refs, refs = refs[:totals], refs[totals:]
    small_out_ref, keys_sum, values_sum, grad_qkv_ref, w_grad_ref, sum_ref, states_sem, *refs = refs
    kept = len(small.scratch())
    small.bind(small_out_ref, refs[:kept])
    plan.bind(list(partials) + [w_grad_ref], total_refs, refs[kept:])
    rows, width = normed_ref.shape
    parts = grad_qkv_ref.shape[0]
    pairs = width // PAIR
    step = pl.program_id(0)
    late = [g for g, group in enumerate(plan.groups) if group[-1]]
    early = [g for g, group in enumerate(plan.groups) if not group[-1]]
    states_copy = pltpu.make_async_copy(grad_states_ref, first_ref, states_sem)

    @pl.when(step == 0)
    def _():
        plan.enter()
        for group in early:
            plan.begin(0, group)
        states_copy.start()
        sum_ref[...] = jnp.zeros_like(sum_ref)

    for when, ticks in schedule.items():

        @pl.when(step == when)
        def _():
            for now in ticks:
                plan.tick(now)

    @pl.when(step < pairs)
    def _():
        attend_back_kernel(
            seg_rows,
            qkv_ref,
            grad_ref,
            attended_ref,
            log_ref,
            grad_qkv_ref,
            keys_sum,
            values_sum,
            at_chunk(step, PAIR),
        )

    @pl.when((step >= pairs) & (step < pairs + parts))
    def _():
        part = step - pairs
        grad_w = tn(normed_ref[...], grad_qkv_ref[part]) + w_in_ref[...]
        w_grad_ref[..., at_chunk(part, width)] = low(grad_w.reshape(GRID + (width // DEVICES, width)))
        for index, group in enumerate(late):

            @pl.when(part == index)
            def _():
                plan.begin(0, group)

    @pl.when(step >= pairs + parts)
    def _():
        sum_ref[...] += nt(grad_qkv_ref[step - pairs - parts], w_ref[...])

    @pl.when(step == pairs + 2 * parts - 1)
    def _():
        gain = gains_ref[0:1, :].astype(f32)
        states_copy.wait()
        small_out_ref[...] = small_in_ref[...]
        mems = rows - seg_rows

        def back(first, at):
            unit, inverse = normal_form(first)
            grad = sum_ref[at, :]
            small_out_ref[mems : mems + 1, :] += jnp.sum(grad * unit, axis=0, keepdims=True)
            first_ref[at, :] += norm_back(grad, unit, inverse, gain)

        def chunk(at):
            back(tokens_ref[at, :].astype(f32), at)

        over_rows(seg_rows, chunk, False)
        last = pl.ds(seg_rows, mems)
        back(mem_ref[...].astype(f32), last)
        small_out_ref[:mems, :] += first_ref[last, :]
        small.enter(small_out_ref[...])
        for event in FINISH_TAIL:
            if isinstance(event, int):
                small.tick(event)
            else:
                plan.tick(plan.order.index(event))


def finish(
    tokens, mem_tokens, kept, grad_attended, grad_states, gains, w_qkv, w_in, small_in, partials, plan, schedule, widths
):
    slots, seg_rows, width = tokens.shape
    mems = mem_tokens.shape[0]
    rows = seg_rows + mems
    qkv = kept["qkv"]
    parts = qkv.shape[0]
    pairs = width // PAIR
    small = SmallSum(small_in.shape)
    logs = kept["logs"]

    def pair(step):
        return jnp.minimum(step, pairs - 1)

    def part(step, start):
        return jnp.clip(step - start, 0, parts - 1)

    column = pl.BlockSpec((rows, PAIR), lambda j: (0, pair(j)))
    outs = pl.pallas_call(
        functools.partial(finish_kernel, plan, small, seg_rows, schedule, (len(partials), len(widths))),
        grid=(pairs + 2 * parts,),
        in_specs=[
            pl.BlockSpec((parts, rows, PAIR), lambda j: (0, 0, pair(j))),
            column,
            column,
            pl.BlockSpec((1,) + logs.shape[1:], lambda j: (pair(j), 0, 0)),
            pl.BlockSpec((None, seg_rows, width), lambda j: (0, 0, 0), pipeline_mode=pl.Buffered(1)),
            whole((mems, width)),
            whole((rows, width)),
            whole(gains.shape),
            pl.BlockSpec((width, width), lambda j: (0, part(j, pairs + parts))),
            pl.BlockSpec((width, width), lambda j: (0, part(j, pairs))),
            whole(small_in.shape),
            ANYWHERE,
        ]
        + [ANYWHERE] * len(partials),
        out_specs=[whole((rows, width))] + [whole(s) for s in widths] + [whole(small_in.shape)],
        out_shape=[shaped((rows, width), f32)]
        + [shaped(s, f32) for s in widths]
        + [shaped(small_in.shape, f32)],
        scratch_shapes=[
            pltpu.VMEM((rows, PAIR), f32),
            pltpu.VMEM((rows, PAIR), f32),
            pltpu.VMEM((parts, rows, width), low_type),
            pltpu.VMEM(GRID + (width // DEVICES, parts * width), low_type),
            pltpu.VMEM((rows, width), f32),
            sems,
        ]
        + small.scratch()
        + plan.scratch(),
        compiler_params=params(collective_id=2, has_side_effects=True),
        name="finish",
    )(
        qkv,
        grad_attended,
        kept["attended"],
        logs,
        tokens,
        mem_tokens,
        kept["normed_one"],
        gains,
        w_qkv,
        w_in,
        small_in,
        grad_states,
        *partials,
    )
    return outs[0], outs[1:-1], outs[-1]


def settle_kernel(count, first_ref, *refs):
    small_ref, *refs = refs
    sums, refs = refs[:count], refs[count + 1 :]
    tokens_ref, mem_ref, gains_ref, beta_ref, *outs = refs
    tokens_ref[...] = first_ref[...]

    @pl.when(pl.program_id(0) == 0)
    def _():
        mems = mem_ref.shape[0]
        mem_ref[...] = small_ref[:mems, :]
        gains_ref[...] = small_ref[mems : mems + 2, :]
        beta_ref[...] = small_ref[mems + 2 : mems + 3, :]
        for source, target in zip(sums, outs):
            target[...] = source[...]


def settle(first, small, sums, grad_tokens, mems):
    slots, seg_rows, width = grad_tokens.shape
    size = 256
    shapes = [(mems, width), (2, width), (1, width)] + [s.shape for s in sums]
    return pl.pallas_call(
        functools.partial(settle_kernel, len(sums)),
        grid=(seg_rows // size,),
        in_specs=[pl.BlockSpec((size, width), lambda j: (j, 0)), whole(small.shape)]
        + [whole(s.shape) for s in sums]
        + [ANYWHERE],
        out_specs=[pl.BlockSpec((None, size, width), lambda j: (0, j, 0))] + [result(s) for s in shapes],
        out_shape=[shaped(grad_tokens.shape, f32)] + [shaped(s, f32) for s in shapes],
        input_output_aliases={2 + len(sums): 0},
        compiler_params=params(),
        name="settle",
    )(first, small, *sums, grad_tokens)


def fast_gather(shards):
    groups = []
    for a, shard in enumerate(shards):
        rows, cols = shard.shape
        if cols < 2048:
            bounds = [(0, cols, (2, 2, 1, 1) if rows > 48 else (1, 1))]
        elif cols % 1024 == 256:
            bounds = [(0, 1280, (4, 4, 1, 1)), (1280, cols - 1280, (1, 1))]
        else:
            bounds = [(0, cols // 2, (5, 5, 1, 1)), (cols // 2, cols // 2, (5, 5, 1, 1))]
        for at, size, shares in bounds:
            groups.append((a, [(order, at + start, n) for order, start, n in cut(size, shares)]))
    return Gather(groups, ARRIVE_ORDER, 2)


def on_device(
    fast, tokens, item_ids, w_mem, w_qkv, w_out, w_up, w_down, mem_tokens, gains, w_beta, out_grad
):
    slots, seg_rows, width = tokens.shape
    mems = mem_tokens.shape[0]
    w_beta = w_beta.reshape(1, width)
    shards = [w_qkv, w_out, w_up, w_down, w_mem]
    if fast:
        plan = fast_gather(shards)
        schedule = spread(plan.order, ARRIVE_STEPS)
        arrived, fulls = arrive(tokens, mem_tokens, gains, shards, plan, schedule)
    else:
        fulls = gather_weights(shards)
    w_qkv, w_out, w_up, w_down, w_mem = fulls
    kept_all = []
    written = [None] * (slots + 1)
    out = None
    for slot in range(slots):
        kept = {}
        start = (tokens, mem_tokens)
        if fast and slot == 0:
            names = ("normed_one", "qkv", "attended", "logs", "out", "mem_out", "states_two")
            kept = dict(zip(names + ("normed_two", "upward"), arrived))
            out, mem_out = kept["out"], kept["mem_out"]
        else:
            entered = enter_segment(slot, tokens, mem_tokens, gains, w_qkv, w_mem, written[slot])
            kept["normed_one"], kept["qkv"] = entered[:2]
            if written[slot] is not None:
                kept["states_one"], kept["query"], kept["match"] = entered[2:]
                start = kept["states_one"]
            kept["attended"], kept["logs"] = attend(kept["qkv"], seg_rows)
        if slot + 1 == slots:
            both = leave_both(slot, start, kept["attended"], out_grad, gains, w_out, w_up, w_down, out, f32)
            out = both["block_out"]
        elif not fast:
            out, mem_out, kept["states_two"], kept["normed_two"], kept["upward"] = leave_segment(
                slot, slots, seg_rows, start, kept["attended"], gains, w_out, w_up, w_down, out
            )
            kept["mem_out"] = mem_out
        if slot + 1 < slots:
            written[slot + 1] = write_memory(slot, item_ids, mem_out, w_mem, w_beta)
        kept_all.append(kept)

    sums = None
    qkv_sum = None
    grad_tokens = None
    grad_mem_tokens = 0.0
    gain_one_sum = 0.0
    gain_two_sum = 0.0
    grad_beta = 0.0
    pulled = None
    for slot in reversed(range(slots)):
        kept = kept_all[slot]
        last = slot == 0
        grad_type = low_type if last else f32
        grad_rows = None
        mem_plan = None
        if slot + 1 < slots:
            grad_rows, w_pair_sum, grad_beta_part = write_back(
                slot, item_ids, kept["mem_out"], w_mem, w_beta, written[slot + 1], *pulled
            )
            grad_beta += grad_beta_part
            if fast and last:
                mem_plan = [slabs(w_query_sum), slabs(w_pair_sum)]
            left = leave_back(
                slot, out_grad, grad_rows, kept, gains, w_out, w_up, w_down, sums, grad_type, mem_plan
            )
        else:
            left = [both[name] for name in ("grad_states", "grad_attended", "up", "down", "out", "gain_two")]
        grad_states, grad_attended, up_sum, down_sum, out_sum, gain_two, *mem_total = left
        gain_two_sum += gain_two
        sums = {"up": up_sum, "down": down_sum, "out": out_sum}
        if fast and last:
            break
        grad_qkv = attend_back(kept["qkv"], grad_attended, kept["attended"], kept["logs"], seg_rows)
        grad_tokens, grad_mem, qkv_sum, gain_one, *extra = enter_back(
            slot,
            tokens,
            mem_tokens,
            kept,
            grad_qkv,
            grad_states,
            gains,
            w_qkv,
            w_mem,
            written[slot],
            qkv_sum,
            grad_tokens,
            grad_type,
        )
        if written[slot] is not None:
            w_query_sum, *pulled = extra
        grad_mem_tokens += grad_mem
        gain_one_sum += gain_one
    if fast:
        small = jnp.concatenate([grad_mem_tokens, gain_one_sum, gain_two_sum, grad_beta], axis=0)
        small = jnp.pad(small, ((0, -small.shape[0] % 8), (0, 0)))
        partials = [slabs(down_sum), slabs(up_sum), slabs(out_sum)]
        shapes = [p.shape[-2:] for p in partials] + [(width // DEVICES, w_qkv.shape[1])]
        third = shapes[1][1] // 3
        places = [(0, 0, 256), (0, 256, width - 256)]
        places += [(1, at, third) for at in range(0, shapes[1][1], third)]
        places += [(2, 0, width)]
        places += [(3, at, width) for at in range(0, shapes[3][1], width)]
        groups = [(a, at, size, a, at, cut(size, (1, 1)), a == 3) for a, at, size in places]
        plan = Reduce(groups, shapes, FINISH_ORDER)
        schedule = spread(plan.order, FINISH_STEPS)
        first, (down_total, up_total, out_total, qkv_total), small = finish(
            tokens,
            mem_tokens,
            kept,
            grad_attended,
            grad_states,
            gains,
            w_qkv,
            qkv_sum,
            small,
            partials,
            plan,
            schedule,
            shapes,
        )
        totals = [mem_total[0], qkv_total, out_total, up_total, down_total]
        grad_tokens, grad_mem_tokens, grad_gains, grad_beta, *totals = settle(
            first, small, totals, grad_tokens, mems
        )
        return (out, grad_tokens, *totals, grad_mem_tokens, grad_gains, grad_beta.reshape(width))
    mem_sum = jnp.concatenate([w_query_sum, w_pair_sum], axis=1)
    grad_gains = jnp.concatenate([gain_one_sum, gain_two_sum], axis=0)
    summed = scatter_sums([mem_sum, qkv_sum, sums["out"], sums["up"], sums["down"]])
    small = lax.psum((grad_mem_tokens, grad_gains, grad_beta.reshape(width)), AXES)
    return (out, grad_tokens, *summed, *small)


def solution(mesh):
    split_rows = P(AXES, None)
    split_items = P(AXES, None, None)
    in_specs = (
        split_items,
        P(AXES),
        split_rows,
        split_rows,
        split_rows,
        split_rows,
        split_rows,
        P(),
        P(),
        P(),
        split_items,
    )
    out_specs = (
        split_items,
        split_items,
        split_rows,
        split_rows,
        split_rows,
        split_rows,
        split_rows,
        P(),
        P(),
        P(),
    )
    fast = mesh.shape["wide"] == DEPTH * SIDE and mesh.shape["narrow"] == SIDE * SIDE
    return jax.shard_map(
        functools.partial(on_device, fast), mesh=mesh, in_specs=in_specs, out_specs=out_specs, check_vma=False
    )
```

```python
import functools

import jax
import jax.numpy as jnp
from jax import lax
from jax.experimental import pallas as pl
from jax.experimental.pallas import tpu as pltpu
from jax.sharding import PartitionSpec as P

HD = 64
PAIR = 2 * HD
AXES = ("wide", "narrow")
eps_norm = 1e-05
score_scale = 0.125
gelu_c = 0.7978845608028654
gelu_a = 0.044715
f32 = jnp.float32
low_type = jnp.bfloat16
MIB = 2**20
ANYWHERE = pl.BlockSpec(memory_space=pl.ANY)


def nn(left, right):
    return lax.dot_general(left, right, (((1,), (0,)), ((), ())), preferred_element_type=f32)


def nt(left, right):
    return lax.dot_general(left, right, (((1,), (1,)), ((), ())), preferred_element_type=f32)


def tn(left, right):
    return lax.dot_general(left, right, (((0,), (0,)), ((), ())), preferred_element_type=f32)


def low(values):
    return values.astype(low_type)


def split(values):
    high = low(values)
    return high, low(values - high.astype(f32))


def row_chunk(rows):
    for count in (208, 256, 128, 80, 64, 16):
        if rows % count == 0:
            return count
    return rows


def over_rows(rows, body, at_once=True):
    if at_once:
        body(pl.ds(0, rows))
        return
    count = row_chunk(rows)

    @pl.loop(0, rows // count)
    def _(step):
        body(pl.ds(pl.multiple_of(step * count, count), count))


def normal_form(values):
    average = jnp.mean(values, axis=-1, keepdims=True)
    centered = values - average
    spread = jnp.mean(centered * centered, axis=-1, keepdims=True)
    inverse = lax.rsqrt(spread + eps_norm)
    return centered * inverse, inverse


def norm_back(grad, unit, inverse, gain):
    scaled = grad * gain
    mean_grad = jnp.mean(scaled, axis=-1, keepdims=True)
    mean_unit = jnp.mean(scaled * unit, axis=-1, keepdims=True)
    return inverse * (scaled - mean_grad - unit * mean_unit)


def softplus(values):
    return jnp.maximum(values, 0.0) + jnp.log1p(jnp.exp(-jnp.abs(values)))


def feature_parts(softer):
    return [softer * pltpu.roll(softer, offset, 1) for offset in (1, 2, 3)]


def feature_back(grads, softer, values):
    width = softer.shape[1]
    total = None
    for offset, grad in zip((1, 2, 3), grads):
        term = grad * pltpu.roll(softer, offset, 1) + pltpu.roll(grad * softer, width - offset, 1)
        total = term if total is None else total + term
    return total * jax.nn.sigmoid(values)


def whole(shape, memory=None):
    zeros = (0,) * len(shape)
    return pl.BlockSpec(shape, lambda *_: zeros, pipeline_mode=pl.Buffered(1))


def result(shape):
    zeros = (0,) * len(shape)
    return pl.BlockSpec(shape, lambda *_: zeros)


def params(mib=60, **extra):
    return pltpu.CompilerParams(vmem_limit_bytes=mib * MIB, **extra)


def shaped(shape, dtype):
    return jax.ShapeDtypeStruct(shape, dtype)


def load_first(tokens_ref, mem_ref, first_ref):
    seg_rows = tokens_ref.shape[0]
    first_ref[:seg_rows, :] = tokens_ref[...]
    first_ref[seg_rows:, :] = mem_ref[...]


def enter_kernel(tokens_ref, mem_ref, gains_ref, w_ref, normed_ref, qkv_ref, first_ref):
    @pl.when(pl.program_id(0) == 0)
    def _():
        load_first(tokens_ref, mem_ref, first_ref)

        def chunk(at):
            unit, _ = normal_form(first_ref[at, :].astype(f32))
            normed_ref[at, :] = low(unit * gains_ref[0:1, :].astype(f32))

        over_rows(first_ref.shape[0], chunk)

    qkv_ref[0] = low(nn(normed_ref[...], w_ref[...]))


def enter_read_kernel(
    tokens_ref,
    mem_ref,
    gains_ref,
    w_ref,
    w_query_ref,
    phi_keys_ref,
    delta_ref,
    beta_ref,
    normed_ref,
    qkv_ref,
    states_ref,
    query_ref,
    match_ref,
    first_ref,
):
    @pl.when(pl.program_id(0) == 0)
    def _():
        load_first(tokens_ref, mem_ref, first_ref)
        width = first_ref.shape[1]
        delta_twice = jnp.concatenate([delta_ref[...], delta_ref[...]], axis=0)

        def chunk(at):
            first = first_ref[at, :]
            query = nn(first, w_query_ref[...])
            query_ref[at, :] = query
            parts = feature_parts(softplus(query))
            match = None
            for index, part in enumerate(parts):
                term = nt(low(part), phi_keys_ref[:, index * width : (index + 1) * width])
                match = term if match is None else match + term
            match_ref[at, :] = match
            numerator = nn(jnp.concatenate(split(match), axis=1), delta_twice)
            below = 1.0 + jnp.sum(match * beta_ref[...], axis=1, keepdims=True)
            states = first.astype(f32) + numerator / below
            states_ref[at, :] = states
            unit, _ = normal_form(states)
            normed_ref[at, :] = low(unit * gains_ref[0:1, :].astype(f32))

        over_rows(first_ref.shape[0], chunk)

    qkv_ref[0] = low(nn(normed_ref[...], w_ref[...]))


def enter_segment(slot, tokens, mem_tokens, gains, w_qkv, w_mem, written):
    slots, seg_rows, width = tokens.shape
    mems = mem_tokens.shape[0]
    rows = seg_rows + mems
    parts = w_qkv.shape[1] // width
    in_specs = [
        pl.BlockSpec((None, seg_rows, width), lambda j: (slot, 0, 0), pipeline_mode=pl.Buffered(1)),
        whole((mems, width)),
        whole(gains.shape),
        pl.BlockSpec((width, width), lambda j: (0, j)),
    ]
    out_shape = [shaped((rows, width), low_type), shaped((parts, rows, width), low_type)]
    out_specs = [
        result((rows, width)),
        pl.BlockSpec((1, rows, width), lambda j: (j, 0, 0)),
    ]
    args = [tokens, mem_tokens, gains, w_qkv]
    body = enter_kernel
    macs = rows * width * width * parts
    if written is not None:
        body = enter_read_kernel
        args += [w_mem, written["phi_keys_low"], written["delta_low"], written["beta_row"]]
        in_specs += [whole((width, width))] + [whole(a.shape) for a in args[5:]]
        out_shape += [
            shaped((rows, width), f32),
            shaped((rows, width), f32),
            shaped((rows, mems), f32),
        ]
        out_specs += [result((rows, width)), result((rows, width)), result((rows, mems))]
        macs += rows * width * width
    return pl.pallas_call(
        body,
        grid=(parts,),
        in_specs=in_specs,
        out_specs=out_specs,
        out_shape=out_shape,
        scratch_shapes=[pltpu.VMEM((rows, width), low_type)],
        compiler_params=params(24),
        cost_estimate=pl.CostEstimate(
            flops=2 * macs, bytes_accessed=20 * 2**20, transcendentals=0
        ),
        name="enter_read" if written is not None else "enter",
    )(*args)


def query_blocks(rows, seg_rows):
    step = 256 if seg_rows % 256 == 0 else seg_rows
    blocks = [(at, step) for at in range(0, seg_rows, step)]
    return blocks + [(seg_rows, rows - seg_rows)]


def packed_lanes(rows, seg_rows):
    places = []
    at = 0
    for _, count in query_blocks(rows, seg_rows):
        places.append(at)
        at += -(-2 * count // 128) * 128
    return places, at


def stack_heads(block):
    lanes = lax.broadcasted_iota(jnp.int32, block.shape, 1)
    zero = jnp.zeros_like(block)
    return jnp.concatenate(
        [jnp.where(lanes < HD, block, zero), jnp.where(lanes < HD, zero, block)], axis=0
    )


def merge_heads(stacked):
    count = stacked.shape[0] // 2
    lanes = lax.broadcasted_iota(jnp.int32, (count, stacked.shape[1]), 1)
    return jnp.where(lanes < HD, stacked[:count], stacked[count:])


def as_row(column):
    count = column.shape[0]
    return jnp.transpose(jnp.broadcast_to(column, (count, 128)))[0:1, :]


def attend_kernel(
    seg_rows, qkv_ref, attended_ref, log_ref, lanes=slice(None), pair=0
):
    rows = qkv_ref.shape[1]
    places, _ = packed_lanes(rows, seg_rows)
    for (start, count), place in zip(query_blocks(rows, seg_rows), places):
        reach = start + count
        queries = stack_heads(qkv_ref[0, start:reach, lanes] * score_scale)
        raw = nt(queries, qkv_ref[1, :reach, lanes])
        place_of = lax.broadcasted_iota(jnp.int32, (2 * count, count), 0)
        place_of = jnp.where(place_of < count, place_of, place_of - count)
        allowed = place_of >= lax.broadcasted_iota(jnp.int32, (2 * count, count), 1)
        edge = jnp.where(allowed, raw[:, start:], -1e30)
        masked = jnp.concatenate([raw[:, :start], edge], axis=1) if start else edge
        peak = jnp.max(masked, axis=1, keepdims=True)
        grown = jnp.exp(masked - peak)
        total = jnp.sum(grown, axis=1, keepdims=True)
        probs = low(grown * (1.0 / total))
        mixed = merge_heads(nn(probs, qkv_ref[2, :reach, lanes]))
        attended_ref[start:reach, lanes] = low(mixed)
        log_row = as_row(peak + jnp.log(total))
        log_ref[pair, 0:1, place : place + 2 * count] = log_row


def attend(qkv, seg_rows):
    parts, rows, width = qkv.shape
    _, lanes = packed_lanes(rows, seg_rows)
    pairs = width // PAIR
    return pl.pallas_call(
        functools.partial(attend_kernel, seg_rows),
        grid=(pairs,),
        in_specs=[pl.BlockSpec((parts, rows, PAIR), lambda h: (0, 0, h))],
        out_specs=[
            pl.BlockSpec((rows, PAIR), lambda h: (0, h)),
            pl.BlockSpec((1, 1, lanes), lambda h: (h, 0, 0)),
        ],
        out_shape=[shaped((rows, width), low_type), shaped((pairs, 1, lanes), f32)],
        compiler_params=params(10),
        cost_estimate=pl.CostEstimate(
            flops=4 * rows * rows * width, bytes_accessed=7 * 2**20, transcendentals=0
        ),
        name="attend",
    )(qkv)


def attend_back_kernel(
    seg_rows,
    qkv_ref,
    grad_ref,
    attended_ref,
    log_ref,
    out_ref,
    keys_sum,
    values_sum,
    lanes=slice(None),
):
    rows = qkv_ref.shape[1]
    places, _ = packed_lanes(rows, seg_rows)
    ones = jnp.ones((8, PAIR), f32)
    blocks = list(zip(query_blocks(rows, seg_rows), places))
    for order, ((start, count), place) in enumerate(reversed(blocks)):
        reach = start + count
        queries = stack_heads(qkv_ref[0, start:reach, :] * score_scale)
        grads = stack_heads(grad_ref[start:reach, :])
        mixed = attended_ref[start:reach, :].astype(f32)
        both = jnp.concatenate([mixed, mixed], axis=0) * grads.astype(f32)
        inner = lax.dot_general(
            ones,
            both,
            (((1,), (1,)), ((), ())),
            precision=lax.Precision.HIGHEST,
            preferred_element_type=f32,
        )[0:1, :]
        keys = qkv_ref[1, :reach, :]
        raw = nt(keys, queries)
        log_row = log_ref[0, 0:1, place : place + 2 * count]
        probs = jnp.exp(raw - log_row)
        place_of = lax.broadcasted_iota(jnp.int32, (count, 2 * count), 1)
        place_of = jnp.where(place_of < count, place_of, place_of - count)
        allowed = place_of >= lax.broadcasted_iota(jnp.int32, (count, 2 * count), 0)
        edge = jnp.where(allowed, probs[start:], 0.0)
        probs = jnp.concatenate([probs[:start], edge], axis=0) if start else edge
        grad_probs = nt(qkv_ref[2, :reach, :], grads)
        grad_raw = low(probs * (grad_probs - inner))
        value_part = nn(low(probs), grads)
        key_part = nn(grad_raw, queries)
        if order == 0:
            values_sum[...] = value_part
            keys_sum[...] = key_part
        else:
            values_sum[:reach, :] += value_part
            keys_sum[:reach, :] += key_part
        out_ref[0, start:reach, lanes] = low(merge_heads(tn(grad_raw, keys)) * score_scale)
    out_ref[1, :, lanes] = low(keys_sum[...])
    out_ref[2, :, lanes] = low(values_sum[...])


def attend_back(qkv, grad_attended, attended, logs, seg_rows):
    parts, rows, width = qkv.shape
    pairs = width // PAIR
    column = pl.BlockSpec((rows, PAIR), lambda h: (0, h))
    three = pl.BlockSpec((parts, rows, PAIR), lambda h: (0, 0, h))
    return pl.pallas_call(
        functools.partial(attend_back_kernel, seg_rows),
        grid=(pairs,),
        in_specs=[
            three,
            column,
            column,
            pl.BlockSpec((1,) + logs.shape[1:], lambda h: (h, 0, 0)),
        ],
        out_specs=three,
        out_shape=shaped((parts, rows, width), low_type),
        scratch_shapes=[pltpu.VMEM((rows, PAIR), f32), pltpu.VMEM((rows, PAIR), f32)],
        compiler_params=params(12),
        cost_estimate=pl.CostEstimate(
            flops=10 * rows * rows * width, bytes_accessed=13 * 2**20, transcendentals=0
        ),
        name="attend_back",
    )(qkv, grad_attended, attended, logs)


def leave_kernel(
    reads, earlier, *refs
):
    if reads:
        (states_one_ref, *refs) = refs
    else:
        (tokens_ref, mem_ref, *refs) = refs
    (attended_ref, gains_ref, w_out_ref, w_up_ref, w_down_ref, *refs) = refs
    if earlier:
        refs = refs[1:]
    (out_ref, mem_out_ref, states_two_ref, normed_ref, upward_ref, sum_ref, *scratch) = refs
    rows, width = attended_ref.shape
    seg_rows = out_ref.shape[0]
    step = pl.program_id(0)

    @pl.when(step == 0)
    def _():
        if not reads:
            load_first(tokens_ref, mem_ref, scratch[0])

        def chunk(at):
            source = states_one_ref if reads else scratch[0]
            states = source[at, :].astype(f32) + nn(attended_ref[at, :], w_out_ref[...])
            states_two_ref[at, :] = states
            unit, _ = normal_form(states)
            normed_ref[at, :] = low(unit * gains_ref[1:2, :].astype(f32))
            sum_ref[at, :] = states

        over_rows(rows, chunk)

    def chunk(at):
        upward = nn(normed_ref[at, :], w_up_ref[...])
        upward_ref[at, :] = upward
        bent = jnp.tanh(upward * (gelu_c + gelu_c * gelu_a * (upward * upward)))
        active = low(upward * (0.5 + 0.5 * bent))
        sum_ref[at, :] += nn(active, w_down_ref[...])

    chunk(pl.ds(0, rows))

    @pl.when(step == pl.num_programs(0) - 1)
    def _():
        out_ref[...] = low(sum_ref[:seg_rows, :])
        mem_out_ref[...] = sum_ref[seg_rows:, :]


def leave_segment(slot, slots, seg_rows, start, attended, gains, w_out, w_up, w_down, earlier):
    rows, width = attended.shape
    hidden = w_up.shape[1]
    size = 512 if hidden % 512 == 0 else hidden
    reads = not isinstance(start, tuple)
    args = []
    in_specs = []
    scratch = [pltpu.VMEM((rows, width), f32)]
    if reads:
        args.append(start)
        in_specs.append(whole((rows, width)))
    else:
        tokens, mem_tokens = start
        args += [tokens, mem_tokens]
        in_specs += [
            pl.BlockSpec((None, seg_rows, width), lambda j: (slot, 0, 0), pipeline_mode=pl.Buffered(1)),
            whole(mem_tokens.shape),
        ]
        scratch.append(pltpu.VMEM((rows, width), low_type))
    args += [attended, gains, w_out, w_up, w_down]
    in_specs += [
        whole((rows, width)),
        whole(gains.shape),
        whole((width, width)),
        pl.BlockSpec((width, size), lambda j: (0, j)),
        pl.BlockSpec((size, width), lambda j: (j, 0)),
    ]
    aliases = {}
    if earlier is not None:
        aliases = {len(args): 0}
        args.append(earlier)
        in_specs.append(pl.BlockSpec(memory_space=pl.ANY))
    return pl.pallas_call(
        functools.partial(leave_kernel, reads, earlier is not None),
        grid=(hidden // size,),
        in_specs=in_specs,
        out_specs=[
            pl.BlockSpec((None, seg_rows, width), lambda j: (slot, 0, 0)),
            result((rows - seg_rows, width)),
            result((rows, width)),
            result((rows, width)),
            pl.BlockSpec((rows, size), lambda j: (0, j)),
        ],
        out_shape=[
            shaped((slots, seg_rows, width), low_type),
            shaped((rows - seg_rows, width), f32),
            shaped((rows, width), f32),
            shaped((rows, width), low_type),
            shaped((rows, hidden), f32),
        ],
        scratch_shapes=scratch,
        input_output_aliases=aliases,
        compiler_params=params(40),
        cost_estimate=pl.CostEstimate(
            flops=2 * rows * width * (width + 2 * hidden), bytes_accessed=36 * 2**20, transcendentals=0
        ),
        name="leave",
    )(*args)


def beta_parts(mem_out, w_beta):
    column = jnp.sum(mem_out * w_beta, axis=1, keepdims=True)
    row = lax.dot_general(
        w_beta,
        mem_out,
        (((1,), (1,)), ((), ())),
        precision=lax.Precision.HIGHEST,
        preferred_element_type=f32,
    )
    return jax.nn.sigmoid(column), jax.nn.sigmoid(row)


def write_kernel(
    slot,
    flag_ref,
    mem_out_ref,
    w_key_ref,
    w_value_ref,
    w_beta_ref,
    key_ref,
    value_ref,
    phi_ref,
    phi_rest_ref,
    delta_ref,
    beta_row_ref,
):
    flag = jnp.where(flag_ref[slot + 1] == flag_ref[slot], 1.0, 0.0).astype(f32)
    width = key_ref.shape[1]
    mem_out = mem_out_ref[...]
    mem_low = low(mem_out)
    key = nn(mem_low, w_key_ref[...])
    value = nn(mem_low, w_value_ref[...])
    key_ref[...] = key
    value_ref[...] = value
    for index, part in enumerate(feature_parts(softplus(key))):
        high, rest = split(part)
        phi_ref[:, index * width : (index + 1) * width] = high
        phi_rest_ref[:, index * width : (index + 1) * width] = rest
    beta, beta_row = beta_parts(mem_out, w_beta_ref[...].astype(f32))
    delta_ref[...] = low(low(beta * value).astype(f32) * flag)
    beta_row_ref[...] = beta_row * flag


def write_memory(slot, flag, mem_out, w_mem, w_beta):
    mems, width = mem_out.shape
    names = ("key", "value", "phi_keys_low", "phi_keys_rest", "delta_low", "beta_row")
    out_shape = [
        shaped((mems, width), f32),
        shaped((mems, width), f32),
        shaped((mems, 3 * width), low_type),
        shaped((mems, 3 * width), low_type),
        shaped((mems, width), low_type),
        shaped((1, mems), f32),
    ]
    outs = pl.pallas_call(
        functools.partial(write_kernel, slot),
        grid=(1,),
        in_specs=[
            pl.BlockSpec(memory_space=pltpu.SMEM),
            whole((mems, width)),
            pl.BlockSpec((width, width), lambda j: (0, 1)),
            pl.BlockSpec((width, width), lambda j: (0, 2)),
            whole((1, width)),
        ],
        out_specs=[result(s.shape) for s in out_shape],
        out_shape=out_shape,
        compiler_params=params(10),
        name="write",
    )(flag, mem_out, w_mem, w_mem, w_beta)
    return dict(zip(names, outs))


def write_back_kernel(
    slot,
    flag_ref,
    mem_out_ref,
    w_key_ref,
    w_value_ref,
    w_beta_ref,
    key_ref,
    value_ref,
    grad_delta_ref,
    grad_phi_ref,
    grad_normal_ref,
    grad_rows_ref,
    grad_w_ref,
    grad_beta_ref,
):
    flag = jnp.where(flag_ref[slot + 1] == flag_ref[slot], 1.0, 0.0).astype(f32)
    width = key_ref.shape[1]
    mem_out = mem_out_ref[...]
    mem_low = low(mem_out)
    w_beta = w_beta_ref[...].astype(f32)
    key = key_ref[...]
    value = value_ref[...]
    beta, _ = beta_parts(mem_out, w_beta)
    softer = softplus(key)
    parts = feature_parts(softer)
    grad_delta = grad_delta_ref[...] * flag
    grad_strength = jnp.sum(grad_delta * value, axis=1, keepdims=True)
    grads = []
    for index, part in enumerate(parts):
        at = slice(index * width, (index + 1) * width)
        grad_normal = grad_normal_ref[:, at] * flag
        grad_strength += jnp.sum(part * grad_normal, axis=1, keepdims=True)
        grads.append(grad_phi_ref[:, at] * flag + beta * grad_normal)
    grad_key = low(feature_back(grads, softer, key))
    grad_value = low(beta * grad_delta)
    grad_logit = grad_strength * beta * (1.0 - beta)
    grad_rows_ref[...] = (
        grad_logit * w_beta + nt(grad_key, w_key_ref[...]) + nt(grad_value, w_value_ref[...])
    )
    grad_beta_ref[...] = jnp.sum(grad_logit * mem_out, axis=0, keepdims=True)
    grad_w_ref[:, :width] = low(tn(mem_low, grad_key))
    grad_w_ref[:, width:] = low(tn(mem_low, grad_value))


def write_back(slot, flag, mem_out, w_mem, w_beta, written, grad_delta, grad_phi, grad_normal):
    mems, width = mem_out.shape
    args = [flag, mem_out, w_mem, w_mem, w_beta, written["key"], written["value"]]
    args += [grad_delta, grad_phi, grad_normal]
    out_shape = [
        shaped((mems, width), f32),
        shaped((width, 2 * width), low_type),
        shaped((1, width), f32),
    ]
    return pl.pallas_call(
        functools.partial(write_back_kernel, slot),
        grid=(1,),
        in_specs=[
            pl.BlockSpec(memory_space=pltpu.SMEM),
            whole((mems, width)),
            pl.BlockSpec((width, width), lambda j: (0, 1)),
            pl.BlockSpec((width, width), lambda j: (0, 2)),
        ]
        + [whole(a.shape) for a in args[4:]],
        out_specs=[result(s.shape) for s in out_shape],
        out_shape=out_shape,
        compiler_params=params(12),
        name="write_back",
    )(*args)


def leave_back_kernel(writes, adds, *refs):
    (out_grad_ref, *refs) = refs
    if writes:
        (grad_rows_ref, *refs) = refs
    (
        states_two_ref,
        normed_ref,
        upward_ref,
        attended_ref,
        gains_ref,
        w_out_ref,
        w_up_ref,
        w_down_ref,
        *refs,
    ) = refs
    if adds:
        (up_in_ref, down_in_ref, out_in_ref, *refs) = refs
    (
        grad_states_ref,
        grad_attended_ref,
        grad_up_ref,
        grad_down_ref,
        grad_out_ref,
        grad_gain_ref,
        grad_low_ref,
        sum_ref,
        grad_two_ref,
    ) = refs
    rows, width = normed_ref.shape
    seg_rows = out_grad_ref.shape[0]
    step = pl.program_id(0)

    @pl.when(step == 0)
    def _():
        grad_low_ref[:seg_rows, :] = out_grad_ref[...]
        grad_states_ref[:seg_rows, :] = out_grad_ref[...].astype(f32)
        if writes:
            grad_low_ref[seg_rows:, :] = low(grad_rows_ref[...])
            grad_states_ref[seg_rows:, :] = grad_rows_ref[...]
        else:
            grad_low_ref[seg_rows:, :] = jnp.zeros((rows - seg_rows, width), low_type)
            grad_states_ref[seg_rows:, :] = jnp.zeros((rows - seg_rows, width), f32)
        sum_ref[...] = jnp.zeros_like(sum_ref)

    upward = upward_ref[...]
    square = upward * upward
    bent = jnp.tanh(upward * (gelu_c + gelu_c * gelu_a * square))
    half = 0.5 + 0.5 * bent
    active = upward * half
    slope = half + (active - active * half) * (2.0 * gelu_c + 6.0 * gelu_c * gelu_a * square)
    grad_low = grad_low_ref[...]
    grad_upward = low(nt(grad_low, w_down_ref[...]) * slope)
    grad_down = tn(low(active), grad_low)
    grad_up = tn(normed_ref[...], grad_upward)
    sum_ref[...] += nt(grad_upward, w_up_ref[...])
    if adds:
        grad_down += down_in_ref[...]
        grad_up += up_in_ref[...]
    grad_down_ref[...] = grad_down.astype(grad_down_ref.dtype)
    grad_up_ref[...] = grad_up.astype(grad_up_ref.dtype)

    @pl.when(step == pl.num_programs(0) - 1)
    def _():
        gain = gains_ref[1:2, :].astype(f32)
        grad_gain_ref[...] = jnp.zeros_like(grad_gain_ref)

        def chunk(at):
            unit, inverse = normal_form(states_two_ref[at, :])
            grad = sum_ref[at, :]
            grad_gain_ref[...] += jnp.sum(grad * unit, axis=0, keepdims=True)
            total = grad_states_ref[at, :] + norm_back(grad, unit, inverse, gain)
            grad_states_ref[at, :] = total
            total_low = low(total)
            grad_two_ref[at, :] = total_low
            grad_attended_ref[at, :] = low(nt(total_low, w_out_ref[...]))

        over_rows(rows, chunk)
        grad_out = tn(attended_ref[...], grad_two_ref[...])
        if adds:
            grad_out += out_in_ref[...]
        grad_out_ref[...] = grad_out.astype(grad_out_ref.dtype)


def leave_back(slot, out_grad, grad_rows, kept, gains, w_out, w_up, w_down, sums, grad_type, moved=None):
    _, seg_rows, width = out_grad.shape
    rows = kept["normed_two"].shape[0]
    hidden = w_up.shape[1]
    size = 512 if hidden % 512 == 0 else hidden
    up_spec = pl.BlockSpec((width, size), lambda j: (0, j))
    down_spec = pl.BlockSpec((size, width), lambda j: (j, 0))
    args = [out_grad]
    in_specs = [
        pl.BlockSpec((None, seg_rows, width), lambda j: (slot, 0, 0), pipeline_mode=pl.Buffered(1))
    ]
    if grad_rows is not None:
        args.append(grad_rows)
        in_specs.append(whole(grad_rows.shape))
    args += [kept["states_two"], kept["normed_two"], kept["upward"], kept["attended"]]
    args += [gains, w_out, w_up, w_down]
    in_specs += [
        whole((rows, width)),
        whole((rows, width)),
        pl.BlockSpec((rows, size), lambda j: (0, j)),
        whole((rows, width)),
        whole(gains.shape),
        whole((width, width)),
        up_spec,
        down_spec,
    ]
    if sums is not None:
        args += [sums["up"], sums["down"], sums["out"]]
        in_specs += [up_spec, down_spec, whole((width, width))]
    body = functools.partial(leave_back_kernel, grad_rows is not None, sums is not None)
    out_specs = [
        result((rows, width)),
        result((rows, width)),
        up_spec,
        down_spec,
        result((width, width)),
        result((1, width)),
    ]
    out_shape = [
        shaped((rows, width), f32),
        shaped((rows, width), low_type),
        shaped((width, hidden), grad_type),
        shaped((hidden, width), grad_type),
        shaped((width, width), grad_type),
        shaped((1, width), f32),
    ]
    scratch = [
        pltpu.VMEM((rows, width), low_type),
        pltpu.VMEM((rows, width), f32),
        pltpu.VMEM((rows, width), low_type),
    ]
    extra = {}
    if moved is not None:
        shapes = [m.shape[-2:] for m in moved]
        groups = []
        before = 0
        for a, (_, cols) in enumerate(shapes):
            for at in range(0, cols, width):
                groups.append((a, at, width, 0, before + at, cut(width, (1, 1)), False))
            before += cols
        plan = Reduce(groups, shapes, event_order(len(groups), 2))
        grid = hidden // size
        schedule = spread(plan.order, {1: (0, 1), 2: (1, 0), 3: (1, 1), 4: (1, 2), 5: (2, 2), grid: (3, 2)})
        counts = (len(args), len(moved), len(out_shape), 1, len(scratch))
        body = functools.partial(carry_kernel, body, plan, counts, schedule, grid)
        args += moved
        in_specs += [ANYWHERE] * len(moved)
        total = (width // DEVICES, before)
        out_specs.append(result(total))
        out_shape.append(shaped(total, f32))
        scratch += plan.scratch()
        extra = dict(collective_id=1, has_side_effects=True)
    return pl.pallas_call(
        body,
        grid=(hidden // size,),
        in_specs=in_specs,
        out_specs=out_specs,
        out_shape=out_shape,
        scratch_shapes=scratch,
        compiler_params=params(**extra),
        cost_estimate=pl.CostEstimate(
            flops=4 * rows * width * (width + 2 * hidden), bytes_accessed=60 * 2**20, transcendentals=0
        ),
        name="leave_back",
    )(*args)


def leave_both_kernel(reads, adds, slot, *refs):
    if reads:
        (states_one_ref, *refs) = refs
    else:
        (tokens_ref, mem_ref, *refs) = refs
    (attended_ref, out_grad_ref, gains_ref, w_out_ref, w_up_ref, w_down_ref, *refs) = refs
    if adds:
        (earlier_ref, *refs) = refs
    (
        out_ref,
        grad_states_ref,
        grad_attended_ref,
        grad_up_ref,
        grad_down_ref,
        grad_out_ref,
        grad_gain_ref,
        states_two_ref,
        normed_ref,
        forward_ref,
        backward_ref,
        grad_low_ref,
        *scratch,
    ) = refs
    rows, width = attended_ref.shape
    seg_rows = out_grad_ref.shape[0]
    copies = []
    if adds == "rows":
        both_ref = out_ref
        out_ref, first_sem, last_sem, *scratch = scratch
        copies = [
            pltpu.make_async_copy(earlier_ref, both_ref.at[0], first_sem),
            pltpu.make_async_copy(out_ref, both_ref.at[slot], last_sem),
        ]
    step = pl.program_id(0)

    @pl.when(step == 0)
    def _():
        if copies:
            copies[0].start()
        if not reads:
            load_first(tokens_ref, mem_ref, scratch[0])
        grad_low_ref[:seg_rows, :] = out_grad_ref[...]
        grad_low_ref[seg_rows:, :] = jnp.zeros((rows - seg_rows, width), low_type)

        def chunk(at):
            source = states_one_ref if reads else scratch[0]
            states = source[at, :].astype(f32) + nn(attended_ref[at, :], w_out_ref[...])
            states_two_ref[at, :] = states
            unit, _ = normal_form(states)
            normed_ref[at, :] = low(unit * gains_ref[1:2, :].astype(f32))
            forward_ref[at, :] = states
            backward_ref[at, :] = jnp.zeros_like(states)

        over_rows(rows, chunk)

    normed = normed_ref[...]
    grad_low = grad_low_ref[...]
    upward = nn(normed, w_up_ref[...])
    grad_active = nt(grad_low, w_down_ref[...])
    active, slope = gelu_parts(upward)
    active = low(active)
    grad_upward = low(grad_active * slope)
    forward_ref[...] += nn(active, w_down_ref[...])
    backward_ref[...] += nt(grad_upward, w_up_ref[...])
    grad_down = tn(active, grad_low)
    grad_up = tn(normed, grad_upward)
    grad_down_ref[...] = grad_down.astype(grad_down_ref.dtype)
    grad_up_ref[...] = grad_up.astype(grad_up_ref.dtype)

    @pl.when(step == pl.num_programs(0) - 1)
    def _():
        gain = gains_ref[1:2, :].astype(f32)
        grad_gain_ref[...] = jnp.zeros_like(grad_gain_ref)

        def chunk(at):
            unit, inverse = normal_form(states_two_ref[at, :])
            grad = backward_ref[at, :]
            grad_gain_ref[...] += jnp.sum(grad * unit, axis=0, keepdims=True)
            total = grad_low_ref[at, :].astype(f32) + norm_back(grad, unit, inverse, gain)
            grad_states_ref[at, :] = total
            total_low = low(total)
            normed_ref[at, :] = total_low
            grad_attended_ref[at, :] = low(nt(total_low, w_out_ref[...]))

        over_rows(rows, chunk)
        grad_out = tn(attended_ref[...], normed_ref[...])
        grad_out_ref[...] = grad_out.astype(grad_out_ref.dtype)
        out_ref[...] = low(forward_ref[:seg_rows, :])
        if copies:
            copies[1].start()
            copies[0].wait()
            copies[1].wait()


def gelu_parts(upward):
    square = upward * upward
    bent = jnp.tanh(upward * (gelu_c + gelu_c * gelu_a * square))
    half = 0.5 + 0.5 * bent
    active = upward * half
    slope = half + (active - active * half) * (2.0 * gelu_c + 6.0 * gelu_c * gelu_a * square)
    return active, slope


def leave_both(slot, start, attended, out_grad, gains, w_out, w_up, w_down, earlier, grad_type):
    slots, seg_rows, width = out_grad.shape
    rows = attended.shape[0]
    mems = rows - seg_rows
    hidden = w_up.shape[1]
    size = 512 if hidden % 512 == 0 else hidden
    reads = not isinstance(start, tuple)
    args = []
    in_specs = []
    scratch = [
        pltpu.VMEM((rows, width), f32),
        pltpu.VMEM((rows, width), low_type),
        pltpu.VMEM((rows, width), f32),
        pltpu.VMEM((rows, width), f32),
        pltpu.VMEM((rows, width), low_type),
    ]
    segment = pl.BlockSpec((None, seg_rows, width), lambda j: (slot, 0, 0), pipeline_mode=pl.Buffered(1))
    if reads:
        args.append(start)
        in_specs.append(whole((rows, width)))
    else:
        args += list(start)
        in_specs += [segment, whole((mems, width))]
        scratch.append(pltpu.VMEM((rows, width), low_type))
    up_spec = pl.BlockSpec((width, size), lambda j: (0, j))
    down_spec = pl.BlockSpec((size, width), lambda j: (j, 0))
    args += [attended, out_grad, gains, w_out, w_up, w_down]
    in_specs += [
        whole((rows, width)),
        segment,
        whole(gains.shape),
        whole((width, width)),
        up_spec,
        down_spec,
    ]
    aliases = {}
    adds = earlier is not None
    if adds and earlier.ndim == 2:
        adds = "rows"
    if earlier is not None:
        args.append(earlier)
        in_specs.append(whole(earlier.shape) if adds == "rows" else ANYWHERE)
        aliases = {} if adds == "rows" else {len(args) - 1: 0}
        if adds == "rows":
            place = 5 if reads else 6
            scratch[place:place] = [pltpu.VMEM((seg_rows, width), low_type), sems, sems]
    outs = pl.pallas_call(
        functools.partial(leave_both_kernel, reads, adds, slot),
        grid=(hidden // size,),
        in_specs=in_specs,
        out_specs=[
            ANYWHERE if adds == "rows" else segment,
            whole((rows, width)),
            whole((rows, width)),
            up_spec,
            down_spec,
            whole((width, width)),
            whole((1, width)),
        ],
        out_shape=[
            shaped((slots, seg_rows, width), low_type),
            shaped((rows, width), f32),
            shaped((rows, width), low_type),
            shaped((width, hidden), grad_type),
            shaped((hidden, width), grad_type),
            shaped((width, width), grad_type),
            shaped((1, width), f32),
        ],
        scratch_shapes=scratch,
        input_output_aliases=aliases,
        compiler_params=params(50),
        cost_estimate=pl.CostEstimate(
            flops=6 * rows * width * (width + 2 * hidden), bytes_accessed=60 * 2**20, transcendentals=0
        ),
        name="leave_both",
    )(*args)
    names = ("block_out", "grad_states", "grad_attended", "up", "down", "out", "gain_two")
    return dict(zip(names, outs))


def enter_back_kernel(reads, adds, earlier, *refs):
    (tokens_ref, mem_ref, normed_ref, grad_qkv_ref, grad_states_ref, gains_ref, w_ref, *refs) = refs
    if reads:
        (
            states_ref,
            query_ref,
            match_ref,
            w_query_ref,
            phi_keys_ref,
            phi_rest_ref,
            delta_ref,
            beta_ref,
            *refs,
        ) = refs
    if adds:
        (w_in_ref, *refs) = refs
    if earlier:
        refs = refs[1:]
    (grad_tokens_ref, grad_mem_ref, grad_w_ref, grad_gain_ref, *refs) = refs
    if reads:
        (grad_w_query_ref, grad_delta_ref, grad_phi_ref, grad_normal_ref, *refs) = refs
    (first_ref, sum_ref, *refs) = refs
    rows, width = normed_ref.shape
    seg_rows = tokens_ref.shape[0]
    step = pl.program_id(0)

    @pl.when(step == 0)
    def _():
        load_first(tokens_ref, mem_ref, first_ref)
        sum_ref[...] = jnp.zeros_like(sum_ref)

    grad_part = grad_qkv_ref[0]
    sum_ref[...] += nt(grad_part, w_ref[...])
    grad_w = tn(normed_ref[...], grad_part)
    if adds:
        grad_w += w_in_ref[...]
    grad_w_ref[...] = grad_w.astype(grad_w_ref.dtype)

    @pl.when(step == pl.num_programs(0) - 1)
    def _():
        gain = gains_ref[0:1, :].astype(f32)
        grad_gain_ref[...] = jnp.zeros_like(grad_gain_ref)
        if reads:
            (grad_query_ref, packed_sum_ref, delta_sum_ref) = refs
            packed_sum_ref[...] = jnp.zeros_like(packed_sum_ref)
            delta_sum_ref[...] = jnp.zeros_like(delta_sum_ref)
            mems = delta_ref.shape[0]
            beta = beta_ref[...]
            basis = jnp.concatenate([phi_keys_ref[...], phi_keys_ref[...], phi_rest_ref[...]], axis=0)

        def chunk(at):
            first = first_ref[at, :].astype(f32)
            states = states_ref[at, :] if reads else first
            unit, inverse = normal_form(states)
            grad = sum_ref[at, :]
            grad_gain_ref[...] += jnp.sum(grad * unit, axis=0, keepdims=True)
            total = grad_states_ref[at, :] + norm_back(grad, unit, inverse, gain)
            if reads:
                match = match_ref[at, :]
                below = 1.0 + jnp.sum(match * beta, axis=1, keepdims=True)
                grad_num = low(total / below)
                grad_below = -jnp.sum(total * (states - first), axis=1, keepdims=True) / below
                pulled = nt(grad_num, delta_ref[...])
                spread_below = grad_below * beta
                both_high, both_low = split(pulled + spread_below)
                weights = jnp.concatenate([both_high, both_low, low(spread_below)], axis=1)
                query = query_ref[at, :]
                softer = softplus(query)
                parts = feature_parts(softer)
                grads = []
                packed = jnp.concatenate(
                    list(split(pulled))
                    + [low(jnp.broadcast_to(part, pulled.shape)) for part in (grad_below,)]
                    + [
                        low(
                            jnp.broadcast_to(
                                grad_below - low(grad_below).astype(f32), pulled.shape
                            )
                        )
                    ],
                    axis=1,
                )
                for index, part in enumerate(parts):
                    cols = slice(index * width, (index + 1) * width)
                    grads.append(nn(weights, basis[:, cols]))
                    packed_sum_ref[:, cols] += tn(packed, low(part))
                delta_sum_ref[...] += tn(jnp.concatenate(split(match), axis=1), grad_num)
                grad_query = low(feature_back(grads, softer, query))
                grad_query_ref[at, :] = grad_query
                total += nt(grad_query, w_query_ref[...])
            sum_ref[at, :] = total

        over_rows(rows, chunk, False)
        grad_tokens_ref[...] = sum_ref[:seg_rows, :]
        grad_mem_ref[...] = sum_ref[seg_rows:, :]
        if reads:
            grad_w_query_ref[...] = low(tn(first_ref[...], grad_query_ref[...]))
            grad_delta_ref[...] = delta_sum_ref[:mems, :] + delta_sum_ref[mems:, :]
            grad_phi_ref[...] = packed_sum_ref[:mems, :] + packed_sum_ref[mems : 2 * mems, :]
            grad_normal_ref[...] = (
                packed_sum_ref[2 * mems : 2 * mems + 1, :]
                + packed_sum_ref[3 * mems : 3 * mems + 1, :]
            )


def enter_back(
    slot, tokens, mem_tokens, kept, grad_qkv, grad_states, gains, w_qkv, w_mem, written, w_sum, earlier, grad_type
):
    slots, seg_rows, width = tokens.shape
    mems = mem_tokens.shape[0]
    rows = seg_rows + mems
    parts = grad_qkv.shape[0]
    reads = written is not None
    args = [tokens, mem_tokens, kept["normed_one"], grad_qkv, grad_states, gains, w_qkv]
    in_specs = [
        pl.BlockSpec((None, seg_rows, width), lambda j: (slot, 0, 0), pipeline_mode=pl.Buffered(1)),
        whole((mems, width)),
        whole((rows, width)),
        pl.BlockSpec((1, rows, width), lambda j: (j, 0, 0)),
        whole((rows, width)),
        whole(gains.shape),
        pl.BlockSpec((width, width), lambda j: (0, j)),
    ]
    scratch = [pltpu.VMEM((rows, width), low_type), pltpu.VMEM((rows, width), f32)]
    if reads:
        more = [written["phi_keys_low"], written["phi_keys_rest"]]
        more += [written["delta_low"], written["beta_row"]]
        args += [kept["states_one"], kept["query"], kept["match"], w_mem] + more
        in_specs += [whole((rows, width)), whole((rows, width)), whole((rows, mems)), whole((width, width))]
        in_specs += [whole(a.shape) for a in more]
        scratch += [
            pltpu.VMEM((rows, width), low_type),
            pltpu.VMEM((4 * mems, 3 * width), f32),
            pltpu.VMEM((2 * mems, width), f32),
        ]
    if w_sum is not None:
        args.append(w_sum)
        in_specs.append(pl.BlockSpec((width, width), lambda j: (0, j)))
    aliases = {}
    if earlier is not None:
        aliases = {len(args): 0}
        args.append(earlier)
        in_specs.append(pl.BlockSpec(memory_space=pl.ANY))
    out_specs = [
        pl.BlockSpec((None, seg_rows, width), lambda j: (slot, 0, 0)),
        result((mems, width)),
        pl.BlockSpec((width, width), lambda j: (0, j)),
        result((1, width)),
    ]
    out_shape = [
        shaped((slots, seg_rows, width), f32),
        shaped((mems, width), f32),
        shaped((width, parts * width), grad_type),
        shaped((1, width), f32),
    ]
    if reads:
        extra = [
            shaped((width, width), low_type),
            shaped((mems, width), f32),
            shaped((mems, 3 * width), f32),
            shaped((1, 3 * width), f32),
        ]
        out_shape += extra
        out_specs += [result(s.shape) for s in extra]
    return pl.pallas_call(
        functools.partial(enter_back_kernel, reads, w_sum is not None, earlier is not None),
        grid=(parts,),
        in_specs=in_specs,
        out_specs=out_specs,
        out_shape=out_shape,
        scratch_shapes=scratch,
        input_output_aliases=aliases,
        compiler_params=params(36),
        cost_estimate=pl.CostEstimate(
            flops=4 * rows * width * width * (parts + 1), bytes_accessed=30 * 2**20, transcendentals=0
        ),
        name="enter_back",
    )(*args)


MESH = pl.DeviceIdType.MESH
DEPTH, SIDE = 4, 2


def events(*numbers):
    return [divmod(number, 10) if number >= 0 else -1 - number for number in numbers]


ARRIVE_ORDER = events(
    0, 1, 10, 11, 20, 21, 2, 3, 30, 31, 12, 4, 13, 5, 22, 14, 23, 15, 32, 24, 6, 33, 25, 7, 34,
    35, 16, 17, 26, 27, 36, 37
)
ARRIVE_STEPS = {0: (3, 1), 1: (0, 4), 2: (0, 5), 3: (1, 4), 4: (1, 5), 6: (0, 6), 8: (0, 7)}
ARRIVE_STEPS.update({9: (3, 5), 10: (1, 7), 11: (2, 7), 12: (3, 6)})
FINISH_ORDER = events(
    0, 1, 10, 2, 11, 3, 20, 12, 4, 21, 13, 5, 30, 22, 14, 31, 23, 15, 6, 32, 24, 7, 33, 25, 8,
    16, 34, 17, 35, 18, 26, 36, 27, 37, 28, 38
)
FINISH_STEPS = {1: (0, 1), 2: (0, 2), 3: (0, 3), 4: (0, 4), 5: (0, 5), 6: (1, 4)}
FINISH_STEPS.update({7: (0, 6), 8: (0, 7), 9: (0, 8), 10: (3, 4), 11: (3, 5)})
FINISH_TAIL = events(
    18, 26, -1, 36, 27, -2, 37, 28, -3, 38, -4
)
GRID = (DEPTH, SIDE, SIDE, SIDE)
DEVICES = DEPTH * SIDE**3
ORDERS = ("zxy", "zyx", "xyz", "yxz")
sems = pltpu.SemaphoreType.DMA


def my_place():
    wide = lax.axis_index("wide")
    narrow = lax.axis_index("narrow")
    return wide // SIDE, wide % SIDE, narrow // SIDE, narrow % SIDE


def device_at(z, x, y, core):
    return (z * SIDE + x, y * SIDE + core)


def partners(z, x, y, core):
    return {
        "z": [device_at((z + step) % DEPTH, x, y, core) for step in range(1, DEPTH)],
        "x": [device_at(z, 1 - x, y, core)],
        "y": [device_at(z, x, 1 - y, core)],
        "c": [device_at(z, x, y, 1 - core)],
    }


def meet(peers):
    barrier = pltpu.get_barrier_semaphore()
    everyone = [peer for group in peers.values() for peer in group]
    for peer in everyone:
        pl.semaphore_signal(barrier, inc=1, device_id=peer, device_id_type=MESH)
    pl.semaphore_wait(barrier, len(everyone))


def remote(source, target, send, recv, peer):
    return pltpu.make_async_remote_copy(
        src_ref=source,
        dst_ref=target,
        send_sem=send,
        recv_sem=recv,
        device_id=peer,
        device_id_type=MESH,
    )


def slab(ref, place, known, at):
    z, x, y, core = place
    return ref.at[
        slice(None) if "z" in known else z,
        slice(None) if "x" in known else x,
        slice(None) if "y" in known else y,
        slice(None) if "c" in known else core,
        :,
        at,
    ]


def cut(cols, shares):
    unit = cols // 128 // sum(shares)
    pieces = []
    at = 0
    for order, share in zip(ORDERS, shares):
        if share:
            pieces.append((order, at, share * unit * 128))
            at += share * unit * 128
    return pieces


def event_order(total, lanes):
    order = []
    for now in range(-(-total // lanes) + 3):
        for lane in range(lanes):
            for index in (3, 2, 1, 0):
                group = (now - index) * lanes + lane
                if now >= index and group < total:
                    order.append((index, group))
    return order


def spread(order, last):
    schedule = {}
    done = 0
    for step, event in last.items():
        until = order.index(event) + 1
        schedule[step] = tuple(range(done, until))
        done = until
    return schedule


class Gather:
    def __init__(self, groups, order, lead):
        self.groups = groups
        self.lead = lead
        self.order = order
        self.ticks = len(self.order)
        self.numbers = {}
        for group, (_, pieces) in enumerate(groups):
            for piece in pieces:
                self.numbers[group, piece] = len(self.numbers)

    def scratch(self):
        count = len(self.numbers)
        return [sems((count,)), sems((count, 6)), sems((count, 6))]

    def bind(self, shards, fulls, scratch):
        self.shards = shards
        self.fulls = fulls
        self.own_sem, self.send_sem, self.recv_sem = scratch
        self.place = my_place()
        self.peers = partners(*self.place)

    def copies(self, index, group):
        a, pieces = self.groups[group]
        made = []
        for piece in pieces:
            order, start, size = piece
            number = self.numbers[group, piece]
            path = order + "c"
            at = pl.ds(start, size)
            target = slab(self.fulls[a], self.place, path[:index], at)
            source = self.shards[a].at[:, at] if index == 0 else target
            if index == 0:
                made.append(pltpu.make_async_copy(source, target, self.own_sem.at[number]))
            for step, peer in enumerate(self.peers[path[index]]):
                slot = index + step if path[index] == "z" else index + 2 * ("z" in path[:index])
                made.append(
                    remote(
                        source,
                        target,
                        self.send_sem.at[number, slot],
                        self.recv_sem.at[number, slot],
                        peer,
                    )
                )
        return made

    def begin(self, index, group):
        for copy in self.copies(index, group):
            copy.start()

    def enter(self):
        meet(self.peers)
        for group in range(min(self.lead, len(self.groups))):
            self.begin(0, group)

    def tick(self, now):
        index, group = self.order[now]
        for copy in self.copies(index, group):
            copy.wait()
        if index < 3:
            self.begin(index + 1, group)
        if index == 0 and group + self.lead < len(self.groups):
            self.begin(0, group + self.lead)


class Reduce:
    def __init__(self, groups, shapes, order):
        self.groups = groups
        self.shapes = shapes
        self.order = order
        self.ticks = len(self.order)
        count = 0
        self.entries = []
        for *_, pieces, _ in groups:
            self.entries.append([(count + i, piece) for i, piece in enumerate(pieces)])
            count += len(pieces)
        self.count = count

    def scratch(self):
        total = len(self.groups)
        made = [sems((total,)), sems((total,)), sems((total,)), sems((self.count, 5)), sems((self.count, 5))]
        for a, _, cols, _, _, pieces, held in self.groups:
            height = self.shapes[a][0]
            full = (DEPTH, SIDE, SIDE, height, cols)
            made.append(pltpu.VMEM(full, low_type))
            if not held:
                made.append(pltpu.VMEM(full, low_type))
            for _, _, size in pieces:
                made.append(pltpu.VMEM((DEPTH, SIDE, height, size), f32))
                made.append(pltpu.VMEM((DEPTH, SIDE, height, size), low_type))
                made.append(pltpu.VMEM((DEPTH, height, size), low_type))
                made.append(pltpu.VMEM((DEPTH - 1, height, size), low_type))
        return made

    def bind(self, partials, totals, scratch):
        self.partials = partials
        self.totals = totals
        self.own_sem, self.core_send, self.core_recv, self.send_sem, self.recv_sem, *scratch = scratch
        self.place = my_place()
        self.peers = partners(*self.place)
        z, x, y, core = self.place
        self.mine = {"x": x, "y": y}
        self.core_in, self.own, self.parts = [], [], {}
        for group, (*_, held) in enumerate(self.groups):
            core_in, *scratch = scratch
            self.core_in.append(core_in)
            if held:
                self.own.append(None)
            else:
                own, *scratch = scratch
                self.own.append(own)
            for number, _ in self.entries[group]:
                self.parts[number] = scratch[:4]
                scratch = scratch[4:]

    def enter(self):
        meet(self.peers)

    def core_copies(self, group):
        a, first, cols, _, _, _, held = self.groups[group]
        at = pl.ds(first, cols)
        core = self.place[3]
        made = [
            remote(
                self.partials[a].at[:, :, :, 1 - core, :, at],
                self.core_in[group],
                self.core_send.at[group],
                self.core_recv.at[group],
                self.peers["c"][0],
            )
        ]
        if not held:
            made.append(
                pltpu.make_async_copy(
                    self.partials[a].at[:, :, :, core, :, at], self.own[group], self.own_sem.at[group]
                )
            )
        return made

    def copies(self, index, group):
        if index == 0:
            return self.core_copies(group)
        made = []
        z = self.place[0]
        for number, (order, start, size) in self.entries[group]:
            kept, in1, in2, in3 = self.parts[number]
            if index == 1:
                axis = order[2]
                far = 1 - self.mine[axis]
                at = pl.ds(start, size)
                core_in = self.core_in[group]
                source = core_in.at[:, :, far, :, at] if axis == "y" else core_in.at[:, far, :, :, at]
                pairs = [(source, in1, self.peers[axis][0], 0)]
            elif index == 2:
                axis = order[1]
                pairs = [(in1.at[:, 1 - self.mine[axis]], in2, self.peers[axis][0], 1)]
            else:
                pairs = [
                    (in2.at[(z + step) % DEPTH], in3.at[step - 1], self.peers["z"][step - 1], 1 + step)
                    for step in range(1, DEPTH)
                ]
            for source, target, peer, slot in pairs:
                made.append(
                    remote(
                        source,
                        target,
                        self.send_sem.at[number, slot],
                        self.recv_sem.at[number, slot],
                        peer,
                    )
                )
        return made

    def begin(self, index, group):
        for copy in self.copies(index, group):
            copy.start()

    def add(self, index, group):
        z, x, y, core = self.place
        a, first, _, out, offset, _, held = self.groups[group]
        core_in = self.core_in[group]
        for number, (order, start, size) in self.entries[group]:
            kept, in1, in2, in3 = self.parts[number]
            at = pl.ds(start, size)
            if index == 0:
                axis = order[2]
                mine = self.mine[axis]

                def spot(step, where):
                    far, side = step // SIDE, step % SIDE
                    return (far, side, where) if axis == "y" else (far, where, side)

                def own_at(place):
                    if held:
                        inside = pl.ds(first + start, size)
                        return self.partials[a][place + (core, slice(None), inside)].astype(f32)
                    return self.own[group][place + (slice(None), at)].astype(f32)

                @pl.loop(0, DEPTH * SIDE)
                def _(step):
                    near = spot(step, mine)
                    away = spot(step, 1 - mine)
                    kept[step // SIDE, step % SIDE] = own_at(near) + core_in[near + (slice(None), at)].astype(f32)
                    moved = own_at(away) + core_in[away + (slice(None), at)].astype(f32)
                    core_in[away + (slice(None), at)] = low(moved)
            elif index == 1:
                mine = self.mine[order[1]]

                @pl.loop(0, DEPTH)
                def _(far):
                    kept[far, mine] += in1[far, mine].astype(f32)
                    in1[far, 1 - mine] = low(kept[far, 1 - mine] + in1[far, 1 - mine].astype(f32))
            elif index == 2:
                mine = self.mine[order[1]]
                kept[z, mine] += in2[z].astype(f32)
                for step in range(1, DEPTH):
                    target = (z + step) % DEPTH
                    in2[target] = low(kept[target, mine] + in2[target].astype(f32))
            else:
                mine = self.mine[order[1]]
                total = kept[z, mine]
                for step in range(DEPTH - 1):
                    total = total + in3[step].astype(f32)
                self.totals[out][:, pl.ds(offset + start, size)] = total

    def tick(self, now):
        index, group = self.order[now]
        for copy in self.copies(index, group):
            copy.wait()
        self.add(index, group)
        if index < 3:
            self.begin(index + 1, group)


class SmallSum:
    def __init__(self, shape):
        self.shape = shape
        self.ticks = 4

    def scratch(self):
        return [
            pltpu.VMEM((4,) + self.shape, f32),
            pltpu.VMEM((3,) + self.shape, f32),
            pltpu.VMEM((DEPTH,) + self.shape, f32),
            sems((6,)),
            sems((6,)),
        ]

    def bind(self, out, scratch):
        self.out = out
        self.sums, self.arrived, self.along, self.send_sem, self.recv_sem = scratch
        self.place = my_place()
        self.peers = partners(*self.place)

    def copies(self, index):
        if index < 3:
            return [
                remote(
                    self.sums.at[index],
                    self.arrived.at[index],
                    self.send_sem.at[index],
                    self.recv_sem.at[index],
                    self.peers["cyx"[index]][0],
                )
            ]
        return [
            remote(
                self.sums.at[3],
                self.along.at[self.place[0]],
                self.send_sem.at[3 + step],
                self.recv_sem.at[3 + step],
                self.peers["z"][step],
            )
            for step in range(DEPTH - 1)
        ]

    def enter(self, value):
        self.sums[0] = value
        for copy in self.copies(0):
            copy.start()

    def tick(self, index):
        for copy in self.copies(index):
            copy.wait()
        if index < 3:
            self.sums[index + 1] = self.sums[index] + self.arrived[index]
            if index == 2:
                self.along[self.place[0]] = self.sums[3]
            for copy in self.copies(index + 1):
                copy.start()
        else:
            total = self.along[0]
            for far in range(1, DEPTH):
                total = total + self.along[far]
            self.out[...] = total


def slabs(array):
    rows, cols = array.shape
    return array.reshape(GRID + (rows // DEVICES, cols))


def flat(array):
    return array.reshape(DEVICES * array.shape[-2], array.shape[-1])


def gather_weights(shards):
    return [lax.all_gather(shard, AXES, axis=0, tiled=True) for shard in shards]


def scatter_sums(totals):
    return [
        lax.psum_scatter(total.astype(f32), AXES, scatter_dimension=0, tiled=True)
        for total in totals
    ]


def at_chunk(step, size):
    return pl.ds(pl.multiple_of(step * size, size), size)


def at_step(step, when):
    return lambda body: pl.when(step == when)(body)


def slab_rows(values):
    return low(values.astype(f32).reshape(-1, values.shape[-1]))


def arrive_kernel(plan, seg_rows, schedule, hidden_size, *refs):
    count = 5
    tokens_ref, mem_ref, gains_ref, *refs = refs
    shards, refs = refs[:count], refs[count:]
    (
        normed_ref,
        qkv_ref,
        attended_ref,
        log_ref,
        out_ref,
        mem_out_ref,
        states_two_ref,
        normed_two_ref,
        upward_ref,
        *refs,
    ) = refs
    fulls, refs = refs[:count], refs[count:]
    w_qkv_full, w_out_full, w_up_full, w_down_full, _ = fulls
    (
        first_ref,
        w_ref,
        w_out_slabs,
        w_out_ref,
        w_up_ref,
        w_down_ref,
        sum_ref,
        w_sem,
        up_sem,
        down_sem,
        *refs,
    ) = refs
    plan.bind(shards, fulls, refs)
    parts, rows, width = qkv_ref.shape
    pairs = width // PAIR
    leave_at = parts + pairs
    step = pl.program_id(0)
    chunk_now = step - leave_at

    @pl.when(step == 0)
    def _():
        plan.enter()
        load_first(tokens_ref, mem_ref, first_ref)

        def chunk(at):
            unit, _ = normal_form(first_ref[at, :].astype(f32))
            normed_ref[at, :] = low(unit * gains_ref[0:1, :].astype(f32))

        over_rows(rows, chunk)

    for when, ticks in schedule.items():

        @pl.when(step == when)
        def _():
            for now in ticks:
                plan.tick(now)

    @pl.when(step == 0)
    def _():
        copy = pltpu.make_async_copy(w_qkv_full, w_ref, w_sem)
        copy.start()
        copy.wait()

    @pl.when(step < parts)
    def _():
        block = slab_rows(w_ref[..., at_chunk(step, width)])
        qkv_ref[step] = low(nn(normed_ref[...], block))

    @pl.when((step >= parts) & (step < leave_at))
    def _():
        attend_kernel(
            seg_rows, qkv_ref, attended_ref, log_ref, at_chunk(step - parts, PAIR), step - parts
        )

    def hidden_copies(index):
        slot = lax.rem(index, 2)
        return [
            pltpu.make_async_copy(
                w_up_full.at[..., at_chunk(index, hidden_size)], w_up_ref.at[slot], up_sem.at[slot]
            ),
            pltpu.make_async_copy(w_down_full.at[index], w_down_ref.at[slot], down_sem.at[slot]),
        ]

    @pl.when(step == leave_at)
    def _():
        copy = pltpu.make_async_copy(w_out_full, w_out_slabs, w_sem)
        copy.start()
        for other in hidden_copies(chunk_now):
            other.start()
        copy.wait()
        w_out_ref[...] = slab_rows(w_out_slabs[...])

        def chunk(at):
            states = first_ref[at, :].astype(f32) + nn(attended_ref[at, :], w_out_ref[...])
            states_two_ref[at, :] = states
            unit, _ = normal_form(states)
            normed_two_ref[at, :] = low(unit * gains_ref[1:2, :].astype(f32))
            sum_ref[at, :] = states

        over_rows(rows, chunk)

    @pl.when(step >= leave_at)
    def _():
        for copy in hidden_copies(chunk_now):
            copy.wait()

        @pl.when(step + 1 < pl.num_programs(0))
        def _():
            for copy in hidden_copies(chunk_now + 1):
                copy.start()

        slot = lax.rem(chunk_now, 2)
        upward = nn(normed_two_ref[...], slab_rows(w_up_ref[slot]))
        upward_ref[...] = upward
        bent = jnp.tanh(upward * (gelu_c + gelu_c * gelu_a * (upward * upward)))
        active = low(upward * (0.5 + 0.5 * bent))
        down = w_down_ref[slot]
        sum_ref[...] += nn(active, down.reshape(hidden_size, width))

    @pl.when(step == pl.num_programs(0) - 1)
    def _():
        out_ref[...] = low(sum_ref[:seg_rows, :])
        mem_out_ref[...] = sum_ref[seg_rows:, :]
        for now in range(sum(len(t) for t in schedule.values()), plan.ticks):
            plan.tick(now)


def arrive(tokens, mem_tokens, gains, shards, plan, schedule):
    slots, seg_rows, width = tokens.shape
    mems = mem_tokens.shape[0]
    rows = seg_rows + mems
    parts = shards[0].shape[1] // width
    pairs = width // PAIR
    hidden = shards[2].shape[1]
    size = hidden // DEPTH
    lanes = packed_lanes(rows, seg_rows)[1]
    tall = shards[3].shape[0]
    segment = pl.BlockSpec((None, seg_rows, width), lambda j: (0, 0, 0), pipeline_mode=pl.Buffered(1))
    outs = pl.pallas_call(
        functools.partial(arrive_kernel, plan, seg_rows, schedule, size),
        grid=(parts + pairs + DEPTH,),
        in_specs=[segment, whole((mems, width)), whole(gains.shape)]
        + [whole(shard.shape) for shard in shards],
        out_specs=[
            whole((rows, width)),
            whole((parts, rows, width)),
            whole((rows, width)),
            whole((pairs, 1, lanes)),
            whole((seg_rows, width)),
            whole((mems, width)),
            whole((rows, width)),
            whole((rows, width)),
            pl.BlockSpec((rows, size), lambda j: (0, jnp.maximum(j - parts - pairs, 0))),
        ]
        + [ANYWHERE] * len(shards),
        out_shape=[
            shaped((rows, width), low_type),
            shaped((parts, rows, width), low_type),
            shaped((rows, width), low_type),
            shaped((pairs, 1, lanes), f32),
            shaped((seg_rows, width), low_type),
            shaped((mems, width), f32),
            shaped((rows, width), f32),
            shaped((rows, width), low_type),
            shaped((rows, hidden), f32),
        ]
        + [shaped(GRID + shard.shape, low_type) for shard in shards],
        scratch_shapes=[
            pltpu.VMEM((rows, width), low_type),
            pltpu.VMEM(GRID + shards[0].shape, low_type),
            pltpu.VMEM(GRID + shards[1].shape, low_type),
            pltpu.VMEM((width, width), low_type),
            pltpu.VMEM((2,) + GRID + (shards[2].shape[0], size), low_type),
            pltpu.VMEM((2,) + GRID[1:] + (tall, width), low_type),
            pltpu.VMEM((rows, width), f32),
            sems,
            sems((2,)),
            sems((2,)),
        ]
        + plan.scratch(),
        compiler_params=params(collective_id=0, has_side_effects=True),
        name="arrive",
    )(tokens, mem_tokens, gains, *shards)
    return outs[:9], [flat(o) for o in outs[9:]]


def carry_kernel(body, plan, counts, schedule, grid, *refs):
    ins, moved, outs, totals, scratch = counts
    parts = []
    for count in (ins, moved, outs, totals, scratch):
        parts.append(refs[:count])
        refs = refs[count:]
    own_in, partials, own_out, total_refs, own_scratch = parts
    plan.bind(partials, total_refs, refs)
    step = pl.program_id(0)

    @pl.when(step == 0)
    def _():
        plan.enter()
        for group in range(len(plan.groups)):
            plan.begin(0, group)

    for when, ticks in schedule.items():
        if when < grid:

            @pl.when(step == when)
            def _():
                for now in ticks:
                    plan.tick(now)

    body(*own_in, *own_out, *own_scratch)

    if grid in schedule:

        @pl.when(step == grid - 1)
        def _():
            for now in schedule[grid]:
                plan.tick(now)


def finish_kernel(plan, small, seg_rows, schedule, counts, *refs):
    (
        qkv_ref,
        grad_ref,
        attended_ref,
        log_ref,
        tokens_ref,
        mem_ref,
        normed_ref,
        gains_ref,
        w_ref,
        w_in_ref,
        small_in_ref,
        grad_states_ref,
        *refs,
    ) = refs
    moved, totals = counts
    partials, refs = refs[:moved], refs[moved:]
    first_ref, *refs = refs
    total_refs, refs = refs[:totals], refs[totals:]
    small_out_ref, keys_sum, values_sum, grad_qkv_ref, w_grad_ref, sum_ref, states_sem, *refs = refs
    kept = len(small.scratch())
    small.bind(small_out_ref, refs[:kept])
    plan.bind(list(partials) + [w_grad_ref], total_refs, refs[kept:])
    rows, width = normed_ref.shape
    parts = grad_qkv_ref.shape[0]
    pairs = width // PAIR
    step = pl.program_id(0)
    late = [g for g, group in enumerate(plan.groups) if group[-1]]
    early = [g for g, group in enumerate(plan.groups) if not group[-1]]
    states_copy = pltpu.make_async_copy(grad_states_ref, first_ref, states_sem)

    @pl.when(step == 0)
    def _():
        plan.enter()
        for group in early:
            plan.begin(0, group)
        states_copy.start()
        sum_ref[...] = jnp.zeros_like(sum_ref)

    for when, ticks in schedule.items():

        @pl.when(step == when)
        def _():
            for now in ticks:
                plan.tick(now)

    @pl.when(step < pairs)
    def _():
        attend_back_kernel(
            seg_rows,
            qkv_ref,
            grad_ref,
            attended_ref,
            log_ref,
            grad_qkv_ref,
            keys_sum,
            values_sum,
            at_chunk(step, PAIR),
        )

    @pl.when((step >= pairs) & (step < pairs + parts))
    def _():
        part = step - pairs
        grad_w = tn(normed_ref[...], grad_qkv_ref[part]) + w_in_ref[...]
        w_grad_ref[..., at_chunk(part, width)] = low(grad_w.reshape(GRID + (width // DEVICES, width)))
        for index, group in enumerate(late):

            @pl.when(part == index)
            def _():
                plan.begin(0, group)

    @pl.when(step >= pairs + parts)
    def _():
        sum_ref[...] += nt(grad_qkv_ref[step - pairs - parts], w_ref[...])

    @pl.when(step == pairs + 2 * parts - 1)
    def _():
        gain = gains_ref[0:1, :].astype(f32)
        states_copy.wait()
        small_out_ref[...] = small_in_ref[...]
        mems = rows - seg_rows

        def back(first, at):
            unit, inverse = normal_form(first)
            grad = sum_ref[at, :]
            small_out_ref[mems : mems + 1, :] += jnp.sum(grad * unit, axis=0, keepdims=True)
            first_ref[at, :] += norm_back(grad, unit, inverse, gain)

        def chunk(at):
            back(tokens_ref[at, :].astype(f32), at)

        over_rows(seg_rows, chunk, False)
        last = pl.ds(seg_rows, mems)
        back(mem_ref[...].astype(f32), last)
        small_out_ref[:mems, :] += first_ref[last, :]
        small.enter(small_out_ref[...])
        for event in FINISH_TAIL:
            if isinstance(event, int):
                small.tick(event)
            else:
                plan.tick(plan.order.index(event))


def finish(
    tokens, mem_tokens, kept, grad_attended, grad_states, gains, w_qkv, w_in, small_in, partials, plan, schedule, widths
):
    slots, seg_rows, width = tokens.shape
    mems = mem_tokens.shape[0]
    rows = seg_rows + mems
    qkv = kept["qkv"]
    parts = qkv.shape[0]
    pairs = width // PAIR
    small = SmallSum(small_in.shape)
    logs = kept["logs"]

    def pair(step):
        return jnp.minimum(step, pairs - 1)

    def part(step, start):
        return jnp.clip(step - start, 0, parts - 1)

    column = pl.BlockSpec((rows, PAIR), lambda j: (0, pair(j)))
    outs = pl.pallas_call(
        functools.partial(finish_kernel, plan, small, seg_rows, schedule, (len(partials), len(widths))),
        grid=(pairs + 2 * parts,),
        in_specs=[
            pl.BlockSpec((parts, rows, PAIR), lambda j: (0, 0, pair(j))),
            column,
            column,
            pl.BlockSpec((1,) + logs.shape[1:], lambda j: (pair(j), 0, 0)),
            pl.BlockSpec((None, seg_rows, width), lambda j: (0, 0, 0), pipeline_mode=pl.Buffered(1)),
            whole((mems, width)),
            whole((rows, width)),
            whole(gains.shape),
            pl.BlockSpec((width, width), lambda j: (0, part(j, pairs + parts))),
            pl.BlockSpec((width, width), lambda j: (0, part(j, pairs))),
            whole(small_in.shape),
            ANYWHERE,
        ]
        + [ANYWHERE] * len(partials),
        out_specs=[whole((rows, width))] + [whole(s) for s in widths] + [whole(small_in.shape)],
        out_shape=[shaped((rows, width), f32)]
        + [shaped(s, f32) for s in widths]
        + [shaped(small_in.shape, f32)],
        scratch_shapes=[
            pltpu.VMEM((rows, PAIR), f32),
            pltpu.VMEM((rows, PAIR), f32),
            pltpu.VMEM((parts, rows, width), low_type),
            pltpu.VMEM(GRID + (width // DEVICES, parts * width), low_type),
            pltpu.VMEM((rows, width), f32),
            sems,
        ]
        + small.scratch()
        + plan.scratch(),
        compiler_params=params(collective_id=2, has_side_effects=True),
        name="finish",
    )(
        qkv,
        grad_attended,
        kept["attended"],
        logs,
        tokens,
        mem_tokens,
        kept["normed_one"],
        gains,
        w_qkv,
        w_in,
        small_in,
        grad_states,
        *partials,
    )
    return outs[0], outs[1:-1], outs[-1]


def settle_kernel(count, first_ref, *refs):
    small_ref, *refs = refs
    sums, refs = refs[:count], refs[count + 1 :]
    tokens_ref, mem_ref, gains_ref, beta_ref, *outs = refs
    tokens_ref[...] = first_ref[...]

    @pl.when(pl.program_id(0) == 0)
    def _():
        mems = mem_ref.shape[0]
        mem_ref[...] = small_ref[:mems, :]
        gains_ref[...] = small_ref[mems : mems + 2, :]
        beta_ref[...] = small_ref[mems + 2, :]
        for source, target in zip(sums, outs):
            target[...] = source[...]


def settle(first, small, sums, grad_tokens, mems):
    slots, seg_rows, width = grad_tokens.shape
    size = 256
    shapes = [(mems, width), (2, width), (width,)] + [s.shape for s in sums]
    return pl.pallas_call(
        functools.partial(settle_kernel, len(sums)),
        grid=(seg_rows // size,),
        in_specs=[pl.BlockSpec((size, width), lambda j: (j, 0)), whole(small.shape)]
        + [whole(s.shape) for s in sums]
        + [ANYWHERE],
        out_specs=[pl.BlockSpec((None, size, width), lambda j: (0, j, 0))] + [result(s) for s in shapes],
        out_shape=[shaped(grad_tokens.shape, f32)] + [shaped(s, f32) for s in shapes],
        input_output_aliases={2 + len(sums): 0},
        compiler_params=params(),
        name="settle",
    )(first, small, *sums, grad_tokens)


def fast_gather(shards):
    groups = []
    for a, shard in enumerate(shards):
        rows, cols = shard.shape
        if cols < 2048:
            bounds = [(0, cols, (2, 2, 1, 1) if rows > 48 else (1, 1))]
        elif cols % 1024 == 256:
            bounds = [(0, 1280, (4, 4, 1, 1)), (1280, cols - 1280, (1, 1))]
        else:
            bounds = [(0, cols // 2, (5, 5, 1, 1)), (cols // 2, cols // 2, (5, 5, 1, 1))]
        for at, size, shares in bounds:
            groups.append((a, [(order, at + start, n) for order, start, n in cut(size, shares)]))
    return Gather(groups, ARRIVE_ORDER, 2)


def on_device(
    fast, tokens, item_ids, w_mem, w_qkv, w_out, w_up, w_down, mem_tokens, gains, w_beta, out_grad
):
    slots, seg_rows, width = tokens.shape
    mems = mem_tokens.shape[0]
    w_beta = w_beta.reshape(1, width)
    shards = [w_qkv, w_out, w_up, w_down, w_mem]
    if fast:
        plan = fast_gather(shards)
        schedule = spread(plan.order, ARRIVE_STEPS)
        arrived, fulls = arrive(tokens, mem_tokens, gains, shards, plan, schedule)
    else:
        fulls = gather_weights(shards)
    w_qkv, w_out, w_up, w_down, w_mem = fulls
    kept_all = []
    written = [None] * (slots + 1)
    out = None
    for slot in range(slots):
        kept = {}
        start = (tokens, mem_tokens)
        if fast and slot == 0:
            names = ("normed_one", "qkv", "attended", "logs", "out", "mem_out", "states_two")
            kept = dict(zip(names + ("normed_two", "upward"), arrived))
            out, mem_out = kept["out"], kept["mem_out"]
        else:
            entered = enter_segment(slot, tokens, mem_tokens, gains, w_qkv, w_mem, written[slot])
            kept["normed_one"], kept["qkv"] = entered[:2]
            if written[slot] is not None:
                kept["states_one"], kept["query"], kept["match"] = entered[2:]
                start = kept["states_one"]
            kept["attended"], kept["logs"] = attend(kept["qkv"], seg_rows)
        if slot + 1 == slots:
            both = leave_both(slot, start, kept["attended"], out_grad, gains, w_out, w_up, w_down, out, f32)
            out = both["block_out"]
        elif not fast:
            out, mem_out, kept["states_two"], kept["normed_two"], kept["upward"] = leave_segment(
                slot, slots, seg_rows, start, kept["attended"], gains, w_out, w_up, w_down, out
            )
            kept["mem_out"] = mem_out
        if slot + 1 < slots:
            written[slot + 1] = write_memory(slot, item_ids, mem_out, w_mem, w_beta)
        kept_all.append(kept)

    sums = None
    qkv_sum = None
    grad_tokens = None
    grad_mem_tokens = 0.0
    gain_one_sum = 0.0
    gain_two_sum = 0.0
    grad_beta = 0.0
    pulled = None
    for slot in reversed(range(slots)):
        kept = kept_all[slot]
        last = slot == 0
        grad_type = low_type if last else f32
        grad_rows = None
        mem_plan = None
        if slot + 1 < slots:
            grad_rows, w_pair_sum, grad_beta_part = write_back(
                slot, item_ids, kept["mem_out"], w_mem, w_beta, written[slot + 1], *pulled
            )
            grad_beta += grad_beta_part
            if fast and last:
                mem_plan = [slabs(w_query_sum), slabs(w_pair_sum)]
            left = leave_back(
                slot, out_grad, grad_rows, kept, gains, w_out, w_up, w_down, sums, grad_type, mem_plan
            )
        else:
            left = [both[name] for name in ("grad_states", "grad_attended", "up", "down", "out", "gain_two")]
        grad_states, grad_attended, up_sum, down_sum, out_sum, gain_two, *mem_total = left
        gain_two_sum += gain_two
        sums = {"up": up_sum, "down": down_sum, "out": out_sum}
        if fast and last:
            break
        grad_qkv = attend_back(kept["qkv"], grad_attended, kept["attended"], kept["logs"], seg_rows)
        grad_tokens, grad_mem, qkv_sum, gain_one, *extra = enter_back(
            slot,
            tokens,
            mem_tokens,
            kept,
            grad_qkv,
            grad_states,
            gains,
            w_qkv,
            w_mem,
            written[slot],
            qkv_sum,
            grad_tokens,
            grad_type,
        )
        if written[slot] is not None:
            w_query_sum, *pulled = extra
        grad_mem_tokens += grad_mem
        gain_one_sum += gain_one
    if fast:
        small = jnp.concatenate([grad_mem_tokens, gain_one_sum, gain_two_sum, grad_beta], axis=0)
        small = jnp.pad(small, ((0, -small.shape[0] % 8), (0, 0)))
        partials = [slabs(down_sum), slabs(up_sum), slabs(out_sum)]
        shapes = [p.shape[-2:] for p in partials] + [(width // DEVICES, w_qkv.shape[1])]
        third = shapes[1][1] // 3
        places = [(0, 0, 256), (0, 256, width - 256)]
        places += [(1, at, third) for at in range(0, shapes[1][1], third)]
        places += [(2, 0, width)]
        places += [(3, at, width) for at in range(0, shapes[3][1], width)]
        groups = [(a, at, size, a, at, cut(size, (1, 1)), a == 3) for a, at, size in places]
        plan = Reduce(groups, shapes, FINISH_ORDER)
        schedule = spread(plan.order, FINISH_STEPS)
        first, (down_total, up_total, out_total, qkv_total), small = finish(
            tokens,
            mem_tokens,
            kept,
            grad_attended,
            grad_states,
            gains,
            w_qkv,
            qkv_sum,
            small,
            partials,
            plan,
            schedule,
            shapes,
        )
        totals = [mem_total[0], qkv_total, out_total, up_total, down_total]
        grad_tokens, grad_mem_tokens, grad_gains, grad_beta, *totals = settle(
            first, small, totals, grad_tokens, mems
        )
        return (out, grad_tokens, *totals, grad_mem_tokens, grad_gains, grad_beta)
    mem_sum = jnp.concatenate([w_query_sum, w_pair_sum], axis=1)
    grad_gains = jnp.concatenate([gain_one_sum, gain_two_sum], axis=0)
    summed = scatter_sums([mem_sum, qkv_sum, sums["out"], sums["up"], sums["down"]])
    small = lax.psum((grad_mem_tokens, grad_gains, grad_beta.reshape(width)), AXES)
    return (out, grad_tokens, *summed, *small)


def solution(mesh):
    split_rows = P(AXES, None)
    split_items = P(AXES, None, None)
    in_specs = (
        split_items,
        P(AXES),
        split_rows,
        split_rows,
        split_rows,
        split_rows,
        split_rows,
        P(),
        P(),
        P(),
        split_items,
    )
    out_specs = (
        split_items,
        split_items,
        split_rows,
        split_rows,
        split_rows,
        split_rows,
        split_rows,
        P(),
        P(),
        P(),
    )
    fast = mesh.shape["wide"] == DEPTH * SIDE and mesh.shape["narrow"] == SIDE * SIDE
    return jax.shard_map(
        functools.partial(on_device, fast), mesh=mesh, in_specs=in_specs, out_specs=out_specs, check_vma=False
    )
```
